32 devices in a mesh: cls: 2 (over y), dom: 4 (over x, core), orient: 4 (over z).
Axes of the slice: x: 2, y: 2, z: 4, core: 2. Of those that a mesh axis runs over, the one named last changes fastest.
Arguments:
- references: bfloat16 [2, 8, 4, 32768], P(None, 'cls', None, ('dom', 'orient')), may hold values from -2 to 2
- images: bfloat16 [2, 256, 32768], P(None, ('dom', 'orient')), may hold values from -16 to 16
- orient_lists: int32 [256, 1], P(('dom', 'orient')), may hold values from 0 to 3; in each aligned block of 16 rows (0 to 15, 16 to 31, ...) at most 6 rows name the same one
- shift_ids: int32 [256, 1], P(('dom', 'orient')), may hold values from 0 to 63
- fixed_weights: float32 [256, 1], P(('dom', 'orient')), may hold values from 0.2 to 2
Outputs:
- class_prob: float32 [256, 8], P(('dom', 'orient'), 'cls')
- volume: float32 [2, 8, 4, 32768], P(None, 'cls', 'orient', 'dom')
The draws below stay inside these ranges and needn't reach their ends.
Inputs may be any that keep to these rules, and one draw needn't show every extreme that they name: `orient_lists`: within the rows of one device (16 particles), no orientation bin is listed by more than 6 particles, a bound that some block reaches.
All inputs are finite; a program needn't handle non-finite values.
Results may differ from the reference program's by a relative error of at most 0.02.
Values may be sent and summed in bfloat16 or wider, within the bound.
No kernel may reach another device: no remote copies, remote signals or barrier semaphores. Data moves between devices by JAX's collectives and lax.ppermute only.
A program may use at most 320 MiB of HBM per device.

```python
import math
import jax
import jax.numpy as jnp
import numpy as np
from jax import lax

IMG = 256
PIX = 32768
TX = 8
TY = 8
SHIFTS = 64
CLASSES = 8
ORIENTS = 4
PART_DEV = 16
PARTICLES = 256
S = 1
MOST = 6


def ref_table(key):
    values = jax.random.normal(jax.random.fold_in(key, 11), (2, CLASSES, ORIENTS, PIX), jnp.float32)
    return jnp.clip(values, -6.0, 6.0) * (3.0 / math.sqrt(2.0 * PIX))


def draw_references(key, part):
    return ref_table(key).astype(jnp.bfloat16)


def draw_images(key, part):
    noise_field = jax.random.normal(jax.random.fold_in(key, 12), (2, PARTICLES, PIX), jnp.float32)
    noise_field = jnp.clip(noise_field, -6.0, 6.0)
    return noise_field.astype(jnp.bfloat16)


def set_ends(drawn, stream_key, smallest, top_value):
    longest = drawn.shape.index(max(drawn.shape))
    spots = []
    for shift in (0, 1):
        where = [jax.random.randint(jax.random.fold_in(stream_key, axis), (), 0, length) for axis, length in enumerate(drawn.shape)]
        where[longest] = (where[longest] + shift) % drawn.shape[longest]
        spots.append(tuple(where))
    return drawn.at[spots[0]].set(smallest).at[spots[1]].set(top_value)


def steps_of(stream_key, dims, pieces, least, top_value):
    def one(axis_at, blocks):
        steps = jax.random.uniform(jax.random.fold_in(jax.random.fold_in(stream_key, 6), axis_at), (blocks,), jnp.float32, least / len(pieces), top_value / len(pieces))
        return jnp.repeat(jnp.exp(steps), dims[axis_at] // blocks).reshape((-1,) + (1,) * (len(dims) - axis_at - 1))

    loudness = one(*pieces[0])
    for cut in pieces[1:]:
        loudness = loudness * one(*cut)
    return loudness


def routed_block(stream_key, own, number, rows, number_of, top, reach, slope):
    sequence = jax.random.permutation(stream_key, number_of)
    packed, ordinary = portions_of(number_of, rows * top, reach, slope, True), portions_of(number_of, rows * top, reach, slope, False)
    places = jnp.arange(number_of)

    def named(sizes, turn):
        used = int((sizes > 0).sum())
        fixed = max(1, used // 4)
        moved = fixed + (places - fixed + turn * (used - fixed)) % max(1, number_of - fixed)
        return jnp.zeros((number_of,), jnp.int32).at[sequence[jnp.where(places < fixed, places, moved)]].set(jnp.asarray(sizes, jnp.int32))

    sizes = jnp.where(number % 4 == 0, named(packed, number // 4), named(ordinary, number - number // 4 - 1))
    mixed = jax.random.permutation(jax.random.fold_in(own, 3), number_of)
    donor, taker = mixed[0:number_of // 2 * 2:2], mixed[1:number_of // 2 * 2:2]
    margin = jnp.minimum(sizes[donor] - 1, reach - sizes[taker]) // 2
    margin = jnp.where((donor == sequence[0]) | (taker == sequence[0]) | (sizes[taker] == 0), 0, jnp.maximum(margin, 0))
    moved = jax.random.randint(jax.random.fold_in(own, 4), (number_of // 2,), 0, 1 << 20) % (margin + 1)
    sizes = sizes.at[donor].add(-moved).at[taker].add(moved)
    labels = jnp.searchsorted(jnp.cumsum(sizes), jnp.arange(rows * top), side="right").astype(jnp.int32)
    grid = labels.reshape(top, rows).T
    grid = grid[jax.random.permutation(jax.random.fold_in(own, 1), rows)]
    turn = jax.random.randint(jax.random.fold_in(own, 2), (rows, 1), 0, top)
    return jnp.take_along_axis(grid, (jnp.arange(top)[None, :] + turn) % top, axis=1)


def portions_of(amount, total, bound, slope, full):
    portions = [(1 << 20) // math.isqrt(standing ** slope) + 1 for standing in range(1, amount + 1)]
    largest = bound if full else min(bound, max(-(-total // amount), total * portions[0] // sum(portions)))
    least = 1 if total - largest >= amount - 1 else 0
    given, surplus = [largest] + [least] * (amount - 1), total - largest - least * (amount - 1)
    while surplus > 0:
        movable = [i for i in range(1, amount) if given[i] < largest] or [i for i in range(1, amount) if given[i] < bound]
        mass, remaining = sum([portions[i] for i in movable]), surplus
        for i in movable:
            more = min(bound - given[i], max(1, remaining * portions[i] // mass), surplus)
            given[i] = given[i] + more
            surplus = surplus - more
    return np.array(given)


def setup_inputs(seed: int = 0) -> dict:
    key_of = jax.random.split(jax.random.key(seed), 6)
    references = draw_references(jax.random.fold_in(key_of[5], 71), 0)
    images = draw_images(jax.random.fold_in(key_of[5], 71), 0)
    orient_lists_keys = jax.random.split(jax.random.fold_in(key_of[2], 1), PARTICLES // PART_DEV)
    orient_lists_turns = jax.random.permutation(jax.random.fold_in(key_of[2], 3), PARTICLES // PART_DEV)
    orient_lists = jax.vmap(lambda own, number: routed_block(jax.random.fold_in(key_of[2], 2), own, number, PART_DEV, ORIENTS, S, MOST, 2))(orient_lists_keys, orient_lists_turns).reshape((PARTICLES, S))
    shift_ids = set_ends(jax.random.randint(key_of[3], (PARTICLES, S), 0, SHIFTS), jax.random.fold_in(key_of[3], 1), 0, SHIFTS - 1).astype(jnp.int32)
    fixed_weights = jnp.clip(jnp.exp(math.log(2.0) - 2.3025851 * jax.random.uniform(key_of[4], (PARTICLES, S), jnp.float32) ** steps_of(key_of[4], (PARTICLES, S), ((0, 16),), -0.2, 0.2)), 0.2, 2.0)
    return dict(references=references, images=images, orient_lists=orient_lists, shift_ids=shift_ids, fixed_weights=fixed_weights)


TWO_PI = 2.0 * math.pi


def freq_ids(columns):
    freq_x = (columns % IMG - IMG // 2).astype(jnp.float32)
    freq_y = (columns // IMG).astype(jnp.float32)
    return freq_x, freq_y


def offsets(number):
    return (jnp.arange(number, dtype=jnp.int32) - number // 2).astype(jnp.float32)


def reference(references, images, orient_lists, shift_ids, fixed_weights):
    columns = jnp.arange(PIX, dtype=jnp.int32)
    freq_x, freq_y = freq_ids(columns)
    angle_x = (TWO_PI / IMG) * (offsets(TX)[:, None] * freq_x[None, :])
    angle_y = (TWO_PI / IMG) * (offsets(TY)[:, None] * freq_y[None, :])
    cosine_x, sine_x = jnp.cos(angle_x), jnp.sin(angle_x)
    cosine_y, sine_y = jnp.cos(angle_y), jnp.sin(angle_y)
    ref_re = references[0].astype(jnp.float32).reshape(CLASSES * ORIENTS, PIX)
    ref_im = references[1].astype(jnp.float32).reshape(CLASSES * ORIENTS, PIX)
    shifted_ref_re = (ref_re[None] * cosine_y[:, None] + ref_im[None] * sine_y[:, None]).astype(jnp.bfloat16).reshape(TY * CLASSES * ORIENTS, PIX)
    shifted_ref_im = (ref_im[None] * cosine_y[:, None] - ref_re[None] * sine_y[:, None]).astype(jnp.bfloat16).reshape(TY * CLASSES * ORIENTS, PIX)
    block_count = PARTICLES // PART_DEV
    orient_range = jnp.arange(ORIENTS, dtype=jnp.int32)

    def scan_step(volume, block_index):
        first_row = (block_index * PART_DEV).astype(jnp.int32)
        image_block = lax.dynamic_slice_in_dim(images, first_row, PART_DEV, 1)
        image_re = image_block[0].astype(jnp.float32)
        image_im = image_block[1].astype(jnp.float32)
        shifted_x_re = (image_re[None] * cosine_x[:, None] - image_im[None] * sine_x[:, None]).astype(jnp.bfloat16).reshape(TX * PART_DEV, PIX)
        shifted_x_im = (image_re[None] * sine_x[:, None] + image_im[None] * cosine_x[:, None]).astype(jnp.bfloat16).reshape(TX * PART_DEV, PIX)
        scores = jnp.dot(shifted_x_re, shifted_ref_re.T, preferred_element_type=jnp.float32)
        scores = scores + jnp.dot(shifted_x_im, shifted_ref_im.T, preferred_element_type=jnp.float32)
        logits = scores.reshape(TX, PART_DEV, TY, CLASSES, ORIENTS)
        global_top = jnp.max(logits, axis=(0, 2, 3, 4))
        exponent = jnp.exp(logits - global_top[None, :, None, None, None])
        totals = jnp.sum(exponent, axis=(0, 2, 3, 4))
        class_prob = jnp.sum(exponent, axis=(0, 2, 4)) / totals[:, None]
        orient_ids = lax.dynamic_slice_in_dim(orient_lists, first_row, PART_DEV, 0).reshape(PART_DEV * S)
        shift_index = lax.dynamic_slice_in_dim(shift_ids, first_row, PART_DEV, 0)
        fixed_block = lax.dynamic_slice_in_dim(fixed_weights, first_row, PART_DEV, 0)
        insert_weight = (fixed_block[:, :, None] * class_prob[:, None, :]).astype(jnp.bfloat16).reshape(PART_DEV * S, CLASSES)
        entry_x = (shift_index % TX - TX // 2).astype(jnp.float32)
        entry_y = (shift_index // TX - TY // 2).astype(jnp.float32)
        angle = (TWO_PI / IMG) * (entry_x[:, :, None] * freq_x[None, None, :] + entry_y[:, :, None] * freq_y[None, None, :])
        cosine, sine = jnp.cos(angle), jnp.sin(angle)
        row_re = (image_re[:, None, :] * cosine - image_im[:, None, :] * sine).astype(jnp.bfloat16).reshape(PART_DEV * S, PIX)
        row_im = (image_re[:, None, :] * sine + image_im[:, None, :] * cosine).astype(jnp.bfloat16).reshape(PART_DEV * S, PIX)
        row_pairs = lax.optimization_barrier(jnp.stack([row_re, row_im], 0)).astype(jnp.float32)
        onehot = (orient_ids[:, None] == orient_range[None, :]).astype(jnp.float32)
        mixing = (insert_weight.astype(jnp.float32)[:, :, None] * onehot[:, None, :]).reshape(PART_DEV * S, CLASSES * ORIENTS)
        increment = jnp.einsum("em,rej->rmj", mixing, row_pairs, precision=lax.Precision.HIGHEST)
        return volume + increment.reshape(2, CLASSES, ORIENTS, PIX), class_prob

    start_volume = jnp.zeros((2, CLASSES, ORIENTS, PIX), jnp.float32)
    volume, probs = lax.scan(scan_step, start_volume, jnp.arange(block_count, dtype=jnp.int32))
    return probs.reshape(PARTICLES, CLASSES), volume
```

```python
import functools
import math

import jax
import jax.numpy as jnp
import numpy as np
from jax import lax
from jax.experimental import pallas as pl
from jax.experimental.pallas import tpu as pltpu
from jax.sharding import PartitionSpec as P

IMG = 256
TX = 8
TY = 8
HALF = TX // 2
LANES = 128
BF = jnp.bfloat16
F32 = jnp.float32


def trig_tables():
    steps = np.arange(1, HALF + 1)
    angle_x = 2.0 * math.pi / IMG * steps[:, None] * (np.arange(IMG) - IMG // 2)[None, :]
    angle_y = 2.0 * math.pi / IMG * np.arange(IMG // 2)[:, None] * steps[None, :]
    table_x = np.concatenate([np.cos(angle_x), np.sin(angle_x)], 0).astype(np.float32)
    table_y = np.concatenate([np.cos(angle_y), np.sin(angle_y)], 1).astype(np.float32)
    return table_x, table_y.reshape(-1)


def xor_pairs(size, step):
    return [(i, i ^ step) for i in range(size)]


def bands_kernel(ids, images, *rest):
    outs, sems = rest[:-1], rest[-1]
    width = outs[0].shape[2]
    copies = []
    for place, out in enumerate(outs):
        band = ids[0] ^ (place + 1)
        start = pl.multiple_of(band * width, width)
        copies.append(
            pltpu.make_async_copy(images.at[:, :, pl.ds(start, width)], out, sems.at[place])
        )
    for copy in copies:
        copy.start()
    for copy in copies:
        copy.wait()


def image_bands(ids, images, dom):
    parts, rows, pixels = images.shape
    width = pixels // dom
    return pl.pallas_call(
        bands_kernel,
        out_shape=[jax.ShapeDtypeStruct((parts, rows, width), images.dtype)] * (dom - 1),
        in_specs=[pl.BlockSpec(memory_space=pltpu.SMEM), pl.BlockSpec(memory_space=pl.ANY)],
        out_specs=[pl.BlockSpec(memory_space=pl.ANY)] * (dom - 1),
        scratch_shapes=[pltpu.SemaphoreType.DMA((dom - 1,))],
        name="image_bands",
    )(ids, images)


def logits_kernel(groups, ids, table_y, table_x, refs, *rest):
    images, outs = rest[:groups], rest[groups : 2 * groups]
    left, right = rest[2 * groups :]
    step = pl.program_id(0)
    chunk = refs.shape[3]
    rows = images[0].shape[1]
    group_rows = TX * rows
    names = refs.shape[1] * refs.shape[2]
    lines = chunk // IMG
    line_base = (ids[0] * pl.num_programs(0) + step) * lines
    for line in range(lines):
        cols = slice(line * IMG, (line + 1) * IMG)
        cols_im = slice(chunk + line * IMG, chunk + (line + 1) * IMG)
        base = (line_base + line) * TY
        ref_re = refs[0, :, :, cols].astype(F32).reshape(names, IMG)
        ref_im = refs[1, :, :, cols].astype(F32).reshape(names, IMG)

        def put_ref(b, re, im):
            right[b * names : (b + 1) * names, cols] = re.astype(BF)
            right[b * names : (b + 1) * names, cols_im] = im.astype(BF)

        put_ref(TY // 2, ref_re, ref_im)
        for t in range(1, HALF + 1):
            cosine = table_y[base + t - 1]
            sine = table_y[base + HALF + t - 1]
            re_c, im_s = ref_re * cosine, ref_im * sine
            im_c, re_s = ref_im * cosine, ref_re * sine
            put_ref(TY // 2 - t, re_c - im_s, im_c + re_s)
            if t < HALF:
                put_ref(TY // 2 + t, re_c + im_s, im_c - re_s)
        for g in range(groups):
            re = images[g][0, :, cols].astype(F32)
            im = images[g][1, :, cols].astype(F32)

            def put(a, re, im):
                top = g * group_rows + a * rows
                left[top : top + rows, cols] = re.astype(BF)
                left[top : top + rows, cols_im] = im.astype(BF)

            put(TX // 2, re, im)
            for t in range(1, HALF + 1):
                cosine = table_x[t - 1 : t, :]
                sine = table_x[HALF + t - 1 : HALF + t, :]
                re_c, im_s = re * cosine, im * sine
                re_s, im_c = re * sine, im * cosine
                put(TX // 2 - t, re_c + im_s, im_c - re_s)
                if t < HALF:
                    put(TX // 2 + t, re_c - im_s, re_s + im_c)
    value = lax.dot_general(
        left[...], right[...], (((1,), (1,)), ((), ())), preferred_element_type=F32
    )

    @pl.when(step == 0)
    def _():
        for g in range(groups):
            outs[g][...] = value[g * group_rows : (g + 1) * group_rows]

    @pl.when(step > 0)
    def _():
        for g in range(groups):
            outs[g][...] += value[g * group_rows : (g + 1) * group_rows]


def chunk_of(width):
    return min(width, 4 * IMG)


def partial_logits(ids, table_x, table_y, refs, own, others):
    parts, classes, orients, width = refs.shape
    chunk = chunk_of(width)
    count = width // chunk
    arrays = ([own] if own is not None else []) + list(others)
    groups = len(arrays)
    rows = arrays[0].shape[1]
    names = classes * orients
    specs = []
    for array in arrays:
        if array is own:
            specs.append(
                pl.BlockSpec((parts, rows, chunk), lambda i, s: (0, 0, s[0] * count + i))
            )
        else:
            specs.append(pl.BlockSpec((parts, rows, chunk), lambda i, s: (0, 0, i)))
    out_shape = (TX * rows, TY * names)
    return pl.pallas_call(
        functools.partial(logits_kernel, groups),
        out_shape=[jax.ShapeDtypeStruct(out_shape, F32)] * groups,
        grid_spec=pltpu.PrefetchScalarGridSpec(
            num_scalar_prefetch=1,
            grid=(count,),
            in_specs=[
                pl.BlockSpec(memory_space=pltpu.SMEM),
                pl.BlockSpec((TX, IMG), lambda i, s: (0, 0)),
                pl.BlockSpec((parts, classes, orients, chunk), lambda i, s: (0, 0, 0, i)),
            ]
            + specs,
            out_specs=[pl.BlockSpec(out_shape, lambda i, s: (0, 0))] * groups,
            scratch_shapes=[
                pltpu.VMEM((groups * TX * rows, 2 * chunk), BF),
                pltpu.VMEM((TY * names, 2 * chunk), BF),
            ],
        ),
        compiler_params=pltpu.CompilerParams(vmem_limit_bytes=32 * 1024 * 1024),
        cost_estimate=pl.CostEstimate(
            flops=2 * groups * TX * rows * TY * names * 2 * width,
            bytes_accessed=2 * 2 * width * (groups * rows + names),
            transcendentals=0,
        ),
        name="partial_logits",
    )(ids, table_y, table_x, refs, *arrays)


def stats_kernel(swap, classes, orients, here, there, out):
    groups, group_rows, lanes = here.shape
    rows = group_rows // TX
    lane = lax.broadcasted_iota(jnp.int32, (rows, lanes), 1)
    class_of = (lane // orients) % classes
    out_lane = lax.broadcasted_iota(jnp.int32, (rows, LANES), 1)
    for g in range(groups):
        logits = here[g] + there[g ^ swap]
        pieces = [logits[a * rows : (a + 1) * rows] for a in range(TX)]
        top = functools.reduce(jnp.maximum, pieces)
        top = jnp.max(top, axis=1, keepdims=True)
        sums = sum(jnp.exp(piece - top) for piece in pieces)
        line = jnp.where(out_lane == 0, top, 0.0)
        for k in range(classes):
            part = jnp.sum(jnp.where(class_of == k, sums, 0.0), axis=1, keepdims=True)
            line = jnp.where(out_lane == k + 1, part, line)
        out[g * rows : (g + 1) * rows, :] = line


def logit_stats(here, there, swap, classes, orients):
    groups, group_rows, lanes = here.shape
    return pl.pallas_call(
        functools.partial(stats_kernel, swap, classes, orients),
        out_shape=jax.ShapeDtypeStruct((groups * group_rows // TX, LANES), F32),
        cost_estimate=pl.CostEstimate(
            flops=4 * here.size, bytes_accessed=8 * here.size, transcendentals=here.size
        ),
        name="logit_stats",
    )(here, there)


def rows_kernel(groups, ids, table_y, table_x, *rest):
    metas, images = rest[:groups], rest[groups : 2 * groups]
    out, phase_c, phase_s = rest[2 * groups :]
    step = pl.program_id(0)
    chunk = out.shape[2]
    rows = images[0].shape[1]
    lines = chunk // IMG
    line_base = (ids[0] * pl.num_programs(0) + step) * lines

    def offsets(g):
        shift = metas[g][:, 1:2].astype(jnp.int32)
        move_x = shift % TX - TX // 2
        move_y = shift // TX - TY // 2
        return move_x, move_y

    @pl.when(step == 0)
    def _():
        for g in range(groups):
            move = jnp.broadcast_to(offsets(g)[0], (rows, IMG))
            cosine = jnp.ones((rows, IMG), F32)
            sine = jnp.zeros((rows, IMG), F32)
            for t in range(1, HALF + 1):
                hit = jnp.abs(move) == t
                cosine = jnp.where(hit, table_x[t - 1 : t, :], cosine)
                sine = jnp.where(hit, table_x[HALF + t - 1 : HALF + t, :], sine)
            phase_c[g * rows : (g + 1) * rows, :] = cosine
            phase_s[g * rows : (g + 1) * rows, :] = jnp.where(move < 0, -sine, sine)

    for g in range(groups):
        own = slice(g * rows, (g + 1) * rows)
        move = jnp.broadcast_to(offsets(g)[1], (rows, LANES))
        hits = [jnp.abs(move) == t for t in range(1, HALF + 1)]
        sign = jnp.where(move < 0, -1.0, 1.0)
        for line in range(lines):
            base = (line_base + line) * TY
            cos_y = jnp.ones((rows, LANES), F32)
            sin_y = jnp.zeros((rows, LANES), F32)
            for t in range(1, HALF + 1):
                cos_y = jnp.where(hits[t - 1], table_y[base + t - 1], cos_y)
                sin_y = jnp.where(hits[t - 1], table_y[base + HALF + t - 1], sin_y)
            sin_y = sin_y * sign
            for part in range(IMG // LANES):
                across = slice(part * LANES, (part + 1) * LANES)
                cols = slice(line * IMG + part * LANES, line * IMG + (part + 1) * LANES)
                cos_x, sin_x = phase_c[own, across], phase_s[own, across]
                cosine = cos_x * cos_y - sin_x * sin_y
                sine = sin_x * cos_y + cos_x * sin_y
                re = images[g][0, :, cols].astype(F32)
                im = images[g][1, :, cols].astype(F32)
                out[0, own, cols] = (re * cosine - im * sine).astype(BF)
                out[1, own, cols] = (re * sine + im * cosine).astype(BF)


def aligned_rows(ids, table_x, table_y, metas, own, others, dom):
    parts, rows, pixels = own.shape
    width = pixels // dom
    chunk = chunk_of(width)
    count = width // chunk
    groups = len(metas)
    return pl.pallas_call(
        functools.partial(rows_kernel, groups),
        out_shape=jax.ShapeDtypeStruct((parts, groups * rows, width), BF),
        grid_spec=pltpu.PrefetchScalarGridSpec(
            num_scalar_prefetch=1,
            grid=(count,),
            in_specs=[
                pl.BlockSpec(memory_space=pltpu.SMEM),
                pl.BlockSpec((TX, IMG), lambda i, s: (0, 0)),
            ]
            + [pl.BlockSpec((rows, LANES), lambda i, s: (0, 0))] * groups
            + [pl.BlockSpec((parts, rows, chunk), lambda i, s: (0, 0, s[0] * count + i))]
            + [pl.BlockSpec((parts, rows, chunk), lambda i, s: (0, 0, i))] * (groups - 1),
            out_specs=pl.BlockSpec((parts, groups * rows, chunk), lambda i, s: (0, 0, i)),
            scratch_shapes=[
                pltpu.VMEM((groups * rows, IMG), F32),
                pltpu.VMEM((groups * rows, IMG), F32),
            ],
        ),
        compiler_params=pltpu.CompilerParams(vmem_limit_bytes=32 * 1024 * 1024),
        cost_estimate=pl.CostEstimate(
            flops=20 * groups * rows * width,
            bytes_accessed=8 * groups * rows * width,
            transcendentals=0,
        ),
        name="aligned_rows",
    )(ids, table_y, table_x, *metas, own, *others)


def volume_kernel(groups, orients, classes, ids, *rest):
    stats, metas = rest[:4], rest[4 : 4 + groups]
    aligned = rest[4 + groups]
    prob, outs, mix = rest[5 + groups], rest[6 + groups : -1], rest[-1]
    step = pl.program_id(0)
    rows = metas[0].shape[0]

    @pl.when(step == 0)
    def _():
        lane = lax.broadcasted_iota(jnp.int32, (rows, LANES), 1)
        pieces = []
        for g in range(groups):
            near, far = (stats[0], stats[2]) if g % 2 == 0 else (stats[1], stats[3])
            place = g // 2
            near = near[place * rows : (place + 1) * rows, :]
            far = far[place * rows : (place + 1) * rows, :]
            top = jnp.maximum(near[:, 0:1], far[:, 0:1])
            near_scale = jnp.exp(near[:, 0:1] - top)
            far_scale = jnp.exp(far[:, 0:1] - top)
            held = (lane >= 1) & (lane <= classes)
            both = jnp.where(held, near * near_scale + far * far_scale, 0.0)
            totals = jnp.sum(both, axis=1, keepdims=True)
            spread = jnp.zeros((rows, LANES), F32)
            for k in range(classes):
                spread = jnp.where(lane % classes == k, near[:, k + 1 : k + 2], spread)
            class_prob = spread * near_scale / totals
            if g == 0:
                prob[...] = class_prob
            weight = (metas[g][:, 2:3] * class_prob).astype(BF).astype(F32)
            bin_of = metas[g][:, 0:1].astype(jnp.int32) ^ ids[1]
            pieces.append(jnp.where(lane // classes == bin_of, weight, 0.0))
        mixing = jnp.concatenate(pieces, axis=0)
        mix[...] = jnp.transpose(mixing)[: orients * classes].astype(BF)

    for part in range(2):
        value = jnp.dot(mix[...], aligned[part], preferred_element_type=F32)
        for o in range(orients):
            outs[o][part] = value[o * classes : (o + 1) * classes].astype(outs[o].dtype)


def volume_terms(ids, stats, metas, aligned, orients, classes):
    parts, entries, width = aligned.shape
    groups = len(metas)
    rows = entries // groups
    chunk = chunk_of(width)
    count = width // chunk
    out_shape = (parts, classes, width)
    fixed = lambda i, s: (0, 0)
    return pl.pallas_call(
        functools.partial(volume_kernel, groups, orients, classes),
        out_shape=[jax.ShapeDtypeStruct((rows, LANES), F32)]
        + [
            jax.ShapeDtypeStruct(out_shape, F32 if o == 0 else BF)
            for o in range(orients)
        ],
        grid_spec=pltpu.PrefetchScalarGridSpec(
            num_scalar_prefetch=1,
            grid=(count,),
            in_specs=[pl.BlockSpec(stats[0].shape, fixed)] * 4
            + [pl.BlockSpec((rows, LANES), fixed)] * groups
            + [pl.BlockSpec((parts, entries, chunk), lambda i, s: (0, 0, i))],
            out_specs=[pl.BlockSpec((rows, LANES), fixed)]
            + [pl.BlockSpec((parts, classes, chunk), lambda i, s: (0, 0, i))] * orients,
            scratch_shapes=[pltpu.VMEM((orients * classes, entries), BF)],
        ),
        cost_estimate=pl.CostEstimate(
            flops=4 * orients * classes * entries * width,
            bytes_accessed=4 * entries * width + 4 * orients * classes * width,
            transcendentals=0,
        ),
        name="volume_terms",
    )(ids, *stats, *metas, aligned)


def local(dom, orient, cls, references, images, orient_lists, shift_ids, fixed_weights):
    classes, orients = references.shape[1], references.shape[2]
    table_x, table_y = (jnp.asarray(t) for t in trig_tables())
    ids = jnp.stack([lax.axis_index("dom"), lax.axis_index("orient")]).astype(jnp.int32)
    rows = images.shape[1]

    def swap_dom(array, step):
        return lax.ppermute(array, "dom", xor_pairs(dom, step))

    refs = lax.all_gather(references, "orient", axis=3, tiled=True)
    bands = image_bands(ids, images, dom)
    others = [swap_dom(band, step + 1) for step, band in enumerate(bands)]
    meta = jnp.concatenate(
        [orient_lists.astype(F32), shift_ids.astype(F32), fixed_weights], axis=1
    )
    meta = jnp.pad(meta, ((0, 0), (0, LANES - meta.shape[1])))
    metas = [meta] + [swap_dom(meta, step) for step in range(1, dom)]

    near = partial_logits(ids, table_x, table_y, refs, images, others[:1])
    far = partial_logits(ids, table_x, table_y, refs, None, others[1:])
    partial = list(near) + list(far)
    kept = [partial[s] + swap_dom(partial[s ^ 1], 1) for s in range(0, dom, 2)]
    here = jnp.stack(kept)
    step = 2
    there, swap = jnp.zeros_like(here), 0
    while step < dom:
        there, swap = swap_dom(here, step), step // 2
        if step * 2 < dom:
            order = np.arange(dom // 2) ^ swap
            here = here + jnp.stack([there[i] for i in order])
        step *= 2
    stats = logit_stats(here, there, swap, classes, orients)

    pairs = [(i, i ^ dom) for i in range(cls * dom)]
    cross = [(i, i ^ dom ^ 1) for i in range(cls * dom)]
    stats_all = [
        stats,
        swap_dom(stats, 1),
        lax.ppermute(stats, ("cls", "dom"), pairs),
        lax.ppermute(stats, ("cls", "dom"), cross),
    ]
    aligned = aligned_rows(ids, table_x, table_y, metas, images, others, dom)
    prob, *terms = volume_terms(ids, stats_all, metas, aligned, orients, classes)
    volume = terms[0]
    for o in range(1, orients):
        volume = volume + lax.ppermute(terms[o], "orient", xor_pairs(orient, o)).astype(F32)
    return prob[:, :classes], volume[:, :, None, :]


def solution(mesh):
    in_specs = (
        P(None, "cls", None, ("dom", "orient")),
        P(None, ("dom", "orient"), None),
        P(("dom", "orient"), None),
        P(("dom", "orient"), None),
        P(("dom", "orient"), None),
    )
    out_specs = (P(("dom", "orient"), "cls"), P(None, "cls", "orient", "dom"))
    body = functools.partial(local, mesh.shape["dom"], mesh.shape["orient"], mesh.shape["cls"])
    return jax.shard_map(body, mesh=mesh, in_specs=in_specs, out_specs=out_specs, check_vma=False)
```

```python
import functools
import math

import jax
import jax.numpy as jnp
import numpy as np
from jax import lax
from jax.experimental import pallas as pl
from jax.experimental.pallas import tpu as pltpu
from jax.sharding import PartitionSpec as P

IMG = 256
TX = 8
TY = 8
HALF = TX // 2
LANES = 128
VMEM_BYTES = 24 * 1024 * 1024
BF = jnp.bfloat16
F32 = jnp.float32


def trig_tables():
    steps = np.arange(1, HALF + 1)
    angle_x = 2.0 * math.pi / IMG * steps[:, None] * (np.arange(IMG) - IMG // 2)[None, :]
    angle_y = 2.0 * math.pi / IMG * np.arange(IMG // 2)[:, None] * steps[None, :]
    table_x = np.concatenate([np.cos(angle_x), np.sin(angle_x)], 0).astype(np.float32)
    table_y = np.concatenate([np.cos(angle_y), np.sin(angle_y)], 1).astype(np.float32)
    return table_x, table_y.reshape(-1)


def chunk_of(width):
    return min(width, 8 * IMG)


def xor_pairs(size, step):
    return [(i, i ^ step) for i in range(size)]


def bands_kernel(ids, *refs):
    half = len(refs) // 2
    for source, target in zip(refs[:half], refs[half:]):
        target[...] = source[...]


def image_bands(ids, images, dom):
    parts, rows, pixels = images.shape
    width = pixels // dom
    chunk = min(width, 16 * IMG)
    count = width // chunk

    def spec(step):
        return pl.BlockSpec(
            (parts, rows, chunk), lambda i, s: (0, 0, (s[0] ^ step) * count + i)
        )

    return pl.pallas_call(
        bands_kernel,
        out_shape=[jax.ShapeDtypeStruct((parts, rows, width), images.dtype)] * (dom - 1),
        grid_spec=pltpu.PrefetchScalarGridSpec(
            num_scalar_prefetch=1,
            grid=(count,),
            in_specs=[spec(step) for step in range(1, dom)],
            out_specs=[pl.BlockSpec((parts, rows, chunk), lambda i, s: (0, 0, i))] * (dom - 1),
        ),
        compiler_params=pltpu.CompilerParams(vmem_limit_bytes=VMEM_BYTES),
        cost_estimate=pl.CostEstimate(
            flops=0, bytes_accessed=4 * parts * rows * (pixels - width), transcendentals=0
        ),
        name="image_bands",
    )(ids, *([images] * (dom - 1)))


def logits_kernel(groups, orients, span, ids, table_y, table_x, *rest):
    shards, rest = rest[:orients], rest[orients:]
    images, outs = rest[:groups], rest[groups : 2 * groups]
    refs, buffers = rest[2 * groups], rest[2 * groups + 1 :]
    step = pl.program_id(0)
    chunk = refs.shape[3]
    rows = images[0].shape[1]
    group_rows = TX * rows
    names = refs.shape[1] * refs.shape[2]
    lines = chunk // IMG
    line_base = (ids[0] * orients + (ids[1] ^ step)) * lines
    for place, shard in enumerate(shards):

        @pl.when(step == place)
        def _():
            refs[...] = shard[...]

    @pl.when(step == 0)
    def _():
        for out in outs:
            out[...] = jnp.zeros_like(out)

    for line in range(lines):
        left, right = buffers[2 * (line // span % 2) : 2 * (line // span % 2) + 2]
        cols = slice(line * IMG, (line + 1) * IMG)
        place = line % span
        to_re = slice(2 * place * IMG, (2 * place + 1) * IMG)
        to_im = slice((2 * place + 1) * IMG, (2 * place + 2) * IMG)
        base = (line_base + line) * TY
        ref_re = refs[0, :, :, cols].astype(F32).reshape(names, IMG)
        ref_im = refs[1, :, :, cols].astype(F32).reshape(names, IMG)

        def put_ref(b, re, im):
            right[b * names : (b + 1) * names, to_re] = re.astype(BF)
            right[b * names : (b + 1) * names, to_im] = im.astype(BF)

        put_ref(TY // 2, ref_re, ref_im)
        for t in range(1, HALF + 1):
            cosine = table_y[base + t - 1]
            sine = table_y[base + HALF + t - 1]
            re_c, im_s = ref_re * cosine, ref_im * sine
            im_c, re_s = ref_im * cosine, ref_re * sine
            put_ref(TY // 2 - t, re_c - im_s, im_c + re_s)
            if t < HALF:
                put_ref(TY // 2 + t, re_c + im_s, im_c - re_s)
        for g in range(groups):
            re = images[g][0, :, cols].astype(F32)
            im = images[g][1, :, cols].astype(F32)

            def put(a, re, im):
                top = g * group_rows + a * rows
                left[top : top + rows, to_re] = re.astype(BF)
                left[top : top + rows, to_im] = im.astype(BF)

            put(TX // 2, re, im)
            for t in range(1, HALF + 1):
                cosine = table_x[t - 1 : t, :]
                sine = table_x[HALF + t - 1 : HALF + t, :]
                re_c, im_s = re * cosine, im * sine
                re_s, im_c = re * sine, im * cosine
                put(TX // 2 - t, re_c + im_s, im_c - re_s)
                if t < HALF:
                    put(TX // 2 + t, re_c - im_s, re_s + im_c)
        if place == span - 1:
            value = lax.dot_general(
                left[...], right[...], (((1,), (1,)), ((), ())), preferred_element_type=F32
            )
            for g in range(groups):
                outs[g][...] += value[g * group_rows : (g + 1) * group_rows]


def partial_logits(ids, table_x, table_y, shards, own, others):
    parts, classes, orients, chunk = shards[0].shape
    arrays = ([own] if own is not None else []) + list(others)
    groups = len(arrays)
    rows = arrays[0].shape[1]
    names = classes * orients
    count = len(shards)
    lines = chunk // IMG
    span = 2 if lines % 4 == 0 else 1
    specs = []
    for array in arrays:
        if array is own:
            specs.append(
                pl.BlockSpec(
                    (parts, rows, chunk), lambda i, s: (0, 0, s[0] * count + (s[1] ^ i))
                )
            )
        else:
            specs.append(pl.BlockSpec((parts, rows, chunk), lambda i, s: (0, 0, s[1] ^ i)))
    out_shape = (TX * rows, TY * names)
    return pl.pallas_call(
        functools.partial(logits_kernel, groups, count, span),
        out_shape=[jax.ShapeDtypeStruct(out_shape, F32)] * groups,
        grid_spec=pltpu.PrefetchScalarGridSpec(
            num_scalar_prefetch=1,
            grid=(count,),
            in_specs=[
                pl.BlockSpec(memory_space=pltpu.SMEM),
                pl.BlockSpec((TX, IMG), lambda i, s: (0, 0)),
            ]
            + [pl.BlockSpec(shards[0].shape, lambda i, s: (0, 0, 0, 0))] * count
            + specs,
            out_specs=[pl.BlockSpec(out_shape, lambda i, s: (0, 0))] * groups,
            scratch_shapes=[pltpu.VMEM(shards[0].shape, BF)]
            + [
                pltpu.VMEM((groups * TX * rows, 2 * span * IMG), BF),
                pltpu.VMEM((TY * names, 2 * span * IMG), BF),
            ]
            * 2,
        ),
        compiler_params=pltpu.CompilerParams(vmem_limit_bytes=VMEM_BYTES),
        cost_estimate=pl.CostEstimate(
            flops=4 * groups * TX * rows * TY * names * count * chunk,
            bytes_accessed=4 * count * chunk * (groups * rows + names),
            transcendentals=0,
        ),
        name="partial_logits",
    )(ids, table_y, table_x, *shards, *arrays)


def stats_kernel(swap, classes, orients, here, there, out):
    groups, group_rows, lanes = here.shape
    rows = group_rows // TX
    lane = lax.broadcasted_iota(jnp.int32, (rows, lanes), 1)
    class_of = (lane // orients) % classes
    out_lane = lax.broadcasted_iota(jnp.int32, (rows, LANES), 1)
    for g in range(groups):
        logits = here[g] + there[g ^ swap]
        pieces = [logits[a * rows : (a + 1) * rows] for a in range(TX)]
        top = functools.reduce(jnp.maximum, pieces)
        top = jnp.max(top, axis=1, keepdims=True)
        sums = sum(jnp.exp(piece - top) for piece in pieces)
        line = jnp.where(out_lane == 0, top, 0.0)
        for k in range(classes):
            part = jnp.sum(jnp.where(class_of == k, sums, 0.0), axis=1, keepdims=True)
            line = jnp.where(out_lane == k + 1, part, line)
        out[g * rows : (g + 1) * rows, :] = line


def logit_stats(here, there, swap, classes, orients):
    groups, group_rows, lanes = here.shape
    return pl.pallas_call(
        functools.partial(stats_kernel, swap, classes, orients),
        out_shape=jax.ShapeDtypeStruct((groups * group_rows // TX, LANES), F32),
        compiler_params=pltpu.CompilerParams(vmem_limit_bytes=VMEM_BYTES),
        cost_estimate=pl.CostEstimate(
            flops=4 * here.size, bytes_accessed=8 * here.size, transcendentals=here.size
        ),
        name="logit_stats",
    )(here, there)


def rows_kernel(groups, ids, table_y, table_x, *rest):
    metas, images = rest[:groups], rest[groups : 2 * groups]
    out, phase_c, phase_s = rest[2 * groups :]
    step = pl.program_id(0)
    chunk = out.shape[2]
    rows = images[0].shape[1]
    lines = chunk // IMG
    line_base = (ids[0] * pl.num_programs(0) + step) * lines

    def offsets(g):
        shift = metas[g][:, 1:2].astype(jnp.int32)
        move_x = shift % TX - TX // 2
        move_y = shift // TX - TY // 2
        return move_x, move_y

    @pl.when(step == 0)
    def _():
        for g in range(groups):
            move = jnp.broadcast_to(offsets(g)[0], (rows, IMG))
            cosine = jnp.ones((rows, IMG), F32)
            sine = jnp.zeros((rows, IMG), F32)
            for t in range(1, HALF + 1):
                hit = jnp.abs(move) == t
                cosine = jnp.where(hit, table_x[t - 1 : t, :], cosine)
                sine = jnp.where(hit, table_x[HALF + t - 1 : HALF + t, :], sine)
            phase_c[g * rows : (g + 1) * rows, :] = cosine
            phase_s[g * rows : (g + 1) * rows, :] = jnp.where(move < 0, -sine, sine)

    for g in range(groups):
        own = slice(g * rows, (g + 1) * rows)
        move = jnp.broadcast_to(offsets(g)[1], (rows, LANES))
        hits = [jnp.abs(move) == t for t in range(1, HALF + 1)]
        sign = jnp.where(move < 0, -1.0, 1.0)
        for line in range(lines):
            base = (line_base + line) * TY
            cos_y = jnp.ones((rows, LANES), F32)
            sin_y = jnp.zeros((rows, LANES), F32)
            for t in range(1, HALF + 1):
                cos_y = jnp.where(hits[t - 1], table_y[base + t - 1], cos_y)
                sin_y = jnp.where(hits[t - 1], table_y[base + HALF + t - 1], sin_y)
            sin_y = sin_y * sign
            for part in range(IMG // LANES):
                across = slice(part * LANES, (part + 1) * LANES)
                cols = slice(line * IMG + part * LANES, line * IMG + (part + 1) * LANES)
                cos_x, sin_x = phase_c[own, across], phase_s[own, across]
                cosine = cos_x * cos_y - sin_x * sin_y
                sine = sin_x * cos_y + cos_x * sin_y
                re = images[g][0, :, cols].astype(F32)
                im = images[g][1, :, cols].astype(F32)
                out[0, own, cols] = (re * cosine - im * sine).astype(BF)
                out[1, own, cols] = (re * sine + im * cosine).astype(BF)


def aligned_rows(ids, table_x, table_y, metas, own, others, width):
    arrays = ([own] if own is not None else []) + list(others)
    parts, rows = arrays[0].shape[:2]
    chunk = chunk_of(width)
    count = width // chunk
    groups = len(metas)
    specs = []
    for array in arrays:
        if array is own:
            specs.append(
                pl.BlockSpec((parts, rows, chunk), lambda i, s: (0, 0, s[0] * count + i))
            )
        else:
            specs.append(pl.BlockSpec((parts, rows, chunk), lambda i, s: (0, 0, i)))
    return pl.pallas_call(
        functools.partial(rows_kernel, groups),
        out_shape=jax.ShapeDtypeStruct((parts, groups * rows, width), BF),
        grid_spec=pltpu.PrefetchScalarGridSpec(
            num_scalar_prefetch=1,
            grid=(count,),
            in_specs=[
                pl.BlockSpec(memory_space=pltpu.SMEM),
                pl.BlockSpec((TX, IMG), lambda i, s: (0, 0)),
            ]
            + [pl.BlockSpec((rows, LANES), lambda i, s: (0, 0))] * groups
            + specs,
            out_specs=pl.BlockSpec((parts, groups * rows, chunk), lambda i, s: (0, 0, i)),
            scratch_shapes=[
                pltpu.VMEM((groups * rows, IMG), F32),
                pltpu.VMEM((groups * rows, IMG), F32),
            ],
        ),
        compiler_params=pltpu.CompilerParams(vmem_limit_bytes=VMEM_BYTES),
        cost_estimate=pl.CostEstimate(
            flops=20 * groups * rows * width,
            bytes_accessed=8 * groups * rows * width,
            transcendentals=0,
        ),
        name="aligned_rows",
    )(ids, table_y, table_x, *metas, *arrays)


def volume_kernel(groups, orients, classes, ids, *rest):
    stats, metas = rest[:4], rest[4 : 4 + groups]
    near, far = rest[4 + groups], rest[5 + groups]
    prob, outs, mixes = rest[6 + groups], rest[7 + groups : -2], rest[-2:]
    step = pl.program_id(0)
    rows = metas[0].shape[0]

    @pl.when(step == 0)
    def _():
        lane = lax.broadcasted_iota(jnp.int32, (rows, LANES), 1)
        pieces = []
        for g in range(groups):
            mine, other = (stats[0], stats[2]) if g % 2 == 0 else (stats[1], stats[3])
            place = g // 2
            mine = mine[place * rows : (place + 1) * rows, :]
            other = other[place * rows : (place + 1) * rows, :]
            top = jnp.maximum(mine[:, 0:1], other[:, 0:1])
            mine_scale = jnp.exp(mine[:, 0:1] - top)
            other_scale = jnp.exp(other[:, 0:1] - top)
            held = (lane >= 1) & (lane <= classes)
            both = jnp.where(held, mine * mine_scale + other * other_scale, 0.0)
            totals = jnp.sum(both, axis=1, keepdims=True)
            spread = jnp.zeros((rows, LANES), F32)
            for k in range(classes):
                spread = jnp.where(lane % classes == k, mine[:, k + 1 : k + 2], spread)
            class_prob = spread * mine_scale / totals
            if g == 0:
                prob[...] = class_prob
            weight = (metas[g][:, 2:3] * class_prob).astype(BF).astype(F32)
            bin_of = metas[g][:, 0:1].astype(jnp.int32) ^ ids[1]
            pieces.append(jnp.where(lane // classes == bin_of, weight, 0.0))
        for mix, held in zip(mixes, (pieces[:2], pieces[2:])):
            mixing = jnp.concatenate(held, axis=0)
            mix[...] = jnp.transpose(mixing)[: orients * classes].astype(BF)

    for part in range(2):
        value = jnp.dot(mixes[0][...], near[part], preferred_element_type=F32)
        value += jnp.dot(mixes[1][...], far[part], preferred_element_type=F32)
        for o in range(orients):
            outs[o][part] = value[o * classes : (o + 1) * classes].astype(outs[o].dtype)


def volume_terms(ids, stats, metas, near, far, orients, classes):
    parts, entries, width = near.shape
    rest = far.shape[1]
    groups = len(metas)
    rows = metas[0].shape[0]
    chunk = chunk_of(width)
    count = width // chunk
    out_shape = (parts, classes, width)
    fixed = lambda i, s: (0, 0)
    return pl.pallas_call(
        functools.partial(volume_kernel, groups, orients, classes),
        out_shape=[jax.ShapeDtypeStruct((rows, LANES), F32)]
        + [
            jax.ShapeDtypeStruct(out_shape, F32 if o == 0 else BF)
            for o in range(orients)
        ],
        grid_spec=pltpu.PrefetchScalarGridSpec(
            num_scalar_prefetch=1,
            grid=(count,),
            in_specs=[pl.BlockSpec(stats[0].shape, fixed)] * 4
            + [pl.BlockSpec((rows, LANES), fixed)] * groups
            + [
                pl.BlockSpec((parts, entries, chunk), lambda i, s: (0, 0, i)),
                pl.BlockSpec((parts, rest, chunk), lambda i, s: (0, 0, i)),
            ],
            out_specs=[pl.BlockSpec((rows, LANES), fixed)]
            + [pl.BlockSpec((parts, classes, chunk), lambda i, s: (0, 0, i))] * orients,
            scratch_shapes=[
                pltpu.VMEM((orients * classes, entries), BF),
                pltpu.VMEM((orients * classes, rest), BF),
            ],
        ),
        compiler_params=pltpu.CompilerParams(vmem_limit_bytes=VMEM_BYTES),
        cost_estimate=pl.CostEstimate(
            flops=4 * orients * classes * (entries + rest) * width,
            bytes_accessed=4 * (entries + rest) * width + 4 * orients * classes * width,
            transcendentals=0,
        ),
        name="volume_terms",
    )(ids, *stats, *metas, near, far)


def total_kernel(first, *rest):
    out = rest[-1]
    total = first[...]
    for term in rest[:-1]:
        total = total + term[...].astype(F32)
    for part in range(out.shape[0]):
        for k in range(out.shape[1]):
            out[part, k] = total[part, k : k + 1]


def total_volume(terms):
    parts, classes, width = terms[0].shape
    return pl.pallas_call(
        total_kernel,
        out_shape=jax.ShapeDtypeStruct((parts, classes, 1, width), F32),
        compiler_params=pltpu.CompilerParams(vmem_limit_bytes=VMEM_BYTES),
        name="total_volume",
    )(*terms)


def local(dom, orient, cls, references, images, orient_lists, shift_ids, fixed_weights):
    classes, orients = references.shape[1], references.shape[2]
    table_x, table_y = (jnp.asarray(t) for t in trig_tables())
    ids = jnp.stack([lax.axis_index("dom"), lax.axis_index("orient")]).astype(jnp.int32)
    rows = images.shape[1]

    def swap_dom(array, step):
        return lax.ppermute(array, "dom", xor_pairs(dom, step))

    def swap_orient(array, step):
        return lax.ppermute(array, "orient", xor_pairs(orient, step))

    bands = image_bands(ids, images, dom)
    others = [swap_dom(band, step + 1) for step, band in enumerate(bands)]
    shards = [references] + [swap_orient(references, step) for step in range(1, orient)]
    meta = jnp.concatenate(
        [orient_lists.astype(F32), shift_ids.astype(F32), fixed_weights], axis=1
    )
    meta = jnp.pad(meta, ((0, 0), (0, LANES - meta.shape[1])))
    metas = [meta] + [swap_dom(meta, step) for step in range(1, dom)]

    width = images.shape[2] // dom
    aligned_near = aligned_rows(ids, table_x, table_y, metas[:2], images, others[:1], width)
    shards[-1], aligned_near = lax.optimization_barrier((shards[-1], aligned_near))
    near = partial_logits(ids, table_x, table_y, shards, images, others[:1])
    far = partial_logits(ids, table_x, table_y, shards, None, others[1:])
    partial = list(near) + list(far)
    kept = [partial[s] + swap_dom(partial[s ^ 1], 1) for s in range(0, dom, 2)]
    here = jnp.stack(kept)
    step = 2
    there, swap = jnp.zeros_like(here), 0
    while step < dom:
        there, swap = swap_dom(here, step), step // 2
        if step * 2 < dom:
            order = np.arange(dom // 2) ^ swap
            here = here + jnp.stack([there[i] for i in order])
        step *= 2
    aligned_far = aligned_rows(ids, table_x, table_y, metas[2:], None, others[1:], width)
    there, aligned_far = lax.optimization_barrier((there, aligned_far))
    stats = logit_stats(here, there, swap, classes, orients)

    pairs = [(i, i ^ dom) for i in range(cls * dom)]
    cross = [(i, i ^ dom ^ 1) for i in range(cls * dom)]
    stats_all = [
        stats,
        swap_dom(stats, 1),
        lax.ppermute(stats, ("cls", "dom"), pairs),
        lax.ppermute(stats, ("cls", "dom"), cross),
    ]
    prob, *terms = volume_terms(
        ids, stats_all, metas, aligned_near, aligned_far, orients, classes
    )
    terms = [terms[0]] + [swap_orient(terms[o], o) for o in range(1, orients)]
    return prob[:, :classes], total_volume(terms)


def solution(mesh):
    in_specs = (
        P(None, "cls", None, ("dom", "orient")),
        P(None, ("dom", "orient"), None),
        P(("dom", "orient"), None),
        P(("dom", "orient"), None),
        P(("dom", "orient"), None),
    )
    out_specs = (P(("dom", "orient"), "cls"), P(None, "cls", "orient", "dom"))
    body = functools.partial(local, mesh.shape["dom"], mesh.shape["orient"], mesh.shape["cls"])
    return jax.shard_map(body, mesh=mesh, in_specs=in_specs, out_specs=out_specs, check_vma=False)
```

```python
import functools
import math

import jax
import jax.numpy as jnp
import numpy as np
from jax import lax
from jax.experimental import pallas as pl
from jax.experimental.pallas import tpu as pltpu
from jax.sharding import PartitionSpec as P

IMG = 256
TX = 8
TY = 8
HALF = TX // 2
LANES = 128
VMEM_BYTES = 24 * 1024 * 1024
BF = jnp.bfloat16
F32 = jnp.float32


def trig_tables():
    steps = np.arange(1, HALF + 1)
    angle_x = 2.0 * math.pi / IMG * steps[:, None] * (np.arange(IMG) - IMG // 2)[None, :]
    angle_y = 2.0 * math.pi / IMG * np.arange(IMG // 2)[:, None] * steps[None, :]
    table_x = np.concatenate([np.cos(angle_x), np.sin(angle_x)], 0).astype(np.float32)
    table_y = np.concatenate([np.cos(angle_y), np.sin(angle_y)], 1).astype(np.float32)
    return table_x, table_y.reshape(-1)


def chunk_of(width):
    return min(width, 8 * IMG)


def xor_pairs(size, step):
    return [(i, i ^ step) for i in range(size)]


def column_of(line):
    size = line.shape[1]
    rows = lax.broadcasted_iota(jnp.int32, (size, size), 0)
    cols = lax.broadcasted_iota(jnp.int32, (size, size), 1)
    return jnp.sum(jnp.where(rows == cols, line, 0.0), axis=1, keepdims=True)


def bands_kernel(steps, ids, images, references, *rest):
    lists, rest = rest[:3], rest[3:]
    outs, meta, shard = rest[: len(steps)], rest[len(steps)], rest[len(steps) + 1]
    lines, sems, meta_sems, line_sems, shard_sem = rest[len(steps) + 2 :]
    width = outs[0].shape[2] - LANES
    copies = [pltpu.make_async_copy(references, shard, shard_sem)]
    for place, (step, out) in enumerate(zip(steps, outs)):
        start = pl.multiple_of((ids[0] ^ step) * width, width)
        for part in range(out.shape[0]):
            copies.append(
                pltpu.make_async_copy(
                    images.at[part, :, pl.ds(start, width)],
                    out.at[part, :, pl.ds(0, width)],
                    sems.at[place, part],
                )
            )
    line_copies = [
        pltpu.make_async_copy(source, lines[place], line_sems.at[place])
        for place, source in enumerate(lists)
    ]
    for copy in line_copies + copies:
        copy.start()
    for copy in line_copies:
        copy.wait()
    lane = lax.broadcasted_iota(jnp.int32, meta.shape[1:], 1)
    fixed = column_of(lines[2][...])
    high = fixed.astype(BF).astype(F32)
    middle = (fixed - high).astype(BF).astype(F32)
    values = [column_of(lines[0][...].astype(F32)), column_of(lines[1][...].astype(F32))]
    table = jnp.zeros(meta.shape[1:], F32)
    for place, value in enumerate(values + [high, middle, fixed - high - middle]):
        table = jnp.where(lane == place, value, table)
    meta[0] = table.astype(BF)
    meta[1] = jnp.zeros(meta.shape[1:], BF)
    meta_copies = [
        pltpu.make_async_copy(meta, out.at[:, :, pl.ds(width, LANES)], meta_sems.at[place])
        for place, out in enumerate(outs)
    ]
    for copy in meta_copies:
        copy.start()
    for copy in copies + meta_copies:
        copy.wait()


def image_bands(ids, orient_lists, shift_ids, fixed_weights, images, references, dom):
    parts, rows, pixels = images.shape
    width = pixels // dom
    steps = list(range(1, dom))
    sources = [images, references] + [
        array.reshape(1, rows) for array in (orient_lists, shift_ids, fixed_weights)
    ]
    sources = [pltpu.with_memory_space_constraint(array, pltpu.HBM) for array in sources]
    *bands, meta, shard = pl.pallas_call(
        functools.partial(bands_kernel, steps),
        out_shape=[pltpu.VMEM((parts, rows, width + LANES), images.dtype)] * len(steps)
        + [
            jax.ShapeDtypeStruct((parts, rows, LANES), BF),
            pltpu.VMEM(references.shape, references.dtype),
        ],
        in_specs=[pl.BlockSpec(memory_space=pltpu.SMEM)]
        + [pl.BlockSpec(memory_space=pl.ANY)] * len(sources),
        out_specs=[pl.BlockSpec(memory_space=pl.ANY)] * len(steps)
        + [pl.BlockSpec(memory_space=pltpu.VMEM), pl.BlockSpec(memory_space=pl.ANY)],
        scratch_shapes=[
            [pltpu.VMEM((1, rows), array.dtype) for array in sources[2:]],
            pltpu.SemaphoreType.DMA((len(steps), parts)),
            pltpu.SemaphoreType.DMA((len(steps),)),
            pltpu.SemaphoreType.DMA((3,)),
            pltpu.SemaphoreType.DMA,
        ],
        compiler_params=pltpu.CompilerParams(vmem_limit_bytes=VMEM_BYTES),
        cost_estimate=pl.CostEstimate(
            flops=0, bytes_accessed=4 * parts * rows * (pixels - width), transcendentals=0
        ),
        name="image_bands",
    )(ids, *sources)
    return bands, meta, shard


def image_specs(groups, own, chunk, column, base):
    parts, rows = own.shape[:2]
    block = (parts, rows, chunk)
    return [
        pl.BlockSpec(block, lambda i, s: (0, 0, base(s) + column(i, s)))
        if image is own
        else pl.BlockSpec(block, lambda i, s: (0, 0, column(i, s)))
        for image, _ in groups
    ]


def table_specs(groups):
    specs = []
    for _, table in groups:
        last = table.shape[2] // LANES - 1
        specs.append(pl.BlockSpec((1, table.shape[1], LANES), lambda i, s, last=last: (0, 0, last)))
    return specs


def logits_kernel(groups, orients, span, ids, table_y, table_x, *rest):
    shards, rest = rest[:orients], rest[orients:]
    images, rest = rest[:groups], rest[groups:]
    outs, refs, buffers = rest[:groups], rest[groups], rest[groups + 1 :]
    step = pl.program_id(0)
    chunk = refs.shape[3]
    rows = images[0].shape[1]
    group_rows = TX * rows
    names = refs.shape[1] * refs.shape[2]
    lines = chunk // IMG
    line_base = (ids[0] * orients + (ids[1] ^ step)) * lines
    for place, shard in enumerate(shards):

        @pl.when(step == place)
        def _():
            refs[...] = shard[...]

    @pl.when(step == 0)
    def _():
        for out in outs:
            out[...] = jnp.zeros_like(out)

    for line in range(lines):
        left, right = buffers[2 * (line // span % 2) : 2 * (line // span % 2) + 2]
        cols = slice(line * IMG, (line + 1) * IMG)
        place = line % span
        to_re = slice(2 * place * IMG, (2 * place + 1) * IMG)
        to_im = slice((2 * place + 1) * IMG, (2 * place + 2) * IMG)
        base = (line_base + line) * TY
        ref_re = refs[0, :, :, cols].astype(F32).reshape(names, IMG)
        ref_im = refs[1, :, :, cols].astype(F32).reshape(names, IMG)

        def put_ref(b, re, im):
            right[b * names : (b + 1) * names, to_re] = re.astype(BF)
            right[b * names : (b + 1) * names, to_im] = im.astype(BF)

        put_ref(TY // 2, ref_re, ref_im)
        for t in range(1, HALF + 1):
            cosine = table_y[base + t - 1]
            sine = table_y[base + HALF + t - 1]
            re_c, im_s = ref_re * cosine, ref_im * sine
            im_c, re_s = ref_im * cosine, ref_re * sine
            put_ref(TY // 2 - t, re_c - im_s, im_c + re_s)
            if t < HALF:
                put_ref(TY // 2 + t, re_c + im_s, im_c - re_s)
        for g in range(groups):
            re = images[g][0, :, cols].astype(F32)
            im = images[g][1, :, cols].astype(F32)

            def put(a, re, im):
                top = g * group_rows + a * rows
                left[top : top + rows, to_re] = re.astype(BF)
                left[top : top + rows, to_im] = im.astype(BF)

            put(TX // 2, re, im)
            for t in range(1, HALF + 1):
                cosine = table_x[t - 1 : t, :]
                sine = table_x[HALF + t - 1 : HALF + t, :]
                re_c, im_s = re * cosine, im * sine
                re_s, im_c = re * sine, im * cosine
                put(TX // 2 - t, re_c + im_s, im_c - re_s)
                if t < HALF:
                    put(TX // 2 + t, re_c - im_s, re_s + im_c)
        if place == span - 1:
            value = lax.dot_general(
                left[...], right[...], (((1,), (1,)), ((), ())), preferred_element_type=F32
            )
            for g in range(groups):
                outs[g][...] += value[g * group_rows : (g + 1) * group_rows]


def partial_logits(ids, table_x, table_y, shards, own, picked):
    parts, classes, orients, chunk = shards[0].shape
    groups = len(picked)
    rows = own.shape[1]
    names = classes * orients
    count = len(shards)
    lines = chunk // IMG
    span = 2 if lines % 4 == 0 else 1
    specs = image_specs(picked, own, chunk, lambda i, s: s[1] ^ i, lambda s: s[0] * count)
    arrays = [image for image, _ in picked]
    out_shape = (TX * rows, TY * names)
    return pl.pallas_call(
        functools.partial(logits_kernel, groups, count, span),
        out_shape=[jax.ShapeDtypeStruct(out_shape, F32)] * groups,
        grid_spec=pltpu.PrefetchScalarGridSpec(
            num_scalar_prefetch=1,
            grid=(count,),
            in_specs=[
                pl.BlockSpec(memory_space=pltpu.SMEM),
                pl.BlockSpec((TX, IMG), lambda i, s: (0, 0)),
            ]
            + [pl.BlockSpec(shards[0].shape, lambda i, s: (0, 0, 0, 0))] * count
            + specs,
            out_specs=[pl.BlockSpec(out_shape, lambda i, s: (0, 0))] * groups,
            scratch_shapes=[pltpu.VMEM(shards[0].shape, BF)]
            + [
                pltpu.VMEM((groups * TX * rows, 2 * span * IMG), BF),
                pltpu.VMEM((TY * names, 2 * span * IMG), BF),
            ]
            * 2,
        ),
        compiler_params=pltpu.CompilerParams(vmem_limit_bytes=VMEM_BYTES),
        cost_estimate=pl.CostEstimate(
            flops=4 * groups * TX * rows * TY * names * count * chunk,
            bytes_accessed=4 * count * chunk * (groups * rows + names),
            transcendentals=0,
        ),
        name="partial_logits",
    )(ids, table_y, table_x, *shards, *arrays)


def stats_kernel(swap, classes, orients, here, there, out):
    groups, group_rows, lanes = here.shape
    rows = group_rows // TX
    lane = lax.broadcasted_iota(jnp.int32, (rows, lanes), 1)
    class_of = (lane // orients) % classes
    out_lane = lax.broadcasted_iota(jnp.int32, (rows, LANES), 1)
    for g in range(groups):
        logits = here[g] + there[g ^ swap]
        pieces = [logits[a * rows : (a + 1) * rows] for a in range(TX)]
        top = functools.reduce(jnp.maximum, pieces)
        top = jnp.max(top, axis=1, keepdims=True)
        sums = sum(jnp.exp(piece - top) for piece in pieces)
        line = jnp.where(out_lane == 0, top, 0.0)
        for k in range(classes):
            part = jnp.sum(jnp.where(class_of == k, sums, 0.0), axis=1, keepdims=True)
            line = jnp.where(out_lane == k + 1, part, line)
        out[g * rows : (g + 1) * rows, :] = line


def logit_stats(here, there, swap, classes, orients):
    groups, group_rows, lanes = here.shape
    return pl.pallas_call(
        functools.partial(stats_kernel, swap, classes, orients),
        out_shape=jax.ShapeDtypeStruct((groups * group_rows // TX, LANES), F32),
        compiler_params=pltpu.CompilerParams(vmem_limit_bytes=VMEM_BYTES),
        cost_estimate=pl.CostEstimate(
            flops=4 * here.size, bytes_accessed=8 * here.size, transcendentals=here.size
        ),
        name="logit_stats",
    )(here, there)


def rows_kernel(groups, ids, table_y, table_x, *rest):
    metas, images = rest[:groups], rest[groups : 2 * groups]
    out, phase_c, phase_s = rest[2 * groups :]
    step = pl.program_id(0)
    chunk = out.shape[2]
    rows = metas[0].shape[1]
    lines = chunk // IMG
    line_base = (ids[0] * pl.num_programs(0) + step) * lines

    def offsets(g):
        shift = metas[g][0].astype(F32)[:, 1:2].astype(jnp.int32)
        move_x = shift % TX - TX // 2
        move_y = shift // TX - TY // 2
        return move_x, move_y

    @pl.when(step == 0)
    def _():
        for g in range(groups):
            move = jnp.broadcast_to(offsets(g)[0], (rows, IMG))
            cosine = jnp.ones((rows, IMG), F32)
            sine = jnp.zeros((rows, IMG), F32)
            for t in range(1, HALF + 1):
                hit = jnp.abs(move) == t
                cosine = jnp.where(hit, table_x[t - 1 : t, :], cosine)
                sine = jnp.where(hit, table_x[HALF + t - 1 : HALF + t, :], sine)
            phase_c[g * rows : (g + 1) * rows, :] = cosine
            phase_s[g * rows : (g + 1) * rows, :] = jnp.where(move < 0, -sine, sine)

    for g in range(groups):
        own = slice(g * rows, (g + 1) * rows)
        move = jnp.broadcast_to(offsets(g)[1], (rows, LANES))
        hits = [jnp.abs(move) == t for t in range(1, HALF + 1)]
        sign = jnp.where(move < 0, -1.0, 1.0)
        for line in range(lines):
            base = (line_base + line) * TY
            cos_y = jnp.ones((rows, LANES), F32)
            sin_y = jnp.zeros((rows, LANES), F32)
            for t in range(1, HALF + 1):
                cos_y = jnp.where(hits[t - 1], table_y[base + t - 1], cos_y)
                sin_y = jnp.where(hits[t - 1], table_y[base + HALF + t - 1], sin_y)
            sin_y = sin_y * sign
            for part in range(IMG // LANES):
                across = slice(part * LANES, (part + 1) * LANES)
                cols = slice(line * IMG + part * LANES, line * IMG + (part + 1) * LANES)
                cos_x, sin_x = phase_c[own, across], phase_s[own, across]
                cosine = cos_x * cos_y - sin_x * sin_y
                sine = sin_x * cos_y + cos_x * sin_y
                re = images[g][0, :, cols].astype(F32)
                im = images[g][1, :, cols].astype(F32)
                out[0, own, cols] = (re * cosine - im * sine).astype(BF)
                out[1, own, cols] = (re * sine + im * cosine).astype(BF)


def aligned_rows(ids, table_x, table_y, own, picked, width):
    parts, rows = own.shape[:2]
    chunk = chunk_of(width)
    count = width // chunk
    groups = len(picked)
    specs = image_specs(picked, own, chunk, lambda i, s: i, lambda s: s[0] * count)
    arrays = [table for _, table in picked] + [image for image, _ in picked]
    return pl.pallas_call(
        functools.partial(rows_kernel, groups),
        out_shape=jax.ShapeDtypeStruct((parts, groups * rows, width), BF),
        grid_spec=pltpu.PrefetchScalarGridSpec(
            num_scalar_prefetch=1,
            grid=(count,),
            in_specs=[
                pl.BlockSpec(memory_space=pltpu.SMEM),
                pl.BlockSpec((TX, IMG), lambda i, s: (0, 0)),
            ]
            + table_specs(picked)
            + specs,
            out_specs=pl.BlockSpec((parts, groups * rows, chunk), lambda i, s: (0, 0, i)),
            scratch_shapes=[
                pltpu.VMEM((groups * rows, IMG), F32),
                pltpu.VMEM((groups * rows, IMG), F32),
            ],
        ),
        compiler_params=pltpu.CompilerParams(vmem_limit_bytes=VMEM_BYTES),
        cost_estimate=pl.CostEstimate(
            flops=20 * groups * rows * width,
            bytes_accessed=8 * groups * rows * width,
            transcendentals=0,
        ),
        name="aligned_rows",
    )(ids, table_y, table_x, *arrays)


def volume_kernel(groups, orients, classes, ids, *rest):
    stats, metas = rest[:4], rest[4 : 4 + groups]
    near, far = rest[4 + groups], rest[5 + groups]
    prob, outs, mixes = rest[6 + groups], rest[7 + groups : -2], rest[-2:]
    step = pl.program_id(0)
    rows = metas[0].shape[1]

    @pl.when(step == 0)
    def _():
        lane = lax.broadcasted_iota(jnp.int32, (rows, LANES), 1)
        pieces = []
        for g in range(groups):
            mine, other = (stats[0], stats[2]) if g % 2 == 0 else (stats[1], stats[3])
            place = g // 2
            mine = mine[place * rows : (place + 1) * rows, :]
            other = other[place * rows : (place + 1) * rows, :]
            top = jnp.maximum(mine[:, 0:1], other[:, 0:1])
            mine_scale = jnp.exp(mine[:, 0:1] - top)
            other_scale = jnp.exp(other[:, 0:1] - top)
            held = (lane >= 1) & (lane <= classes)
            both = jnp.where(held, mine * mine_scale + other * other_scale, 0.0)
            totals = jnp.sum(both, axis=1, keepdims=True)
            spread = jnp.zeros((rows, LANES), F32)
            for k in range(classes):
                spread = jnp.where(lane % classes == k, mine[:, k + 1 : k + 2], spread)
            class_prob = spread * mine_scale / totals
            if g == 0:
                prob[...] = class_prob
            table = metas[g][0].astype(F32)
            fixed = table[:, 2:3] + table[:, 3:4] + table[:, 4:5]
            weight = (fixed * class_prob).astype(BF).astype(F32)
            bin_of = table[:, 0:1].astype(jnp.int32) ^ ids[1]
            pieces.append(jnp.where(lane // classes == bin_of, weight, 0.0))
        for mix, held in zip(mixes, (pieces[:2], pieces[2:])):
            mixing = jnp.concatenate(held, axis=0)
            mix[...] = jnp.transpose(mixing)[: orients * classes].astype(BF)

    for part in range(2):
        value = jnp.dot(mixes[0][...], near[part], preferred_element_type=F32)
        value += jnp.dot(mixes[1][...], far[part], preferred_element_type=F32)
        for o in range(orients):
            outs[o][part] = value[o * classes : (o + 1) * classes].astype(outs[o].dtype)


def volume_terms(ids, stats, groups, near, far, orients, classes):
    parts, entries, width = near.shape
    rest = far.shape[1]
    rows = groups[0][0].shape[1]
    chunk = chunk_of(width)
    count = width // chunk
    out_shape = (parts, classes, width)
    fixed = lambda i, s: (0, 0)
    return pl.pallas_call(
        functools.partial(volume_kernel, len(groups), orients, classes),
        out_shape=[jax.ShapeDtypeStruct((rows, LANES), F32)]
        + [
            jax.ShapeDtypeStruct(out_shape, F32 if o == 0 else BF)
            for o in range(orients)
        ],
        grid_spec=pltpu.PrefetchScalarGridSpec(
            num_scalar_prefetch=1,
            grid=(count,),
            in_specs=[pl.BlockSpec(stats[0].shape, fixed)] * 4
            + table_specs(groups)
            + [
                pl.BlockSpec((parts, entries, chunk), lambda i, s: (0, 0, i)),
                pl.BlockSpec((parts, rest, chunk), lambda i, s: (0, 0, i)),
            ],
            out_specs=[pl.BlockSpec((rows, LANES), fixed)]
            + [pl.BlockSpec((parts, classes, chunk), lambda i, s: (0, 0, i))] * orients,
            scratch_shapes=[
                pltpu.VMEM((orients * classes, entries), BF),
                pltpu.VMEM((orients * classes, rest), BF),
            ],
        ),
        compiler_params=pltpu.CompilerParams(vmem_limit_bytes=VMEM_BYTES),
        cost_estimate=pl.CostEstimate(
            flops=4 * orients * classes * (entries + rest) * width,
            bytes_accessed=4 * (entries + rest) * width + 4 * orients * classes * width,
            transcendentals=0,
        ),
        name="volume_terms",
    )(ids, *stats, *[table for _, table in groups], near, far)


def total_kernel(first, *rest):
    out = rest[-1]
    total = first[...]
    for term in rest[:-1]:
        total = total + term[...].astype(F32)
    for part in range(out.shape[0]):
        for k in range(out.shape[1]):
            out[part, k] = total[part, k : k + 1]


def total_volume(terms):
    parts, classes, width = terms[0].shape
    return pl.pallas_call(
        total_kernel,
        out_shape=jax.ShapeDtypeStruct((parts, classes, 1, width), F32),
        compiler_params=pltpu.CompilerParams(vmem_limit_bytes=VMEM_BYTES),
        name="total_volume",
    )(*terms)


def local(dom, orient, cls, references, images, orient_lists, shift_ids, fixed_weights):
    classes, orients = references.shape[1], references.shape[2]
    table_x, table_y = (jnp.asarray(t) for t in trig_tables())
    ids = jnp.stack([lax.axis_index(name) for name in ("dom", "orient", "cls")])
    ids = ids.astype(jnp.int32)

    def swap_dom(array, step):
        return lax.ppermute(array, "dom", xor_pairs(dom, step))

    def swap_orient(array, step):
        return lax.ppermute(array, "orient", xor_pairs(orient, step))

    bands, meta, shard = image_bands(
        ids, orient_lists, shift_ids, fixed_weights, images, references, dom
    )
    arrived = {step: swap_dom(bands[step - 1], step) for step in [1, *range(dom - 1, 1, -1)]}
    shards = [shard] + [swap_orient(shard, step) for step in range(1, orient)]
    groups = [(images, meta)] + [(arrived[step], arrived[step]) for step in range(1, dom)]

    def logits_of(picked):
        return partial_logits(ids, table_x, table_y, shards, images, picked)

    width = images.shape[2] // dom
    aligned_near = aligned_rows(ids, table_x, table_y, images, groups[:2], width)
    *shards, aligned_near = lax.optimization_barrier((*shards, aligned_near))
    partial = [None] * dom
    partial[0:2] = logits_of(groups[:2])
    partial[3::2] = logits_of(groups[3::2])
    partial[2::2] = logits_of(groups[2::2])
    kept = [partial[s] + swap_dom(partial[s ^ 1], 1) for s in range(0, dom, 2)]
    here = jnp.stack(kept)
    step = 2
    there, swap = jnp.zeros_like(here), 0
    while step < dom:
        there, swap = swap_dom(here, step), step // 2
        if step * 2 < dom:
            order = np.arange(dom // 2) ^ swap
            here = here + jnp.stack([there[i] for i in order])
        step *= 2
    aligned_far = aligned_rows(ids, table_x, table_y, images, groups[2:], width)
    there, aligned_far = lax.optimization_barrier((there, aligned_far))
    stats = logit_stats(here, there, swap, classes, orients)

    pairs = [(i, i ^ dom) for i in range(cls * dom)]
    cross = [(i, i ^ dom ^ 1) for i in range(cls * dom)]
    stats_all = [
        stats,
        swap_dom(stats, 1),
        lax.ppermute(stats, ("cls", "dom"), pairs),
        lax.ppermute(stats, ("cls", "dom"), cross),
    ]
    prob, *terms = volume_terms(
        ids, stats_all, groups, aligned_near, aligned_far, orients, classes
    )
    terms = [terms[0]] + [swap_orient(terms[o], o) for o in range(orients - 1, 0, -1)]
    return prob[:, :classes], total_volume(terms)


def solution(mesh):
    in_specs = (
        P(None, "cls", None, ("dom", "orient")),
        P(None, ("dom", "orient"), None),
        P(("dom", "orient"), None),
        P(("dom", "orient"), None),
        P(("dom", "orient"), None),
    )
    out_specs = (P(("dom", "orient"), "cls"), P(None, "cls", "orient", "dom"))
    body = functools.partial(local, mesh.shape["dom"], mesh.shape["orient"], mesh.shape["cls"])
    return jax.shard_map(body, mesh=mesh, in_specs=in_specs, out_specs=out_specs, check_vma=False)
```

```python
import functools
import math

import jax
import jax.numpy as jnp
import numpy as np
from jax import lax
from jax.experimental import pallas as pl
from jax.experimental.pallas import tpu as pltpu
from jax.sharding import PartitionSpec as P

IMG = 256
TX = 8
TY = 8
HALF = TX // 2
LANES = 128
SUBLANES = 8
VMEM_BYTES = 24 * 1024 * 1024
VMEM_SPEC = pl.BlockSpec(memory_space=pltpu.VMEM)
SMEM_SPEC = pl.BlockSpec(memory_space=pltpu.SMEM)
BF = jnp.bfloat16
F32 = jnp.float32


def trig_tables():
    steps = np.arange(1, HALF + 1)
    angle_x = 2.0 * math.pi / IMG * steps[:, None] * (np.arange(IMG) - IMG // 2)[None, :]
    angle_y = 2.0 * math.pi / IMG * np.arange(IMG // 2)[:, None] * steps[None, :]
    table_x = np.concatenate([np.cos(angle_x), np.sin(angle_x)], 0).astype(np.float32)
    table_y = np.concatenate([np.cos(angle_y), np.sin(angle_y)], 1).astype(np.float32)
    return table_x, table_y.reshape(-1)


def xor_pairs(size, step):
    return [(i, i ^ step) for i in range(size)]


def column_of(line):
    size = line.shape[1]
    rows = lax.broadcasted_iota(jnp.int32, (size, size), 0)
    cols = lax.broadcasted_iota(jnp.int32, (size, size), 1)
    return jnp.sum(jnp.where(rows == cols, line, 0.0), axis=1, keepdims=True)


def bands_kernel(steps, ids, images, references, *rest):
    lists, rest = rest[:3], rest[3:]
    outs, meta, shard = rest[: len(steps)], rest[len(steps)], rest[len(steps) + 1]
    lines, sems, meta_sems, line_sems, shard_sem = rest[len(steps) + 2 :]
    width = outs[0].shape[2] - LANES
    copies = [pltpu.make_async_copy(references, shard, shard_sem)]
    for place, (step, out) in enumerate(zip(steps, outs)):
        start = pl.multiple_of((ids[0] ^ step) * width, width)
        for part in range(out.shape[0]):
            copies.append(
                pltpu.make_async_copy(
                    images.at[part, :, pl.ds(start, width)],
                    out.at[part, :, pl.ds(0, width)],
                    sems.at[place, part],
                )
            )
    line_copies = [
        pltpu.make_async_copy(source, lines[place], line_sems.at[place])
        for place, source in enumerate(lists)
    ]
    for copy in line_copies + copies:
        copy.start()
    for copy in line_copies:
        copy.wait()
    lane = lax.broadcasted_iota(jnp.int32, meta.shape[1:], 1)
    fixed = column_of(lines[2][...])
    high = fixed.astype(BF).astype(F32)
    middle = (fixed - high).astype(BF).astype(F32)
    values = [column_of(lines[0][...].astype(F32)), column_of(lines[1][...].astype(F32))]
    table = jnp.zeros(meta.shape[1:], F32)
    for place, value in enumerate(values + [high, middle, fixed - high - middle]):
        table = jnp.where(lane == place, value, table)
    meta[0] = table.astype(BF)
    meta[1] = jnp.zeros(meta.shape[1:], BF)
    meta_copies = [
        pltpu.make_async_copy(meta, out.at[:, :, pl.ds(width, LANES)], meta_sems.at[place])
        for place, out in enumerate(outs)
    ]
    for copy in meta_copies:
        copy.start()
    for copy in copies + meta_copies:
        copy.wait()


def image_bands(ids, orient_lists, shift_ids, fixed_weights, images, references, dom):
    parts, rows, pixels = images.shape
    width = pixels // dom
    steps = list(range(1, dom))
    sources = [images, references] + [
        array.reshape(1, rows) for array in (orient_lists, shift_ids, fixed_weights)
    ]
    sources = [pltpu.with_memory_space_constraint(array, pltpu.HBM) for array in sources]
    *bands, meta, shard = pl.pallas_call(
        functools.partial(bands_kernel, steps),
        out_shape=[pltpu.VMEM((parts, rows, width + LANES), images.dtype)] * len(steps)
        + [
            jax.ShapeDtypeStruct((parts, rows, LANES), BF),
            pltpu.VMEM(references.shape, references.dtype),
        ],
        in_specs=[pl.BlockSpec(memory_space=pltpu.SMEM)]
        + [pl.BlockSpec(memory_space=pl.ANY)] * len(sources),
        out_specs=[pl.BlockSpec(memory_space=pl.ANY)] * len(steps)
        + [pl.BlockSpec(memory_space=pltpu.VMEM), pl.BlockSpec(memory_space=pl.ANY)],
        scratch_shapes=[
            [pltpu.VMEM((1, rows), array.dtype) for array in sources[2:]],
            pltpu.SemaphoreType.DMA((len(steps), parts)),
            pltpu.SemaphoreType.DMA((len(steps),)),
            pltpu.SemaphoreType.DMA((3,)),
            pltpu.SemaphoreType.DMA,
        ],
        compiler_params=pltpu.CompilerParams(vmem_limit_bytes=VMEM_BYTES),
        cost_estimate=pl.CostEstimate(
            flops=0, bytes_accessed=4 * parts * rows * (pixels - width), transcendentals=0
        ),
        name="image_bands",
    )(ids, *sources)
    return bands, meta, shard


def own_kernel(ids, images, band, sems):
    width = band.shape[2]
    start = pl.multiple_of(ids[0] * width, width)
    copies = [
        pltpu.make_async_copy(images.at[part, :, pl.ds(start, width)], band.at[part], sems.at[part])
        for part in range(band.shape[0])
    ]
    for copy in copies:
        copy.start()
    for copy in copies:
        copy.wait()


def own_band(ids, images, dom):
    parts, rows, pixels = images.shape
    shape = (parts, rows, pixels // dom)
    return pl.pallas_call(
        own_kernel,
        out_shape=pltpu.VMEM(shape, images.dtype),
        in_specs=[pl.BlockSpec(memory_space=pltpu.SMEM), pl.BlockSpec(memory_space=pl.ANY)],
        out_specs=pl.BlockSpec(memory_space=pl.ANY),
        scratch_shapes=[pltpu.SemaphoreType.DMA((parts,))],
        compiler_params=pltpu.CompilerParams(vmem_limit_bytes=VMEM_BYTES),
        name="own_band",
    )(ids, pltpu.with_memory_space_constraint(images, pltpu.HBM))


def in_vmem(arrays):
    placed = [pltpu.with_memory_space_constraint(array, pltpu.VMEM) for array in arrays]
    return placed, [VMEM_SPEC] * len(placed)


def logits_kernel(groups, orients, ids, table_y, table_x, *rest):
    shards, rest = rest[:orients], rest[orients:]
    images, rest = rest[:groups], rest[groups:]
    outs, (refs, left, right) = rest[:groups], rest[groups:]
    chunk = shards[0].shape[3]
    rows = images[0].shape[1]
    group_rows = TX * rows
    names = refs.shape[1]
    lines = chunk // IMG
    per_class = shards[0].shape[2]
    for place, shard in enumerate(shards):
        cols = slice(place * chunk, (place + 1) * chunk)
        for part in range(2):
            for k in range(shard.shape[1]):
                refs[part, k * per_class : (k + 1) * per_class, cols] = shard[part, k]
    for out in outs:
        out[...] = jnp.zeros_like(out)

    def add_shard(step, carry):
        column = ids[1] ^ step
        line_base = (ids[0] * orients + column) * lines
        for line in range(lines):
            to_re = slice(2 * line * IMG, (2 * line + 1) * IMG)
            to_im = slice((2 * line + 1) * IMG, (2 * line + 2) * IMG)
            base = (line_base + line) * TY
            ref_cols = pl.ds(pl.multiple_of(step * chunk + line * IMG, IMG), IMG)
            ref_re = refs[0, :, ref_cols].astype(F32)
            ref_im = refs[1, :, ref_cols].astype(F32)

            def put_ref(b, re, im):
                right[b * names : (b + 1) * names, to_re] = re.astype(BF)
                right[b * names : (b + 1) * names, to_im] = im.astype(BF)

            put_ref(TY // 2, ref_re, ref_im)
            for t in range(1, HALF + 1):
                cosine = table_y[base + t - 1]
                sine = table_y[base + HALF + t - 1]
                re_c, im_s = ref_re * cosine, ref_im * sine
                im_c, re_s = ref_im * cosine, ref_re * sine
                put_ref(TY // 2 - t, re_c - im_s, im_c + re_s)
                if t < HALF:
                    put_ref(TY // 2 + t, re_c + im_s, im_c - re_s)
            for g in range(groups):
                cols = pl.ds(pl.multiple_of(column * chunk + line * IMG, IMG), IMG)
                re = images[g][0, :, cols].astype(F32)
                im = images[g][1, :, cols].astype(F32)

                def put(a, re, im):
                    top = g * group_rows + a * rows
                    left[top : top + rows, to_re] = re.astype(BF)
                    left[top : top + rows, to_im] = im.astype(BF)

                put(TX // 2, re, im)
                for t in range(1, HALF + 1):
                    cosine = table_x[t - 1 : t, :]
                    sine = table_x[HALF + t - 1 : HALF + t, :]
                    re_c, im_s = re * cosine, im * sine
                    re_s, im_c = re * sine, im * cosine
                    put(TX // 2 - t, re_c + im_s, im_c - re_s)
                    if t < HALF:
                        put(TX // 2 + t, re_c - im_s, re_s + im_c)
        value = lax.dot_general(
            left[...], right[...], (((1,), (1,)), ((), ())), preferred_element_type=F32
        )
        for g in range(groups):
            outs[g][...] += value[g * group_rows : (g + 1) * group_rows]
        return carry

    lax.fori_loop(0, orients, add_shard, 0)


def partial_logits(ids, table_x, table_y, shards, picked):
    parts, classes, orients, chunk = shards[0].shape
    groups = len(picked)
    rows = picked[0][0].shape[1]
    names = classes * orients
    count = len(shards)
    out_shape = (TX * rows, TY * names)
    arrays, specs = in_vmem([table_x, *shards, *(image for image, _ in picked)])
    return pl.pallas_call(
        functools.partial(logits_kernel, groups, count),
        out_shape=[pltpu.VMEM(out_shape, F32)] * groups,
        in_specs=[SMEM_SPEC] * 2 + specs,
        out_specs=[VMEM_SPEC] * groups,
        scratch_shapes=[
            pltpu.VMEM((parts, names, count * chunk), BF),
            pltpu.VMEM((groups * TX * rows, 2 * chunk), BF),
            pltpu.VMEM((TY * names, 2 * chunk), BF),
        ],
        compiler_params=pltpu.CompilerParams(vmem_limit_bytes=VMEM_BYTES),
        cost_estimate=pl.CostEstimate(
            flops=4 * groups * TX * rows * TY * names * count * chunk,
            bytes_accessed=4 * count * chunk * (groups * rows + names),
            transcendentals=0,
        ),
        name="partial_logits",
    )(ids, table_y, *arrays)


def stats_kernel(swap, classes, orients, here, there, out):
    groups, group_rows, lanes = here.shape
    rows = group_rows // TX
    lane = lax.broadcasted_iota(jnp.int32, (rows, lanes), 1)
    class_of = (lane // orients) % classes
    out_lane = lax.broadcasted_iota(jnp.int32, (rows, LANES), 1)
    for g in range(groups):
        logits = here[g] + there[g ^ swap]
        pieces = [logits[a * rows : (a + 1) * rows] for a in range(TX)]
        top = functools.reduce(jnp.maximum, pieces)
        top = jnp.max(top, axis=1, keepdims=True)
        sums = sum(jnp.exp(piece - top) for piece in pieces)
        line = jnp.where(out_lane == 0, top, 0.0)
        for k in range(classes):
            part = jnp.sum(jnp.where(class_of == k, sums, 0.0), axis=1, keepdims=True)
            line = jnp.where(out_lane == k + 1, part, line)
        out[g * rows : (g + 1) * rows, :] = line


def logit_stats(here, there, swap, classes, orients):
    groups, group_rows, lanes = here.shape
    arrays, specs = in_vmem([here, there])
    return pl.pallas_call(
        functools.partial(stats_kernel, swap, classes, orients),
        out_shape=pltpu.VMEM((groups * group_rows // TX, LANES), F32),
        in_specs=specs,
        out_specs=VMEM_SPEC,
        compiler_params=pltpu.CompilerParams(vmem_limit_bytes=VMEM_BYTES),
        cost_estimate=pl.CostEstimate(
            flops=4 * here.size, bytes_accessed=8 * here.size, transcendentals=here.size
        ),
        name="logit_stats",
    )(*arrays)


def rows_kernel(groups, ids, table_y, table_x, *rest):
    metas, images = rest[:groups], rest[groups : 2 * groups]
    out = rest[2 * groups]
    rows = metas[0].shape[1]
    width = out.shape[2]
    lines = width // IMG
    line_base = ids[0] * lines
    for g in range(groups):
        own = slice(g * rows, (g + 1) * rows)
        last = metas[g].shape[2] - LANES
        shift = metas[g][0, :, last:].astype(F32)[:, 1:2].astype(jnp.int32)
        move_x = jnp.broadcast_to(shift % TX - TX // 2, (rows, IMG))
        move_y = jnp.broadcast_to(shift // TX - TY // 2, (rows, LANES))
        phase_c = jnp.ones((rows, IMG), F32)
        phase_s = jnp.zeros((rows, IMG), F32)
        for t in range(1, HALF + 1):
            hit = jnp.abs(move_x) == t
            phase_c = jnp.where(hit, table_x[t - 1 : t, :], phase_c)
            phase_s = jnp.where(hit, table_x[HALF + t - 1 : HALF + t, :], phase_s)
        phase_s = jnp.where(move_x < 0, -phase_s, phase_s)
        hits = [jnp.abs(move_y) == t for t in range(1, HALF + 1)]
        sign = jnp.where(move_y < 0, -1.0, 1.0)

        def add_line(line, carry):
            base = (line_base + line) * TY
            cos_y = jnp.ones((rows, LANES), F32)
            sin_y = jnp.zeros((rows, LANES), F32)
            for t in range(1, HALF + 1):
                cos_y = jnp.where(hits[t - 1], table_y[base + t - 1], cos_y)
                sin_y = jnp.where(hits[t - 1], table_y[base + HALF + t - 1], sin_y)
            sin_y = sin_y * sign
            for part in range(IMG // LANES):
                across = slice(part * LANES, (part + 1) * LANES)
                start = pl.multiple_of(line * IMG + part * LANES, LANES)
                cols = pl.ds(start, LANES)
                cos_x, sin_x = phase_c[:, across], phase_s[:, across]
                cosine = cos_x * cos_y - sin_x * sin_y
                sine = sin_x * cos_y + cos_x * sin_y
                re = images[g][0, :, cols].astype(F32)
                im = images[g][1, :, cols].astype(F32)
                out[0, own, cols] = (re * cosine - im * sine).astype(BF)
                out[1, own, cols] = (re * sine + im * cosine).astype(BF)
            return carry

        lax.fori_loop(0, lines, add_line, 0, unroll=min(lines, 4))


def aligned_rows(ids, table_x, table_y, picked, width):
    parts, rows = picked[0][0].shape[:2]
    groups = len(picked)
    arrays, specs = in_vmem(
        [table_x] + [table for _, table in picked] + [image for image, _ in picked]
    )
    return pl.pallas_call(
        functools.partial(rows_kernel, groups),
        out_shape=pltpu.VMEM((parts, groups * rows, width), BF),
        in_specs=[SMEM_SPEC] * 2 + specs,
        out_specs=VMEM_SPEC,
        compiler_params=pltpu.CompilerParams(vmem_limit_bytes=VMEM_BYTES),
        cost_estimate=pl.CostEstimate(
            flops=20 * groups * rows * width,
            bytes_accessed=8 * groups * rows * width,
            transcendentals=0,
        ),
        name="aligned_rows",
    )(ids, table_y, *arrays)


def volume_kernel(groups, orients, classes, ids, *rest):
    stats, metas = rest[:4], rest[4 : 4 + groups]
    near, far = rest[4 + groups], rest[5 + groups]
    prob, outs = rest[6 + groups], rest[7 + groups :]
    rows = metas[0].shape[1]
    width = near.shape[2]
    chunk = min(width, 8 * IMG)
    lane = lax.broadcasted_iota(jnp.int32, (rows, LANES), 1)
    pieces = []
    for g in range(groups):
        mine, other = (stats[0], stats[2]) if g % 2 == 0 else (stats[1], stats[3])
        place = g // 2
        mine = mine[place * rows : (place + 1) * rows, :]
        other = other[place * rows : (place + 1) * rows, :]
        top = jnp.maximum(mine[:, 0:1], other[:, 0:1])
        mine_scale = jnp.exp(mine[:, 0:1] - top)
        other_scale = jnp.exp(other[:, 0:1] - top)
        held = (lane >= 1) & (lane <= classes)
        both = jnp.where(held, mine * mine_scale + other * other_scale, 0.0)
        totals = jnp.sum(both, axis=1, keepdims=True)
        spread = jnp.zeros((rows, LANES), F32)
        for k in range(classes):
            spread = jnp.where(lane % SUBLANES == k, mine[:, k + 1 : k + 2], spread)
        class_prob = spread * mine_scale / totals
        if g == 0:
            prob[...] = class_prob
        last = metas[g].shape[2] - LANES
        table = metas[g][0, :, last:].astype(F32)
        fixed = table[:, 2:3] + table[:, 3:4] + table[:, 4:5]
        weight = (fixed * class_prob).astype(BF).astype(F32)
        bin_of = table[:, 0:1].astype(jnp.int32) ^ ids[1]
        pieces.append(jnp.where(lane // SUBLANES == bin_of, weight, 0.0))
    mixes = []
    for held in (pieces[:2], pieces[2:]):
        mixing = jnp.transpose(jnp.concatenate(held, axis=0))
        mixes.append(mixing[: orients * SUBLANES].astype(BF))
    for part in range(2):
        for column in range(0, width, chunk):
            cols = slice(column, column + chunk)
            value = jnp.dot(mixes[0], near[part, :, cols], preferred_element_type=F32)
            value += jnp.dot(mixes[1], far[part, :, cols], preferred_element_type=F32)
            for o in range(orients):
                term = value[o * SUBLANES : o * SUBLANES + classes]
                outs[o][part, :, cols] = term.astype(outs[o].dtype)


def volume_terms(ids, stats, groups, near, far, orients, classes):
    parts, entries, width = near.shape
    rest = far.shape[1]
    rows = groups[0][0].shape[1]
    out_shape = (parts, classes, width)
    arrays, specs = in_vmem([*stats, *(table for _, table in groups), near, far])
    return pl.pallas_call(
        functools.partial(volume_kernel, len(groups), orients, classes),
        out_shape=[jax.ShapeDtypeStruct((rows, LANES), F32)]
        + [pltpu.VMEM(out_shape, F32 if o == 0 else BF) for o in range(orients)],
        in_specs=[SMEM_SPEC] + specs,
        out_specs=[VMEM_SPEC] * (1 + orients),
        compiler_params=pltpu.CompilerParams(vmem_limit_bytes=VMEM_BYTES),
        cost_estimate=pl.CostEstimate(
            flops=4 * orients * classes * (entries + rest) * width,
            bytes_accessed=4 * (entries + rest) * width + 4 * orients * classes * width,
            transcendentals=0,
        ),
        name="volume_terms",
    )(ids, *arrays)


def total_kernel(first, *rest):
    out = rest[-1]
    total = first[...]
    for term in rest[:-1]:
        total = total + term[...].astype(F32)
    for part in range(out.shape[0]):
        for k in range(out.shape[1]):
            out[part, k] = total[part, k : k + 1]


def total_volume(terms):
    parts, classes, width = terms[0].shape
    arrays, specs = in_vmem(terms)
    return pl.pallas_call(
        total_kernel,
        out_shape=jax.ShapeDtypeStruct((parts, classes, 1, width), F32),
        in_specs=specs,
        compiler_params=pltpu.CompilerParams(vmem_limit_bytes=VMEM_BYTES),
        name="total_volume",
    )(*arrays)


def local(dom, orient, cls, references, images, orient_lists, shift_ids, fixed_weights):
    classes, orients = references.shape[1], references.shape[2]
    table_x, table_y = (jnp.asarray(t) for t in trig_tables())
    ids = jnp.stack([lax.axis_index(name) for name in ("dom", "orient", "cls")])
    ids = ids.astype(jnp.int32)

    def swap_dom(array, step):
        return lax.ppermute(array, "dom", xor_pairs(dom, step))

    def swap_orient(array, step):
        return lax.ppermute(array, "orient", xor_pairs(orient, step))

    bands, meta, shard = image_bands(
        ids, orient_lists, shift_ids, fixed_weights, images, references, dom
    )
    arrived = {step: swap_dom(bands[step - 1], step) for step in [1, *range(dom - 1, 1, -1)]}
    shards = [shard] + [swap_orient(shard, step) for step in range(1, orient)]
    groups = [(own_band(ids, images, dom), meta)] + [(arrived[step], arrived[step]) for step in range(1, dom)]

    def logits_of(picked):
        return partial_logits(ids, table_x, table_y, shards, picked)

    width = images.shape[2] // dom
    aligned_near = aligned_rows(ids, table_x, table_y, groups[:2], width)
    *shards, aligned_near = lax.optimization_barrier((*shards, aligned_near))
    partial = [None] * dom
    partial[0:2] = logits_of(groups[:2])
    partial[3::2] = logits_of(groups[3::2])
    partial[2::2] = logits_of(groups[2::2])
    kept = [partial[s] + swap_dom(partial[s ^ 1], 1) for s in range(0, dom, 2)]
    here = jnp.stack(kept)
    step = 2
    there, swap = jnp.zeros_like(here), 0
    while step < dom:
        there, swap = swap_dom(here, step), step // 2
        if step * 2 < dom:
            order = np.arange(dom // 2) ^ swap
            here = here + jnp.stack([there[i] for i in order])
        step *= 2
    aligned_far = aligned_rows(ids, table_x, table_y, groups[2:], width)
    there, aligned_far = lax.optimization_barrier((there, aligned_far))
    stats = logit_stats(here, there, swap, classes, orients)

    pairs = [(i, i ^ dom) for i in range(cls * dom)]
    cross = [(i, i ^ dom ^ 1) for i in range(cls * dom)]
    stats_all = [
        stats,
        swap_dom(stats, 1),
        lax.ppermute(stats, ("cls", "dom"), pairs),
        lax.ppermute(stats, ("cls", "dom"), cross),
    ]
    prob, *terms = volume_terms(
        ids, stats_all, groups, aligned_near, aligned_far, orients, classes
    )
    terms = [terms[0]] + [swap_orient(terms[o], o) for o in range(orients - 1, 0, -1)]
    return prob[:, :classes], total_volume(terms)


def solution(mesh):
    in_specs = (
        P(None, "cls", None, ("dom", "orient")),
        P(None, ("dom", "orient"), None),
        P(("dom", "orient"), None),
        P(("dom", "orient"), None),
        P(("dom", "orient"), None),
    )
    out_specs = (P(("dom", "orient"), "cls"), P(None, "cls", "orient", "dom"))
    body = functools.partial(local, mesh.shape["dom"], mesh.shape["orient"], mesh.shape["cls"])
    return jax.shard_map(body, mesh=mesh, in_specs=in_specs, out_specs=out_specs, check_vma=False)
```

```python
import functools
import math

import jax
import jax.numpy as jnp
import numpy as np
from jax import lax
from jax.experimental import pallas as pl
from jax.experimental.pallas import tpu as pltpu
from jax.sharding import PartitionSpec as P

IMG = 256
TX = 8
TY = 8
HALF = TX // 2
LANES = 128
SUBLANES = 8
SHARED = 2
EARLY = 2
FLOPS_OF_MICRO = 1_000_000_000
VMEM_BYTES = 24 * 1024 * 1024
VMEM_SPEC = pl.BlockSpec(memory_space=pltpu.VMEM)
SMEM_SPEC = pl.BlockSpec(memory_space=pltpu.SMEM)
BF = jnp.bfloat16
F32 = jnp.float32


def trig_tables():
    steps = np.arange(1, HALF + 1)
    angle_x = 2.0 * math.pi / IMG * steps[:, None] * (np.arange(IMG) - IMG // 2)[None, :]
    angle_y = 2.0 * math.pi / IMG * np.arange(IMG // 2)[:, None] * steps[None, :]
    table_x = np.concatenate([np.cos(angle_x), np.sin(angle_x)], 0).astype(np.float32)
    table_y = np.concatenate([np.cos(angle_y), np.sin(angle_y)], 1).astype(np.float32)
    return table_x, table_y.reshape(-1)


def xor_pairs(size, step):
    return [(i, i ^ step) for i in range(size)]


def column_of(line):
    size = line.shape[1]
    rows = lax.broadcasted_iota(jnp.int32, (size, size), 0)
    cols = lax.broadcasted_iota(jnp.int32, (size, size), 1)
    return jnp.sum(jnp.where(rows == cols, line, 0.0), axis=1, keepdims=True)


def bands_kernel(steps, ids, images, references, *rest):
    lists, rest = rest[:3], rest[3:]
    outs, meta, shard = rest[: len(steps)], rest[len(steps)], rest[len(steps) + 1]
    lines, sems, meta_sems, line_sems, shard_sem = rest[len(steps) + 2 :]
    copies = [pltpu.make_async_copy(references, shard, shard_sem)]
    for place, (step, out) in enumerate(zip(steps, outs)):
        width = out.shape[2] - LANES
        start = (ids[0] ^ step) * width
        if step == SHARED:
            start = 2 * start + ids[2] * width
        start = pl.multiple_of(start, width)
        for part in range(out.shape[0]):
            copies.append(
                pltpu.make_async_copy(
                    images.at[part, :, pl.ds(start, width)],
                    out.at[part, :, pl.ds(0, width)],
                    sems.at[place, part],
                )
            )
    line_copies = [
        pltpu.make_async_copy(source, lines[place], line_sems.at[place])
        for place, source in enumerate(lists)
    ]
    for copy in line_copies + copies:
        copy.start()
    for copy in line_copies:
        copy.wait()
    lane = lax.broadcasted_iota(jnp.int32, meta.shape[1:], 1)
    fixed = column_of(lines[2][...])
    high = fixed.astype(BF).astype(F32)
    middle = (fixed - high).astype(BF).astype(F32)
    values = [column_of(lines[0][...].astype(F32)), column_of(lines[1][...].astype(F32))]
    table = jnp.zeros(meta.shape[1:], F32)
    for place, value in enumerate(values + [high, middle, fixed - high - middle]):
        table = jnp.where(lane == place, value, table)
    meta[0] = table.astype(BF)
    meta[1] = jnp.zeros(meta.shape[1:], BF)
    meta_copies = [
        pltpu.make_async_copy(
            meta, out.at[:, :, pl.ds(out.shape[2] - LANES, LANES)], meta_sems.at[place]
        )
        for place, out in enumerate(outs)
    ]
    for copy in meta_copies:
        copy.start()
    for copy in copies + meta_copies:
        copy.wait()


def image_bands(ids, orient_lists, shift_ids, fixed_weights, images, references, dom):
    parts, rows, pixels = images.shape
    width = pixels // dom
    steps = list(range(1, dom))
    sources = [images, references] + [
        array.reshape(1, rows) for array in (orient_lists, shift_ids, fixed_weights)
    ]
    sources = [pltpu.with_memory_space_constraint(array, pltpu.HBM) for array in sources]
    *bands, meta, shard = pl.pallas_call(
        functools.partial(bands_kernel, steps),
        out_shape=[
            pltpu.VMEM((parts, rows, width // (1 + (step == SHARED)) + LANES), images.dtype)
            for step in steps
        ]
        + [
            jax.ShapeDtypeStruct((parts, rows, LANES), BF),
            pltpu.VMEM(references.shape, references.dtype),
        ],
        in_specs=[pl.BlockSpec(memory_space=pltpu.SMEM)]
        + [pl.BlockSpec(memory_space=pl.ANY)] * len(sources),
        out_specs=[pl.BlockSpec(memory_space=pl.ANY)] * len(steps)
        + [pl.BlockSpec(memory_space=pltpu.VMEM), pl.BlockSpec(memory_space=pl.ANY)],
        scratch_shapes=[
            [pltpu.VMEM((1, rows), array.dtype) for array in sources[2:]],
            pltpu.SemaphoreType.DMA((len(steps), parts)),
            pltpu.SemaphoreType.DMA((len(steps),)),
            pltpu.SemaphoreType.DMA((3,)),
            pltpu.SemaphoreType.DMA,
        ],
        compiler_params=pltpu.CompilerParams(vmem_limit_bytes=VMEM_BYTES),
        cost_estimate=pl.CostEstimate(
            flops=0, bytes_accessed=4 * parts * rows * (pixels - width), transcendentals=0
        ),
        name="image_bands",
    )(ids, *sources)
    return bands, meta, shard


def own_kernel(ids, images, band, sems):
    width = band.shape[2]
    start = pl.multiple_of(ids[0] * width, width)
    copies = [
        pltpu.make_async_copy(images.at[part, :, pl.ds(start, width)], band.at[part], sems.at[part])
        for part in range(band.shape[0])
    ]
    for copy in copies:
        copy.start()
    for copy in copies:
        copy.wait()


def own_band(ids, images, dom):
    parts, rows, pixels = images.shape
    shape = (parts, rows, pixels // dom)
    return pl.pallas_call(
        own_kernel,
        out_shape=pltpu.VMEM(shape, images.dtype),
        in_specs=[pl.BlockSpec(memory_space=pltpu.SMEM), pl.BlockSpec(memory_space=pl.ANY)],
        out_specs=pl.BlockSpec(memory_space=pl.ANY),
        scratch_shapes=[pltpu.SemaphoreType.DMA((parts,))],
        compiler_params=pltpu.CompilerParams(vmem_limit_bytes=VMEM_BYTES),
        name="own_band",
    )(ids, pltpu.with_memory_space_constraint(images, pltpu.HBM))


def in_vmem(arrays):
    placed = [pltpu.with_memory_space_constraint(array, pltpu.VMEM) for array in arrays]
    return placed, [VMEM_SPEC] * len(placed)


def flat(groups):
    return [image for images, _ in groups for image in images]


def sizes_of(groups):
    return [len(images) for images, _ in groups]


def by_group(sizes, refs):
    images, at = [], 0
    for size in sizes:
        images.append(refs[at : at + size])
        at += size
    return images, refs[at:]


def load(images, ids, part, start, size):
    if len(images) == 1:
        return images[0][part, :, pl.ds(pl.multiple_of(start, size), size)].astype(F32)
    half = images[0].shape[2] - LANES
    side = start // half
    cols = pl.ds(pl.multiple_of(start - side * half, size), size)
    mine, other = (image[part, :, cols].astype(F32) for image in images)
    return jnp.where(side == ids[2], mine, other)


def logits_kernel(sizes, orients, steps, sums, ids, table_y, table_x, *rest):
    groups, count = len(sizes), len(steps)
    shards, rest = rest[:count], rest[count:]
    images, rest = by_group(sizes, rest)
    before, rest = rest[: groups * sums], rest[groups * sums :]
    outs, (refs, left, right) = rest[:groups], rest[groups:]
    chunk = shards[0].shape[3]
    rows = images[0][0].shape[1]
    group_rows = TX * rows
    names = refs.shape[1]
    lines = chunk // IMG
    per_class = shards[0].shape[2]
    for place, shard in enumerate(shards):
        cols = slice(place * chunk, (place + 1) * chunk)
        for part in range(2):
            for k in range(shard.shape[1]):
                refs[part, k * per_class : (k + 1) * per_class, cols] = shard[part, k]
    for g, out in enumerate(outs):
        out[...] = before[g][...] if sums else jnp.zeros_like(out)

    def add_shard(step, carry):
        column = ids[1] ^ (step + steps[0])
        line_base = (ids[0] * orients + column) * lines
        for line in range(lines):
            to_re = slice(2 * line * IMG, (2 * line + 1) * IMG)
            to_im = slice((2 * line + 1) * IMG, (2 * line + 2) * IMG)
            base = (line_base + line) * TY
            ref_cols = pl.ds(pl.multiple_of(step * chunk + line * IMG, IMG), IMG)
            ref_re = refs[0, :, ref_cols].astype(F32)
            ref_im = refs[1, :, ref_cols].astype(F32)

            def put_ref(b, re, im):
                right[b * names : (b + 1) * names, to_re] = re.astype(BF)
                right[b * names : (b + 1) * names, to_im] = im.astype(BF)

            put_ref(TY // 2, ref_re, ref_im)
            for t in range(1, HALF + 1):
                cosine = table_y[base + t - 1]
                sine = table_y[base + HALF + t - 1]
                re_c, im_s = ref_re * cosine, ref_im * sine
                im_c, re_s = ref_im * cosine, ref_re * sine
                put_ref(TY // 2 - t, re_c - im_s, im_c + re_s)
                if t < HALF:
                    put_ref(TY // 2 + t, re_c + im_s, im_c - re_s)
            for g in range(groups):
                start = column * chunk + line * IMG
                re = load(images[g], ids, 0, start, IMG)
                im = load(images[g], ids, 1, start, IMG)

                def put(a, re, im):
                    top = g * group_rows + a * rows
                    left[top : top + rows, to_re] = re.astype(BF)
                    left[top : top + rows, to_im] = im.astype(BF)

                put(TX // 2, re, im)
                for t in range(1, HALF + 1):
                    cosine = table_x[t - 1 : t, :]
                    sine = table_x[HALF + t - 1 : HALF + t, :]
                    re_c, im_s = re * cosine, im * sine
                    re_s, im_c = re * sine, im * cosine
                    put(TX // 2 - t, re_c + im_s, im_c - re_s)
                    if t < HALF:
                        put(TX // 2 + t, re_c - im_s, re_s + im_c)
        value = lax.dot_general(
            left[...], right[...], (((1,), (1,)), ((), ())), preferred_element_type=F32
        )
        for g in range(groups):
            outs[g][...] += value[g * group_rows : (g + 1) * group_rows]
        return carry

    lax.fori_loop(0, count, add_shard, 0)


def partial_logits(ids, table_x, table_y, shards, picked, steps, before, micros):
    parts, classes, orients, chunk = shards[0].shape
    groups = len(picked)
    rows = picked[0][0][0].shape[1]
    names = classes * orients
    count = len(steps)
    out_shape = (TX * rows, TY * names)
    used = [shards[step] for step in steps]
    arrays, specs = in_vmem([table_x, *used, *flat(picked), *before])
    return pl.pallas_call(
        functools.partial(
            logits_kernel, sizes_of(picked), len(shards), steps, len(before) > 0
        ),
        out_shape=[pltpu.VMEM(out_shape, F32)] * groups,
        in_specs=[SMEM_SPEC] * 2 + specs,
        out_specs=[VMEM_SPEC] * groups,
        scratch_shapes=[
            pltpu.VMEM((parts, names, count * chunk), BF),
            pltpu.VMEM((groups * TX * rows, 2 * chunk), BF),
            pltpu.VMEM((TY * names, 2 * chunk), BF),
        ],
        compiler_params=pltpu.CompilerParams(vmem_limit_bytes=VMEM_BYTES),
        cost_estimate=pl.CostEstimate(
            flops=micros * FLOPS_OF_MICRO,
            bytes_accessed=0,
            transcendentals=0,
        ),
        name="partial_logits",
    )(ids, table_y, *arrays)


def stats_kernel(swap, classes, orients, here, there, out):
    groups, group_rows, lanes = here.shape
    rows = group_rows // TX
    lane = lax.broadcasted_iota(jnp.int32, (rows, lanes), 1)
    class_of = (lane // orients) % classes
    out_lane = lax.broadcasted_iota(jnp.int32, (rows, LANES), 1)
    for g in range(groups):
        logits = here[g] + there[g ^ swap]
        pieces = [logits[a * rows : (a + 1) * rows] for a in range(TX)]
        top = functools.reduce(jnp.maximum, pieces)
        top = jnp.max(top, axis=1, keepdims=True)
        sums = sum(jnp.exp(piece - top) for piece in pieces)
        line = jnp.where(out_lane == 0, top, 0.0)
        for k in range(classes):
            part = jnp.sum(jnp.where(class_of == k, sums, 0.0), axis=1, keepdims=True)
            line = jnp.where(out_lane == k + 1, part, line)
        out[g * rows : (g + 1) * rows, :] = line


def logit_stats(here, there, swap, classes, orients):
    groups, group_rows, lanes = here.shape
    arrays, specs = in_vmem([here, there])
    return pl.pallas_call(
        functools.partial(stats_kernel, swap, classes, orients),
        out_shape=pltpu.VMEM((groups * group_rows // TX, LANES), F32),
        in_specs=specs,
        out_specs=VMEM_SPEC,
        compiler_params=pltpu.CompilerParams(vmem_limit_bytes=VMEM_BYTES),
        cost_estimate=pl.CostEstimate(
            flops=4 * here.size, bytes_accessed=8 * here.size, transcendentals=here.size
        ),
        name="logit_stats",
    )(*arrays)


def rows_kernel(sizes, ids, table_y, table_x, *rest):
    groups = len(sizes)
    metas = rest[:groups]
    images, (out,) = by_group(sizes, rest[groups:])
    rows = metas[0].shape[1]
    width = out.shape[2]
    lines = width // IMG
    line_base = ids[0] * lines
    for g in range(groups):
        own = slice(g * rows, (g + 1) * rows)
        last = metas[g].shape[2] - LANES
        shift = metas[g][0, :, last:].astype(F32)[:, 1:2].astype(jnp.int32)
        move_x = jnp.broadcast_to(shift % TX - TX // 2, (rows, IMG))
        move_y = jnp.broadcast_to(shift // TX - TY // 2, (rows, LANES))
        phase_c = jnp.ones((rows, IMG), F32)
        phase_s = jnp.zeros((rows, IMG), F32)
        for t in range(1, HALF + 1):
            hit = jnp.abs(move_x) == t
            phase_c = jnp.where(hit, table_x[t - 1 : t, :], phase_c)
            phase_s = jnp.where(hit, table_x[HALF + t - 1 : HALF + t, :], phase_s)
        phase_s = jnp.where(move_x < 0, -phase_s, phase_s)
        hits = [jnp.abs(move_y) == t for t in range(1, HALF + 1)]
        sign = jnp.where(move_y < 0, -1.0, 1.0)

        def add_line(line, carry):
            base = (line_base + line) * TY
            cos_y = jnp.ones((rows, LANES), F32)
            sin_y = jnp.zeros((rows, LANES), F32)
            for t in range(1, HALF + 1):
                cos_y = jnp.where(hits[t - 1], table_y[base + t - 1], cos_y)
                sin_y = jnp.where(hits[t - 1], table_y[base + HALF + t - 1], sin_y)
            sin_y = sin_y * sign
            for part in range(IMG // LANES):
                across = slice(part * LANES, (part + 1) * LANES)
                start = pl.multiple_of(line * IMG + part * LANES, LANES)
                cols = pl.ds(start, LANES)
                cos_x, sin_x = phase_c[:, across], phase_s[:, across]
                cosine = cos_x * cos_y - sin_x * sin_y
                sine = sin_x * cos_y + cos_x * sin_y
                re = load(images[g], ids, 0, start, LANES)
                im = load(images[g], ids, 1, start, LANES)
                out[0, own, cols] = (re * cosine - im * sine).astype(BF)
                out[1, own, cols] = (re * sine + im * cosine).astype(BF)
            return carry

        lax.fori_loop(0, lines, add_line, 0, unroll=min(lines, 4))


def aligned_rows(ids, table_x, table_y, picked, width):
    parts, rows = picked[0][0][0].shape[:2]
    groups = len(picked)
    arrays, specs = in_vmem([table_x] + [table for _, table in picked] + flat(picked))
    return pl.pallas_call(
        functools.partial(rows_kernel, sizes_of(picked)),
        out_shape=pltpu.VMEM((parts, groups * rows, width), BF),
        in_specs=[SMEM_SPEC] * 2 + specs,
        out_specs=VMEM_SPEC,
        compiler_params=pltpu.CompilerParams(vmem_limit_bytes=VMEM_BYTES),
        cost_estimate=pl.CostEstimate(
            flops=0,
            bytes_accessed=0,
            transcendentals=0,
        ),
        name="aligned_rows",
    )(ids, table_y, *arrays)


def volume_kernel(groups, orients, classes, ids, *rest):
    stats, metas = rest[:4], rest[4 : 4 + groups]
    near, far = rest[4 + groups], rest[5 + groups]
    prob, outs = rest[6 + groups], rest[7 + groups :]
    rows = metas[0].shape[1]
    width = near.shape[2]
    chunk = min(width, 8 * IMG)
    lane = lax.broadcasted_iota(jnp.int32, (rows, LANES), 1)
    pieces = []
    for g in range(groups):
        mine, other = (stats[0], stats[2]) if g % 2 == 0 else (stats[1], stats[3])
        place = g // 2
        mine = mine[place * rows : (place + 1) * rows, :]
        other = other[place * rows : (place + 1) * rows, :]
        top = jnp.maximum(mine[:, 0:1], other[:, 0:1])
        mine_scale = jnp.exp(mine[:, 0:1] - top)
        other_scale = jnp.exp(other[:, 0:1] - top)
        held = (lane >= 1) & (lane <= classes)
        both = jnp.where(held, mine * mine_scale + other * other_scale, 0.0)
        totals = jnp.sum(both, axis=1, keepdims=True)
        spread = jnp.zeros((rows, LANES), F32)
        for k in range(classes):
            spread = jnp.where(lane % SUBLANES == k, mine[:, k + 1 : k + 2], spread)
        class_prob = spread * mine_scale / totals
        if g == 0:
            prob[...] = class_prob
        last = metas[g].shape[2] - LANES
        table = metas[g][0, :, last:].astype(F32)
        fixed = table[:, 2:3] + table[:, 3:4] + table[:, 4:5]
        weight = (fixed * class_prob).astype(BF).astype(F32)
        bin_of = table[:, 0:1].astype(jnp.int32) ^ ids[1]
        pieces.append(jnp.where(lane // SUBLANES == bin_of, weight, 0.0))
    mixes = []
    for held in (pieces[:2], pieces[2:]):
        mixing = jnp.transpose(jnp.concatenate(held, axis=0))
        mixes.append(mixing[: orients * SUBLANES].astype(BF))
    for part in range(2):
        for column in range(0, width, chunk):
            cols = slice(column, column + chunk)
            value = jnp.dot(mixes[0], near[part, :, cols], preferred_element_type=F32)
            value += jnp.dot(mixes[1], far[part, :, cols], preferred_element_type=F32)
            for o in range(orients):
                term = value[o * SUBLANES : o * SUBLANES + classes]
                outs[o][part, :, cols] = term.astype(outs[o].dtype)


def volume_terms(ids, stats, groups, near, far, orients, classes):
    parts, entries, width = near.shape
    rest = far.shape[1]
    rows = groups[0][1].shape[1]
    out_shape = (parts, classes, width)
    arrays, specs = in_vmem([*stats, *(table for _, table in groups), near, far])
    return pl.pallas_call(
        functools.partial(volume_kernel, len(groups), orients, classes),
        out_shape=[jax.ShapeDtypeStruct((rows, LANES), F32)]
        + [pltpu.VMEM(out_shape, F32 if o == 0 else BF) for o in range(orients)],
        in_specs=[SMEM_SPEC] + specs,
        out_specs=[VMEM_SPEC] * (1 + orients),
        compiler_params=pltpu.CompilerParams(vmem_limit_bytes=VMEM_BYTES),
        cost_estimate=pl.CostEstimate(
            flops=4 * orients * classes * (entries + rest) * width,
            bytes_accessed=4 * (entries + rest) * width + 4 * orients * classes * width,
            transcendentals=0,
        ),
        name="volume_terms",
    )(ids, *arrays)


def total_kernel(first, *rest):
    out = rest[-1]
    total = first[...]
    for term in rest[:-1]:
        total = total + term[...].astype(F32)
    for part in range(out.shape[0]):
        for k in range(out.shape[1]):
            out[part, k] = total[part, k : k + 1]


def total_volume(terms):
    parts, classes, width = terms[0].shape
    arrays, specs = in_vmem(terms)
    return pl.pallas_call(
        total_kernel,
        out_shape=jax.ShapeDtypeStruct((parts, classes, 1, width), F32),
        in_specs=specs,
        compiler_params=pltpu.CompilerParams(vmem_limit_bytes=VMEM_BYTES),
        name="total_volume",
    )(*arrays)


def local(dom, orient, cls, references, images, orient_lists, shift_ids, fixed_weights):
    classes, orients = references.shape[1], references.shape[2]
    table_x, table_y = (jnp.asarray(t) for t in trig_tables())
    ids = jnp.stack([lax.axis_index(name) for name in ("dom", "orient", "cls")])
    ids = ids.astype(jnp.int32)

    def swap_dom(array, step):
        return lax.ppermute(array, "dom", xor_pairs(dom, step))

    def swap_orient(array, step):
        return lax.ppermute(array, "orient", xor_pairs(orient, step))

    bands, meta, shard = image_bands(
        ids, orient_lists, shift_ids, fixed_weights, images, references, dom
    )
    arrived = {step: swap_dom(bands[step - 1], step) for step in [1, *range(dom - 1, 1, -1)]}
    shard, arrived[1] = lax.optimization_barrier((shard, arrived[1]))
    shards = [shard] + [swap_orient(shard, step) for step in range(1, orient)]
    half = arrived[SHARED]
    groups = [([own_band(ids, images, dom)], meta)]
    groups += [([arrived[step]], arrived[step]) for step in range(1, dom)]
    groups[SHARED] = ([half, lax.ppermute(half, "cls", xor_pairs(cls, 1))], half)

    def logits_of(picked, steps, before, micros):
        return partial_logits(ids, table_x, table_y, shards, picked, steps, before, micros)

    width = images.shape[2] // dom
    aligned_near = aligned_rows(ids, table_x, table_y, groups[:2], width)
    shards[1], aligned_near = lax.optimization_barrier((shards[1], aligned_near))
    partial = [None] * dom
    every = range(orient)
    first = logits_of(groups[:2], every[:EARLY], [], 0)
    partial[0:2] = logits_of(groups[:2], every[EARLY:], first, 20)
    partial[2:] = logits_of(groups[2:], every, [], 3)
    kept = [partial[s] + swap_dom(partial[s ^ 1], 1) for s in range(0, dom, 2)]
    here = jnp.stack(kept)
    step = 2
    there, swap = jnp.zeros_like(here), 0
    while step < dom:
        there, swap = swap_dom(here, step), step // 2
        if step * 2 < dom:
            order = np.arange(dom // 2) ^ swap
            here = here + jnp.stack([there[i] for i in order])
        step *= 2
    aligned_far = aligned_rows(ids, table_x, table_y, groups[2:], width)
    there, aligned_far = lax.optimization_barrier((there, aligned_far))
    stats = logit_stats(here, there, swap, classes, orients)

    pairs = [(i, i ^ dom) for i in range(cls * dom)]
    cross = [(i, i ^ dom ^ 1) for i in range(cls * dom)]
    stats_all = [
        stats,
        swap_dom(stats, 1),
        lax.ppermute(stats, ("cls", "dom"), pairs),
        lax.ppermute(stats, ("cls", "dom"), cross),
    ]
    prob, *terms = volume_terms(
        ids, stats_all, groups, aligned_near, aligned_far, orients, classes
    )
    terms = [terms[0]] + [swap_orient(terms[o], o) for o in range(orients - 1, 0, -1)]
    return prob[:, :classes], total_volume(terms)


def solution(mesh):
    in_specs = (
        P(None, "cls", None, ("dom", "orient")),
        P(None, ("dom", "orient"), None),
        P(("dom", "orient"), None),
        P(("dom", "orient"), None),
        P(("dom", "orient"), None),
    )
    out_specs = (P(("dom", "orient"), "cls"), P(None, "cls", "orient", "dom"))
    body = functools.partial(local, mesh.shape["dom"], mesh.shape["orient"], mesh.shape["cls"])
    return jax.shard_map(body, mesh=mesh, in_specs=in_specs, out_specs=out_specs, check_vma=False)
```

```python
import functools
import math

import jax
import jax.numpy as jnp
import numpy as np
from jax import lax
from jax.experimental import pallas as pl
from jax.experimental.pallas import tpu as pltpu
from jax.sharding import PartitionSpec as P

IMG = 256
TX = 8
TY = 8
HALF = TX // 2
LANES = 128
SUBLANES = 8
SHARED = 2
EARLY = 2
FLOPS_OF_MICRO = 1_000_000_000
VMEM_BYTES = 24 * 1024 * 1024
VMEM_SPEC = pl.BlockSpec(memory_space=pltpu.VMEM)
SMEM_SPEC = pl.BlockSpec(memory_space=pltpu.SMEM)
BF = jnp.bfloat16
F32 = jnp.float32


def trig_tables():
    steps = np.arange(1, HALF + 1)
    angle_x = 2.0 * math.pi / IMG * steps[:, None] * (np.arange(IMG) - IMG // 2)[None, :]
    angle_y = 2.0 * math.pi / IMG * np.arange(IMG // 2)[:, None] * steps[None, :]
    table_x = np.concatenate([np.cos(angle_x), np.sin(angle_x)], 0).astype(np.float32)
    table_y = np.concatenate([np.cos(angle_y), np.sin(angle_y)], 1).astype(np.float32)
    return table_x, table_y.reshape(-1)


def device_ids():
    return [lax.axis_index(name) for name in ("dom", "orient", "cls")]


def xor_pairs(size, step):
    return [(i, i ^ step) for i in range(size)]


def column_of(line):
    size = line.shape[1]
    rows = lax.broadcasted_iota(jnp.int32, (size, size), 0)
    cols = lax.broadcasted_iota(jnp.int32, (size, size), 1)
    return jnp.sum(jnp.where(rows == cols, line, 0.0), axis=1, keepdims=True)


def bands_kernel(steps, images, references, *rest):
    ids = device_ids()
    lists, rest = rest[:3], rest[3:]
    outs, meta, shard = rest[: len(steps)], rest[len(steps)], rest[len(steps) + 1]
    lines, sems, meta_sems, line_sems, shard_sem = rest[len(steps) + 2 :]
    copies = [pltpu.make_async_copy(references, shard, shard_sem)]
    for place, (step, out) in enumerate(zip(steps, outs)):
        width = out.shape[2] - LANES
        start = (ids[0] ^ step) * width
        if step == SHARED:
            start = 2 * start + ids[2] * width
        start = pl.multiple_of(start, width)
        for part in range(out.shape[0]):
            copies.append(
                pltpu.make_async_copy(
                    images.at[part, :, pl.ds(start, width)],
                    out.at[part, :, pl.ds(0, width)],
                    sems.at[place, part],
                )
            )
    line_copies = [
        pltpu.make_async_copy(source, lines[place], line_sems.at[place])
        for place, source in enumerate(lists)
    ]
    for copy in line_copies + copies:
        copy.start()
    for copy in line_copies:
        copy.wait()
    lane = lax.broadcasted_iota(jnp.int32, meta.shape[1:], 1)
    fixed = column_of(lines[2][...])
    high = fixed.astype(BF).astype(F32)
    middle = (fixed - high).astype(BF).astype(F32)
    values = [column_of(lines[0][...].astype(F32)), column_of(lines[1][...].astype(F32))]
    table = jnp.zeros(meta.shape[1:], F32)
    for place, value in enumerate(values + [high, middle, fixed - high - middle]):
        table = jnp.where(lane == place, value, table)
    meta[0] = table.astype(BF)
    meta[1] = jnp.zeros(meta.shape[1:], BF)
    meta_copies = [
        pltpu.make_async_copy(
            meta, out.at[:, :, pl.ds(out.shape[2] - LANES, LANES)], meta_sems.at[place]
        )
        for place, out in enumerate(outs)
    ]
    for copy in meta_copies:
        copy.start()
    for copy in copies + meta_copies:
        copy.wait()


def image_bands(orient_lists, shift_ids, fixed_weights, images, references, dom):
    parts, rows, pixels = images.shape
    width = pixels // dom
    steps = list(range(1, dom))
    sources = [images, references] + [
        array.reshape(1, rows) for array in (orient_lists, shift_ids, fixed_weights)
    ]
    sources = [pltpu.with_memory_space_constraint(array, pltpu.HBM) for array in sources]
    *bands, meta, shard = pl.pallas_call(
        functools.partial(bands_kernel, steps),
        out_shape=[
            pltpu.VMEM((parts, rows, width // (1 + (step == SHARED)) + LANES), images.dtype)
            for step in steps
        ]
        + [
            jax.ShapeDtypeStruct((parts, rows, LANES), BF),
            pltpu.VMEM(references.shape, references.dtype),
        ],
        in_specs=[pl.BlockSpec(memory_space=pl.ANY)] * len(sources),
        out_specs=[pl.BlockSpec(memory_space=pl.ANY)] * len(steps)
        + [pl.BlockSpec(memory_space=pltpu.VMEM), pl.BlockSpec(memory_space=pl.ANY)],
        scratch_shapes=[
            [pltpu.VMEM((1, rows), array.dtype) for array in sources[2:]],
            pltpu.SemaphoreType.DMA((len(steps), parts)),
            pltpu.SemaphoreType.DMA((len(steps),)),
            pltpu.SemaphoreType.DMA((3,)),
            pltpu.SemaphoreType.DMA,
        ],
        compiler_params=pltpu.CompilerParams(vmem_limit_bytes=VMEM_BYTES),
        cost_estimate=pl.CostEstimate(
            flops=0, bytes_accessed=4 * parts * rows * (pixels - width), transcendentals=0
        ),
        name="image_bands",
    )(*sources)
    return bands, meta, shard


def own_kernel(images, band, sems):
    ids = device_ids()
    width = band.shape[2]
    start = pl.multiple_of(ids[0] * width, width)
    copies = [
        pltpu.make_async_copy(images.at[part, :, pl.ds(start, width)], band.at[part], sems.at[part])
        for part in range(band.shape[0])
    ]
    for copy in copies:
        copy.start()
    for copy in copies:
        copy.wait()


def own_band(images, dom):
    parts, rows, pixels = images.shape
    shape = (parts, rows, pixels // dom)
    return pl.pallas_call(
        own_kernel,
        out_shape=pltpu.VMEM(shape, images.dtype),
        in_specs=[pl.BlockSpec(memory_space=pl.ANY)],
        out_specs=pl.BlockSpec(memory_space=pl.ANY),
        scratch_shapes=[pltpu.SemaphoreType.DMA((parts,))],
        compiler_params=pltpu.CompilerParams(vmem_limit_bytes=VMEM_BYTES),
        name="own_band",
    )(pltpu.with_memory_space_constraint(images, pltpu.HBM))


def in_vmem(arrays):
    placed = [pltpu.with_memory_space_constraint(array, pltpu.VMEM) for array in arrays]
    return placed, [VMEM_SPEC] * len(placed)


def flat(groups):
    return [image for images, _ in groups for image in images]


def sizes_of(groups):
    return [len(images) for images, _ in groups]


def by_group(sizes, refs):
    images, at = [], 0
    for size in sizes:
        images.append(refs[at : at + size])
        at += size
    return images, refs[at:]


def load(images, ids, part, start, size):
    if len(images) == 1:
        return images[0][part, :, pl.ds(pl.multiple_of(start, size), size)].astype(F32)
    half = images[0].shape[2] - LANES
    side = start // half
    cols = pl.ds(pl.multiple_of(start - side * half, size), size)
    mine, other = (image[part, :, cols].astype(F32) for image in images)
    return jnp.where(side == ids[2], mine, other)


def shift_references(refs, right, step, ids, orients, table_y):
    names = refs.shape[1]
    chunk = right.shape[2] // 2
    lines = chunk // IMG
    line_base = (ids[0] * orients + (ids[1] ^ step[1])) * lines
    for line in range(lines):
        to_re = slice(2 * line * IMG, (2 * line + 1) * IMG)
        to_im = slice((2 * line + 1) * IMG, (2 * line + 2) * IMG)
        base = (line_base + line) * TY
        cols = pl.ds(pl.multiple_of(step[0] * chunk + line * IMG, IMG), IMG)
        ref_re = refs[0, :, cols].astype(F32)
        ref_im = refs[1, :, cols].astype(F32)

        def put(b, re, im):
            right[step[0], b * names : (b + 1) * names, to_re] = re.astype(BF)
            right[step[0], b * names : (b + 1) * names, to_im] = im.astype(BF)

        put(TY // 2, ref_re, ref_im)
        for t in range(1, HALF + 1):
            cosine = table_y[base + t - 1]
            sine = table_y[base + HALF + t - 1]
            re_c, im_s = ref_re * cosine, ref_im * sine
            im_c, re_s = ref_im * cosine, ref_re * sine
            put(TY // 2 - t, re_c - im_s, im_c + re_s)
            if t < HALF:
                put(TY // 2 + t, re_c + im_s, im_c - re_s)


def shift_images(images, left, column, ids, table_x):
    chunk = left.shape[1] // 2
    rows = images[0][0].shape[1]
    for line in range(chunk // IMG):
        to_re = slice(2 * line * IMG, (2 * line + 1) * IMG)
        to_im = slice((2 * line + 1) * IMG, (2 * line + 2) * IMG)
        for g, group in enumerate(images):
            start = column * chunk + line * IMG
            re = load(group, ids, 0, start, IMG)
            im = load(group, ids, 1, start, IMG)

            def put(a, re, im):
                top = (g * TX + a) * rows
                left[top : top + rows, to_re] = re.astype(BF)
                left[top : top + rows, to_im] = im.astype(BF)

            put(TX // 2, re, im)
            for t in range(1, HALF + 1):
                cosine = table_x[t - 1 : t, :]
                sine = table_x[HALF + t - 1 : HALF + t, :]
                re_c, im_s = re * cosine, im * sine
                re_s, im_c = re * sine, im * cosine
                put(TX // 2 - t, re_c + im_s, im_c - re_s)
                if t < HALF:
                    put(TX // 2 + t, re_c - im_s, re_s + im_c)


def add_products(outs, left, right):
    rows = outs[0].shape[0]
    value = lax.dot_general(left, right, (((1,), (1,)), ((), ())), preferred_element_type=F32)
    for g, out in enumerate(outs):
        out[...] += value[g * rows : (g + 1) * rows]


def near_kernel(sizes, orients, steps, sums, table_y, table_x, *rest):
    ids = device_ids()
    groups, count = len(sizes), len(steps)
    shards, rest = rest[:count], rest[count:]
    images, rest = by_group(sizes, rest)
    before, rest = rest[: groups * sums], rest[groups * sums :]
    outs, (right, refs, left) = rest[:groups], rest[groups:]
    chunk = shards[0].shape[3]
    per_class = shards[0].shape[2]
    for place, shard in enumerate(shards):
        cols = slice(place * chunk, (place + 1) * chunk)
        for part in range(2):
            for k in range(shard.shape[1]):
                refs[part, k * per_class : (k + 1) * per_class, cols] = shard[part, k]
    for g, out in enumerate(outs):
        out[...] = before[g][...] if sums else jnp.zeros_like(out)

    def add_shard(place, carry):
        step = place + steps[0]
        shift_references(refs, right, (place, step), ids, orients, table_y)
        shift_images(images, left, ids[1] ^ step, ids, table_x)
        add_products(outs, left[...], right[place])
        return carry

    lax.fori_loop(0, count, add_shard, 0)


def far_kernel(sizes, counts, table_x, *rest):
    ids = device_ids()
    groups = len(sizes)
    rights, rest = rest[: len(counts)], rest[len(counts) :]
    images, rest = by_group(sizes, rest)
    outs, left = rest[:groups], rest[groups]
    for out in outs:
        out[...] = jnp.zeros_like(out)
    base = 0
    for right, count in zip(rights, counts):

        def add_shard(place, carry, base=base, right=right):
            shift_images(images, left, ids[1] ^ (place + base), ids, table_x)
            add_products(outs, left[...], right[place])
            return carry

        lax.fori_loop(0, count, add_shard, 0)
        base += count


def logits_cost(micros):
    return pl.CostEstimate(flops=micros * FLOPS_OF_MICRO, bytes_accessed=0, transcendentals=0)


def near_logits(table_x, table_y, shards, picked, steps, before, micros):
    parts, classes, orients, chunk = shards[0].shape
    groups = len(picked)
    rows = picked[0][0][0].shape[1]
    names = classes * orients
    count = len(steps)
    out_shape = (TX * rows, TY * names)
    used = [shards[step] for step in steps]
    arrays, specs = in_vmem([table_x, *used, *flat(picked), *before])
    *sums, right = pl.pallas_call(
        functools.partial(
            near_kernel, sizes_of(picked), len(shards), steps, len(before) > 0
        ),
        out_shape=[pltpu.VMEM(out_shape, F32)] * groups
        + [pltpu.VMEM((count, TY * names, 2 * chunk), BF)],
        in_specs=[SMEM_SPEC] + specs,
        out_specs=[VMEM_SPEC] * (groups + 1),
        scratch_shapes=[
            pltpu.VMEM((parts, names, count * chunk), BF),
            pltpu.VMEM((groups * TX * rows, 2 * chunk), BF),
        ],
        compiler_params=pltpu.CompilerParams(vmem_limit_bytes=VMEM_BYTES),
        cost_estimate=logits_cost(micros),
        name="near_logits",
    )(table_y, *arrays)
    return sums, right


def far_logits(table_x, rights, picked, micros):
    groups = len(picked)
    rows = picked[0][0][0].shape[1]
    names, chunk = rights[0].shape[1:]
    out_shape = (TX * rows, names)
    arrays, specs = in_vmem([table_x, *rights, *flat(picked)])
    return pl.pallas_call(
        functools.partial(far_kernel, sizes_of(picked), [right.shape[0] for right in rights]),
        out_shape=[pltpu.VMEM(out_shape, F32)] * groups,
        in_specs=specs,
        out_specs=[VMEM_SPEC] * groups,
        scratch_shapes=[pltpu.VMEM((groups * TX * rows, chunk), BF)],
        compiler_params=pltpu.CompilerParams(vmem_limit_bytes=VMEM_BYTES),
        cost_estimate=logits_cost(micros),
        name="far_logits",
    )(*arrays)


def stats_kernel(swap, classes, orients, here, there, out):
    groups, group_rows, lanes = here.shape
    rows = group_rows // TX
    lane = lax.broadcasted_iota(jnp.int32, (rows, lanes), 1)
    class_of = (lane // orients) % classes
    out_lane = lax.broadcasted_iota(jnp.int32, (rows, LANES), 1)
    for g in range(groups):
        logits = here[g] + there[g ^ swap]
        pieces = [logits[a * rows : (a + 1) * rows] for a in range(TX)]
        top = functools.reduce(jnp.maximum, pieces)
        top = jnp.max(top, axis=1, keepdims=True)
        sums = sum(jnp.exp(piece - top) for piece in pieces)
        line = jnp.where(out_lane == 0, top, 0.0)
        for k in range(classes):
            part = jnp.sum(jnp.where(class_of == k, sums, 0.0), axis=1, keepdims=True)
            line = jnp.where(out_lane == k + 1, part, line)
        out[g * rows : (g + 1) * rows, :] = line


def logit_stats(here, there, swap, classes, orients):
    groups, group_rows, lanes = here.shape
    arrays, specs = in_vmem([here, there])
    return pl.pallas_call(
        functools.partial(stats_kernel, swap, classes, orients),
        out_shape=pltpu.VMEM((groups * group_rows // TX, LANES), F32),
        in_specs=specs,
        out_specs=VMEM_SPEC,
        compiler_params=pltpu.CompilerParams(vmem_limit_bytes=VMEM_BYTES),
        cost_estimate=pl.CostEstimate(
            flops=4 * here.size, bytes_accessed=8 * here.size, transcendentals=here.size
        ),
        name="logit_stats",
    )(*arrays)


def rows_kernel(sizes, table_y, table_x, *rest):
    ids = device_ids()
    groups = len(sizes)
    metas = rest[:groups]
    images, (out,) = by_group(sizes, rest[groups:])
    rows = metas[0].shape[1]
    width = out.shape[2]
    lines = width // IMG
    line_base = ids[0] * lines
    for g in range(groups):
        own = slice(g * rows, (g + 1) * rows)
        last = metas[g].shape[2] - LANES
        shift = metas[g][0, :, last:].astype(F32)[:, 1:2].astype(jnp.int32)
        move_x = jnp.broadcast_to(shift % TX - TX // 2, (rows, IMG))
        move_y = jnp.broadcast_to(shift // TX - TY // 2, (rows, LANES))
        phase_c = jnp.ones((rows, IMG), F32)
        phase_s = jnp.zeros((rows, IMG), F32)
        for t in range(1, HALF + 1):
            hit = jnp.abs(move_x) == t
            phase_c = jnp.where(hit, table_x[t - 1 : t, :], phase_c)
            phase_s = jnp.where(hit, table_x[HALF + t - 1 : HALF + t, :], phase_s)
        phase_s = jnp.where(move_x < 0, -phase_s, phase_s)
        hits = [jnp.abs(move_y) == t for t in range(1, HALF + 1)]
        sign = jnp.where(move_y < 0, -1.0, 1.0)

        def add_line(line, carry):
            base = (line_base + line) * TY
            cos_y = jnp.ones((rows, LANES), F32)
            sin_y = jnp.zeros((rows, LANES), F32)
            for t in range(1, HALF + 1):
                cos_y = jnp.where(hits[t - 1], table_y[base + t - 1], cos_y)
                sin_y = jnp.where(hits[t - 1], table_y[base + HALF + t - 1], sin_y)
            sin_y = sin_y * sign
            for part in range(IMG // LANES):
                across = slice(part * LANES, (part + 1) * LANES)
                start = pl.multiple_of(line * IMG + part * LANES, LANES)
                cols = pl.ds(start, LANES)
                cos_x, sin_x = phase_c[:, across], phase_s[:, across]
                cosine = cos_x * cos_y - sin_x * sin_y
                sine = sin_x * cos_y + cos_x * sin_y
                re = load(images[g], ids, 0, start, LANES)
                im = load(images[g], ids, 1, start, LANES)
                out[0, own, cols] = (re * cosine - im * sine).astype(BF)
                out[1, own, cols] = (re * sine + im * cosine).astype(BF)
            return carry

        lax.fori_loop(0, lines, add_line, 0, unroll=min(lines, 4))


def aligned_rows(table_x, table_y, picked, width):
    parts, rows = picked[0][0][0].shape[:2]
    groups = len(picked)
    arrays, specs = in_vmem([table_x] + [table for _, table in picked] + flat(picked))
    return pl.pallas_call(
        functools.partial(rows_kernel, sizes_of(picked)),
        out_shape=pltpu.VMEM((parts, groups * rows, width), BF),
        in_specs=[SMEM_SPEC] + specs,
        out_specs=VMEM_SPEC,
        compiler_params=pltpu.CompilerParams(vmem_limit_bytes=VMEM_BYTES),
        cost_estimate=pl.CostEstimate(
            flops=0,
            bytes_accessed=0,
            transcendentals=0,
        ),
        name="aligned_rows",
    )(table_y, *arrays)


def volume_kernel(groups, orients, classes, *rest):
    ids = device_ids()
    stats, metas = rest[:4], rest[4 : 4 + groups]
    near, far = rest[4 + groups], rest[5 + groups]
    prob, outs = rest[6 + groups], rest[7 + groups :]
    rows = metas[0].shape[1]
    width = near.shape[2]
    chunk = min(width, 8 * IMG)
    lane = lax.broadcasted_iota(jnp.int32, (rows, LANES), 1)
    pieces = []
    for g in range(groups):
        mine, other = (stats[0], stats[2]) if g % 2 == 0 else (stats[1], stats[3])
        place = g // 2
        mine = mine[place * rows : (place + 1) * rows, :]
        other = other[place * rows : (place + 1) * rows, :]
        top = jnp.maximum(mine[:, 0:1], other[:, 0:1])
        mine_scale = jnp.exp(mine[:, 0:1] - top)
        other_scale = jnp.exp(other[:, 0:1] - top)
        held = (lane >= 1) & (lane <= classes)
        both = jnp.where(held, mine * mine_scale + other * other_scale, 0.0)
        totals = jnp.sum(both, axis=1, keepdims=True)
        spread = jnp.zeros((rows, LANES), F32)
        for k in range(classes):
            spread = jnp.where(lane % SUBLANES == k, mine[:, k + 1 : k + 2], spread)
        class_prob = spread * mine_scale / totals
        if g == 0:
            prob[...] = class_prob
        last = metas[g].shape[2] - LANES
        table = metas[g][0, :, last:].astype(F32)
        fixed = table[:, 2:3] + table[:, 3:4] + table[:, 4:5]
        weight = (fixed * class_prob).astype(BF).astype(F32)
        bin_of = table[:, 0:1].astype(jnp.int32) ^ ids[1]
        pieces.append(jnp.where(lane // SUBLANES == bin_of, weight, 0.0))
    mixes = []
    for held in (pieces[:2], pieces[2:]):
        mixing = jnp.transpose(jnp.concatenate(held, axis=0))
        mixes.append(mixing[: orients * SUBLANES].astype(BF))
    for part in range(2):
        for column in range(0, width, chunk):
            cols = slice(column, column + chunk)
            value = jnp.dot(mixes[0], near[part, :, cols], preferred_element_type=F32)
            value += jnp.dot(mixes[1], far[part, :, cols], preferred_element_type=F32)
            for o in range(orients):
                term = value[o * SUBLANES : o * SUBLANES + classes]
                outs[o][part, :, cols] = term.astype(outs[o].dtype)


def volume_terms(stats, groups, near, far, orients, classes):
    parts, entries, width = near.shape
    rest = far.shape[1]
    rows = groups[0][1].shape[1]
    out_shape = (parts, classes, width)
    arrays, specs = in_vmem([*stats, *(table for _, table in groups), near, far])
    return pl.pallas_call(
        functools.partial(volume_kernel, len(groups), orients, classes),
        out_shape=[pltpu.VMEM((rows, LANES), F32)]
        + [pltpu.VMEM(out_shape, F32 if o == 0 else BF) for o in range(orients)],
        in_specs=specs,
        out_specs=[VMEM_SPEC] * (1 + orients),
        compiler_params=pltpu.CompilerParams(vmem_limit_bytes=VMEM_BYTES),
        cost_estimate=pl.CostEstimate(
            flops=4 * orients * classes * (entries + rest) * width,
            bytes_accessed=4 * (entries + rest) * width + 4 * orients * classes * width,
            transcendentals=0,
        ),
        name="volume_terms",
    )(*arrays)


def total_kernel(first, *rest):
    out = rest[-1]
    total = first[...]
    for term in rest[:-1]:
        total = total + term[...].astype(F32)
    for part in range(out.shape[0]):
        for k in range(out.shape[1]):
            out[part, k] = total[part, k : k + 1]


def total_volume(terms):
    parts, classes, width = terms[0].shape
    arrays, specs = in_vmem(terms)
    return pl.pallas_call(
        total_kernel,
        out_shape=jax.ShapeDtypeStruct((parts, classes, 1, width), F32),
        in_specs=specs,
        compiler_params=pltpu.CompilerParams(vmem_limit_bytes=VMEM_BYTES),
        name="total_volume",
    )(*arrays)


def local(dom, orient, cls, references, images, orient_lists, shift_ids, fixed_weights):
    classes, orients = references.shape[1], references.shape[2]
    table_x, table_y = (jnp.asarray(t) for t in trig_tables())

    def swap_dom(array, step):
        return lax.ppermute(array, "dom", xor_pairs(dom, step))

    def swap_orient(array, step):
        return lax.ppermute(array, "orient", xor_pairs(orient, step))

    bands, meta, shard = image_bands(
        orient_lists, shift_ids, fixed_weights, images, references, dom
    )
    arrived = {step: swap_dom(bands[step - 1], step) for step in [1, *range(dom - 1, 1, -1)]}
    shard, arrived[1] = lax.optimization_barrier((shard, arrived[1]))
    shards = [shard] + [swap_orient(shard, step) for step in range(1, orient)]
    half = arrived[SHARED]
    groups = [([own_band(images, dom)], meta)]
    groups += [([arrived[step]], arrived[step]) for step in range(1, dom)]
    groups[SHARED] = ([half, lax.ppermute(half, "cls", xor_pairs(cls, 1))], half)

    width = images.shape[2] // dom
    aligned_near = aligned_rows(table_x, table_y, groups[:2], width)
    shards[1], aligned_near = lax.optimization_barrier((shards[1], aligned_near))
    every = range(orient)
    first, right = near_logits(table_x, table_y, shards, groups[:2], every[:EARLY], [], 0)
    near, right_late = near_logits(
        table_x, table_y, shards, groups[:2], every[EARLY:], first, 20
    )
    swapped = swap_dom(near[1], 1)
    right_late, swapped = lax.optimization_barrier((right_late, swapped))
    far = far_logits(table_x, [right, right_late], groups[2:], 6)
    partial = [*near, *far]
    kept = [near[0] + swapped]
    kept += [partial[s] + swap_dom(partial[s ^ 1], 1) for s in range(2, dom, 2)]
    here = jnp.stack(kept)
    step = 2
    there, swap = jnp.zeros_like(here), 0
    while step < dom:
        there, swap = swap_dom(here, step), step // 2
        if step * 2 < dom:
            order = np.arange(dom // 2) ^ swap
            here = here + jnp.stack([there[i] for i in order])
        step *= 2
    aligned_far = aligned_rows(table_x, table_y, groups[2:], width)
    there, aligned_far = lax.optimization_barrier((there, aligned_far))
    stats = logit_stats(here, there, swap, classes, orients)

    pairs = [(i, i ^ dom) for i in range(cls * dom)]
    cross = [(i, i ^ dom ^ 1) for i in range(cls * dom)]
    stats_all = [
        stats,
        swap_dom(stats, 1),
        lax.ppermute(stats, ("cls", "dom"), pairs),
        lax.ppermute(stats, ("cls", "dom"), cross),
    ]
    prob, *terms = volume_terms(
        stats_all, groups, aligned_near, aligned_far, orients, classes
    )
    order = sorted(range(1, orients), key=lambda place: place != orients // 2)
    terms = [terms[0]] + [swap_orient(terms[o], o) for o in order]
    return prob[:, :classes], total_volume(terms)


def solution(mesh):
    in_specs = (
        P(None, "cls", None, ("dom", "orient")),
        P(None, ("dom", "orient"), None),
        P(("dom", "orient"), None),
        P(("dom", "orient"), None),
        P(("dom", "orient"), None),
    )
    out_specs = (P(("dom", "orient"), "cls"), P(None, "cls", "orient", "dom"))
    body = functools.partial(local, mesh.shape["dom"], mesh.shape["orient"], mesh.shape["cls"])
    return jax.shard_map(body, mesh=mesh, in_specs=in_specs, out_specs=out_specs, check_vma=False)
```

```python
import functools
import math

import jax
import jax.numpy as jnp
import numpy as np
from jax import lax
from jax.experimental import pallas as pl
from jax.experimental.pallas import tpu as pltpu
from jax.sharding import PartitionSpec as P

IMG = 256
TX = 8
TY = 8
HALF = TX // 2
LANES = 128
SUBLANES = 8
SHARED = 2
EARLY = 2
FLOPS_OF_MICRO = 1_000_000_000
VMEM_BYTES = 24 * 1024 * 1024
VMEM_SPEC = pl.BlockSpec(memory_space=pltpu.VMEM)
SMEM_SPEC = pl.BlockSpec(memory_space=pltpu.SMEM)
BF = jnp.bfloat16
F32 = jnp.float32


def trig_tables():
    steps = np.arange(1, HALF + 1)
    angle_x = 2.0 * math.pi / IMG * steps[:, None] * (np.arange(IMG) - IMG // 2)[None, :]
    angle_y = 2.0 * math.pi / IMG * np.arange(IMG // 2)[:, None] * steps[None, :]
    table_x = np.concatenate([np.cos(angle_x), np.sin(angle_x)], 0).astype(np.float32)
    table_y = np.concatenate([np.cos(angle_y), np.sin(angle_y)], 1).astype(np.float32)
    return table_x, table_y.reshape(-1)


def device_ids():
    return [lax.axis_index(name) for name in ("dom", "orient", "cls")]


def xor_pairs(size, step):
    return [(i, i ^ step) for i in range(size)]


def column_of(line):
    size = line.shape[1]
    rows = lax.broadcasted_iota(jnp.int32, (size, size), 0)
    cols = lax.broadcasted_iota(jnp.int32, (size, size), 1)
    return jnp.sum(jnp.where(rows == cols, line, 0.0), axis=1, keepdims=True)


def bands_kernel(steps, images, references, *rest):
    ids = device_ids()
    lists, rest = rest[:3], rest[3:]
    outs, meta, shard = rest[: len(steps)], rest[len(steps)], rest[len(steps) + 1]
    lines, sems, meta_sems, line_sems, shard_sem = rest[len(steps) + 2 :]
    copies = [pltpu.make_async_copy(references, shard, shard_sem)]
    for place, (step, out) in enumerate(zip(steps, outs)):
        width = out.shape[2] - LANES
        start = (ids[0] ^ step) * width
        if step == SHARED:
            start = 2 * start + ids[2] * width
        start = pl.multiple_of(start, width)
        for part in range(out.shape[0]):
            copies.append(
                pltpu.make_async_copy(
                    images.at[part, :, pl.ds(start, width)],
                    out.at[part, :, pl.ds(0, width)],
                    sems.at[place, part],
                )
            )
    line_copies = [
        pltpu.make_async_copy(source, lines[place], line_sems.at[place])
        for place, source in enumerate(lists)
    ]
    for copy in line_copies + copies:
        copy.start()
    for copy in line_copies:
        copy.wait()
    lane = lax.broadcasted_iota(jnp.int32, meta.shape[1:], 1)
    fixed = column_of(lines[2][...])
    high = fixed.astype(BF).astype(F32)
    middle = (fixed - high).astype(BF).astype(F32)
    values = [column_of(lines[0][...].astype(F32)), column_of(lines[1][...].astype(F32))]
    table = jnp.zeros(meta.shape[1:], F32)
    for place, value in enumerate(values + [high, middle, fixed - high - middle]):
        table = jnp.where(lane == place, value, table)
    meta[0] = table.astype(BF)
    meta[1] = jnp.zeros(meta.shape[1:], BF)
    meta_copies = [
        pltpu.make_async_copy(
            meta, out.at[:, :, pl.ds(out.shape[2] - LANES, LANES)], meta_sems.at[place]
        )
        for place, out in enumerate(outs)
    ]
    for copy in meta_copies:
        copy.start()
    for copy in copies + meta_copies:
        copy.wait()


def image_bands(orient_lists, shift_ids, fixed_weights, images, references, dom):
    parts, rows, pixels = images.shape
    width = pixels // dom
    steps = list(range(1, dom))
    sources = [images, references] + [
        array.reshape(1, rows) for array in (orient_lists, shift_ids, fixed_weights)
    ]
    sources = [pltpu.with_memory_space_constraint(array, pltpu.HBM) for array in sources]
    *bands, meta, shard = pl.pallas_call(
        functools.partial(bands_kernel, steps),
        out_shape=[
            pltpu.VMEM((parts, rows, width // (1 + (step == SHARED)) + LANES), images.dtype)
            for step in steps
        ]
        + [
            jax.ShapeDtypeStruct((parts, rows, LANES), BF),
            pltpu.VMEM(references.shape, references.dtype),
        ],
        in_specs=[pl.BlockSpec(memory_space=pl.ANY)] * len(sources),
        out_specs=[pl.BlockSpec(memory_space=pl.ANY)] * len(steps)
        + [pl.BlockSpec(memory_space=pltpu.VMEM), pl.BlockSpec(memory_space=pl.ANY)],
        scratch_shapes=[
            [pltpu.VMEM((1, rows), array.dtype) for array in sources[2:]],
            pltpu.SemaphoreType.DMA((len(steps), parts)),
            pltpu.SemaphoreType.DMA((len(steps),)),
            pltpu.SemaphoreType.DMA((3,)),
            pltpu.SemaphoreType.DMA,
        ],
        compiler_params=pltpu.CompilerParams(vmem_limit_bytes=VMEM_BYTES),
        cost_estimate=pl.CostEstimate(
            flops=0, bytes_accessed=4 * parts * rows * (pixels - width), transcendentals=0
        ),
        name="image_bands",
    )(*sources)
    return bands, meta, shard


def own_kernel(images, band, sems):
    ids = device_ids()
    width = band.shape[2]
    start = pl.multiple_of(ids[0] * width, width)
    copies = [
        pltpu.make_async_copy(images.at[part, :, pl.ds(start, width)], band.at[part], sems.at[part])
        for part in range(band.shape[0])
    ]
    for copy in copies:
        copy.start()
    for copy in copies:
        copy.wait()


def own_band(images, dom):
    parts, rows, pixels = images.shape
    shape = (parts, rows, pixels // dom)
    return pl.pallas_call(
        own_kernel,
        out_shape=pltpu.VMEM(shape, images.dtype),
        in_specs=[pl.BlockSpec(memory_space=pl.ANY)],
        out_specs=pl.BlockSpec(memory_space=pl.ANY),
        scratch_shapes=[pltpu.SemaphoreType.DMA((parts,))],
        compiler_params=pltpu.CompilerParams(vmem_limit_bytes=VMEM_BYTES),
        name="own_band",
    )(pltpu.with_memory_space_constraint(images, pltpu.HBM))


def in_vmem(arrays):
    placed = [pltpu.with_memory_space_constraint(array, pltpu.VMEM) for array in arrays]
    return placed, [VMEM_SPEC] * len(placed)


def flat(groups):
    return [image for images, _ in groups for image in images]


def sizes_of(groups):
    return [len(images) for images, _ in groups]


def by_group(sizes, refs):
    images, at = [], 0
    for size in sizes:
        images.append(refs[at : at + size])
        at += size
    return images, refs[at:]


def load(images, ids, part, start, size):
    if len(images) == 1:
        return images[0][part, :, pl.ds(pl.multiple_of(start, size), size)].astype(F32)
    half = images[0].shape[2] - LANES
    side = start // half
    cols = pl.ds(pl.multiple_of(start - side * half, size), size)
    mine, other = (image[part, :, cols].astype(F32) for image in images)
    return jnp.where(side == ids[2], mine, other)


def shift_references(refs, right, step, ids, orients, table_y):
    names = refs.shape[1]
    chunk = right.shape[2] // 2
    lines = chunk // IMG
    line_base = (ids[0] * orients + (ids[1] ^ step[1])) * lines
    for line in range(lines):
        to_re = slice(2 * line * IMG, (2 * line + 1) * IMG)
        to_im = slice((2 * line + 1) * IMG, (2 * line + 2) * IMG)
        base = (line_base + line) * TY
        cols = pl.ds(pl.multiple_of(step[0] * chunk + line * IMG, IMG), IMG)
        ref_re = refs[0, :, cols].astype(F32)
        ref_im = refs[1, :, cols].astype(F32)

        def put(b, re, im):
            right[step[0], b * names : (b + 1) * names, to_re] = re.astype(BF)
            right[step[0], b * names : (b + 1) * names, to_im] = im.astype(BF)

        put(TY // 2, ref_re, ref_im)
        for t in range(1, HALF + 1):
            cosine = table_y[base + t - 1]
            sine = table_y[base + HALF + t - 1]
            re_c, im_s = ref_re * cosine, ref_im * sine
            im_c, re_s = ref_im * cosine, ref_re * sine
            put(TY // 2 - t, re_c - im_s, im_c + re_s)
            if t < HALF:
                put(TY // 2 + t, re_c + im_s, im_c - re_s)


def shift_images(images, left, column, ids, table_x):
    chunk = left.shape[1] // 2
    rows = images[0][0].shape[1]
    for line in range(chunk // IMG):
        to_re = slice(2 * line * IMG, (2 * line + 1) * IMG)
        to_im = slice((2 * line + 1) * IMG, (2 * line + 2) * IMG)
        for g, group in enumerate(images):
            start = column * chunk + line * IMG
            re = load(group, ids, 0, start, IMG)
            im = load(group, ids, 1, start, IMG)

            def put(a, re, im):
                top = (g * TX + a) * rows
                left[top : top + rows, to_re] = re.astype(BF)
                left[top : top + rows, to_im] = im.astype(BF)

            put(TX // 2, re, im)
            for t in range(1, HALF + 1):
                cosine = table_x[t - 1 : t, :]
                sine = table_x[HALF + t - 1 : HALF + t, :]
                re_c, im_s = re * cosine, im * sine
                re_s, im_c = re * sine, im * cosine
                put(TX // 2 - t, re_c + im_s, im_c - re_s)
                if t < HALF:
                    put(TX // 2 + t, re_c - im_s, re_s + im_c)


def add_products(outs, left, right):
    rows = outs[0].shape[0]
    value = lax.dot_general(left, right, (((1,), (1,)), ((), ())), preferred_element_type=F32)
    for g, out in enumerate(outs):
        out[...] += value[g * rows : (g + 1) * rows]


def near_kernel(sizes, orients, steps, sums, table_y, table_x, *rest):
    ids = device_ids()
    groups, count = len(sizes), len(steps)
    shards, rest = rest[:count], rest[count:]
    images, rest = by_group(sizes, rest)
    before, rest = rest[: groups * sums], rest[groups * sums :]
    outs, (right, refs, left) = rest[:groups], rest[groups:]
    chunk = shards[0].shape[3]
    per_class = shards[0].shape[2]
    for place, shard in enumerate(shards):
        cols = slice(place * chunk, (place + 1) * chunk)
        for part in range(2):
            for k in range(shard.shape[1]):
                refs[part, k * per_class : (k + 1) * per_class, cols] = shard[part, k]
    for g, out in enumerate(outs):
        out[...] = before[g][...] if sums else jnp.zeros_like(out)

    def add_shard(place, carry):
        step = place + steps[0]
        shift_references(refs, right, (place, step), ids, orients, table_y)
        shift_images(images, left, ids[1] ^ step, ids, table_x)
        add_products(outs, left[...], right[place])
        return carry

    lax.fori_loop(0, count, add_shard, 0)


def far_kernel(sizes, counts, table_x, *rest):
    ids = device_ids()
    groups = len(sizes)
    rights, rest = rest[: len(counts)], rest[len(counts) :]
    images, rest = by_group(sizes, rest)
    outs, left = rest[:groups], rest[groups]
    for out in outs:
        out[...] = jnp.zeros_like(out)
    base = 0
    for right, count in zip(rights, counts):

        def add_shard(place, carry, base=base, right=right):
            shift_images(images, left, ids[1] ^ (place + base), ids, table_x)
            add_products(outs, left[...], right[place])
            return carry

        lax.fori_loop(0, count, add_shard, 0)
        base += count


def logits_cost(micros):
    return pl.CostEstimate(flops=micros * FLOPS_OF_MICRO, bytes_accessed=0, transcendentals=0)


def near_logits(table_x, table_y, shards, picked, steps, before, micros):
    parts, classes, orients, chunk = shards[0].shape
    groups = len(picked)
    rows = picked[0][0][0].shape[1]
    names = classes * orients
    count = len(steps)
    out_shape = (TX * rows, TY * names)
    used = [shards[step] for step in steps]
    arrays, specs = in_vmem([table_x, *used, *flat(picked), *before])
    *sums, right = pl.pallas_call(
        functools.partial(
            near_kernel, sizes_of(picked), len(shards), steps, len(before) > 0
        ),
        out_shape=[pltpu.VMEM(out_shape, F32)] * groups
        + [pltpu.VMEM((count, TY * names, 2 * chunk), BF)],
        in_specs=[SMEM_SPEC] + specs,
        out_specs=[VMEM_SPEC] * (groups + 1),
        scratch_shapes=[
            pltpu.VMEM((parts, names, count * chunk), BF),
            pltpu.VMEM((groups * TX * rows, 2 * chunk), BF),
        ],
        compiler_params=pltpu.CompilerParams(vmem_limit_bytes=VMEM_BYTES),
        cost_estimate=logits_cost(micros),
        name="near_logits",
    )(table_y, *arrays)
    return sums, right


def far_logits(table_x, rights, picked, micros):
    groups = len(picked)
    rows = picked[0][0][0].shape[1]
    names, chunk = rights[0].shape[1:]
    out_shape = (TX * rows, names)
    arrays, specs = in_vmem([table_x, *rights, *flat(picked)])
    return pl.pallas_call(
        functools.partial(far_kernel, sizes_of(picked), [right.shape[0] for right in rights]),
        out_shape=[pltpu.VMEM(out_shape, F32)] * groups,
        in_specs=specs,
        out_specs=[VMEM_SPEC] * groups,
        scratch_shapes=[pltpu.VMEM((groups * TX * rows, chunk), BF)],
        compiler_params=pltpu.CompilerParams(vmem_limit_bytes=VMEM_BYTES),
        cost_estimate=logits_cost(micros),
        name="far_logits",
    )(*arrays)


def stats_kernel(counts, classes, orients, *refs):
    *logits, out = refs
    rows, lanes = logits[0].shape[0] // TX, logits[0].shape[1]
    lane = lax.broadcasted_iota(jnp.int32, (rows, lanes), 1)
    class_of = (lane // orients) % classes
    out_lane = lax.broadcasted_iota(jnp.int32, (rows, LANES), 1)
    packed = jnp.zeros((SUBLANES, LANES), F32)
    for g, count in enumerate(counts):
        total = sum(ref[...] for ref in logits[:count])
        logits = logits[count:]
        pieces = [total[a * rows : (a + 1) * rows] for a in range(TX)]
        top = functools.reduce(jnp.maximum, pieces)
        top = jnp.max(top, axis=1, keepdims=True)
        sums = sum(jnp.exp(piece - top) for piece in pieces)
        line = jnp.where(out_lane == 0, top, 0.0)
        for k in range(classes):
            part = jnp.sum(jnp.where(class_of == k, sums, 0.0), axis=1, keepdims=True)
            line = jnp.where(out_lane == k + 1, part, line)
        for half in range(rows // SUBLANES):
            block = line[half * SUBLANES : (half + 1) * SUBLANES]
            place = (g * (rows // SUBLANES) + half) * SUBLANES
            packed = packed + pltpu.roll(block, place, 1)
    out[...] = packed


def logit_stats(terms, classes, orients):
    arrays, specs = in_vmem([array for held in terms for array in held])
    return pl.pallas_call(
        functools.partial(stats_kernel, [len(held) for held in terms], classes, orients),
        out_shape=pltpu.VMEM((SUBLANES, LANES), F32),
        in_specs=specs,
        out_specs=VMEM_SPEC,
        compiler_params=pltpu.CompilerParams(vmem_limit_bytes=VMEM_BYTES),
        name="logit_stats",
    )(*arrays)


def rows_kernel(sizes, table_y, table_x, *rest):
    ids = device_ids()
    groups = len(sizes)
    metas = rest[:groups]
    images, (out,) = by_group(sizes, rest[groups:])
    rows = metas[0].shape[1]
    width = out.shape[2]
    lines = width // IMG
    line_base = ids[0] * lines
    for g in range(groups):
        own = slice(g * rows, (g + 1) * rows)
        last = metas[g].shape[2] - LANES
        shift = metas[g][0, :, last:].astype(F32)[:, 1:2].astype(jnp.int32)
        move_x = jnp.broadcast_to(shift % TX - TX // 2, (rows, IMG))
        move_y = jnp.broadcast_to(shift // TX - TY // 2, (rows, LANES))
        phase_c = jnp.ones((rows, IMG), F32)
        phase_s = jnp.zeros((rows, IMG), F32)
        for t in range(1, HALF + 1):
            hit = jnp.abs(move_x) == t
            phase_c = jnp.where(hit, table_x[t - 1 : t, :], phase_c)
            phase_s = jnp.where(hit, table_x[HALF + t - 1 : HALF + t, :], phase_s)
        phase_s = jnp.where(move_x < 0, -phase_s, phase_s)
        hits = [jnp.abs(move_y) == t for t in range(1, HALF + 1)]
        sign = jnp.where(move_y < 0, -1.0, 1.0)

        def add_line(line, carry):
            base = (line_base + line) * TY
            cos_y = jnp.ones((rows, LANES), F32)
            sin_y = jnp.zeros((rows, LANES), F32)
            for t in range(1, HALF + 1):
                cos_y = jnp.where(hits[t - 1], table_y[base + t - 1], cos_y)
                sin_y = jnp.where(hits[t - 1], table_y[base + HALF + t - 1], sin_y)
            sin_y = sin_y * sign
            for part in range(IMG // LANES):
                across = slice(part * LANES, (part + 1) * LANES)
                start = pl.multiple_of(line * IMG + part * LANES, LANES)
                cols = pl.ds(start, LANES)
                cos_x, sin_x = phase_c[:, across], phase_s[:, across]
                cosine = cos_x * cos_y - sin_x * sin_y
                sine = sin_x * cos_y + cos_x * sin_y
                re = load(images[g], ids, 0, start, LANES)
                im = load(images[g], ids, 1, start, LANES)
                out[0, own, cols] = (re * cosine - im * sine).astype(BF)
                out[1, own, cols] = (re * sine + im * cosine).astype(BF)
            return carry

        lax.fori_loop(0, lines, add_line, 0, unroll=min(lines, 4))


def aligned_rows(table_x, table_y, picked, width):
    parts, rows = picked[0][0][0].shape[:2]
    groups = len(picked)
    arrays, specs = in_vmem([table_x] + [table for _, table in picked] + flat(picked))
    return pl.pallas_call(
        functools.partial(rows_kernel, sizes_of(picked)),
        out_shape=pltpu.VMEM((parts, groups * rows, width), BF),
        in_specs=[SMEM_SPEC] + specs,
        out_specs=VMEM_SPEC,
        compiler_params=pltpu.CompilerParams(vmem_limit_bytes=VMEM_BYTES),
        cost_estimate=pl.CostEstimate(
            flops=0,
            bytes_accessed=0,
            transcendentals=0,
        ),
        name="aligned_rows",
    )(table_y, *arrays)


def unpacked(packed, place, blocks):
    first = place * blocks * SUBLANES
    return jnp.concatenate(
        [pltpu.roll(packed, (LANES - first - i * SUBLANES) % LANES, 1) for i in range(blocks)]
    )


def volume_kernel(groups, orients, classes, *rest):
    ids = device_ids()
    stats, metas = rest[:2], rest[2 : 2 + groups]
    near, far = rest[2 + groups], rest[3 + groups]
    prob, outs = rest[4 + groups], rest[5 + groups :]
    rows = metas[0].shape[1]
    width = near.shape[2]
    chunk = min(width, 8 * IMG)
    lane = lax.broadcasted_iota(jnp.int32, (rows, LANES), 1)
    pieces = []
    for g in range(groups):
        top = g % 2 * SUBLANES
        mine, other = (
            unpacked(ref[top : top + SUBLANES, :], g // 2, rows // SUBLANES) for ref in stats
        )
        top = jnp.maximum(mine[:, 0:1], other[:, 0:1])
        mine_scale = jnp.exp(mine[:, 0:1] - top)
        other_scale = jnp.exp(other[:, 0:1] - top)
        held = (lane >= 1) & (lane <= classes)
        both = jnp.where(held, mine * mine_scale + other * other_scale, 0.0)
        totals = jnp.sum(both, axis=1, keepdims=True)
        spread = jnp.zeros((rows, LANES), F32)
        for k in range(classes):
            spread = jnp.where(lane % SUBLANES == k, mine[:, k + 1 : k + 2], spread)
        class_prob = spread * mine_scale / totals
        if g == 0:
            prob[...] = class_prob
        last = metas[g].shape[2] - LANES
        table = metas[g][0, :, last:].astype(F32)
        fixed = table[:, 2:3] + table[:, 3:4] + table[:, 4:5]
        weight = (fixed * class_prob).astype(BF).astype(F32)
        bin_of = table[:, 0:1].astype(jnp.int32) ^ ids[1]
        pieces.append(jnp.where(lane // SUBLANES == bin_of, weight, 0.0))
    mixes = []
    for held in (pieces[:2], pieces[2:]):
        mixing = jnp.transpose(jnp.concatenate(held, axis=0))
        mixes.append(mixing[: orients * SUBLANES].astype(BF))
    for part in range(2):
        for column in range(0, width, chunk):
            cols = slice(column, column + chunk)
            value = jnp.dot(mixes[0], near[part, :, cols], preferred_element_type=F32)
            value += jnp.dot(mixes[1], far[part, :, cols], preferred_element_type=F32)
            for o in range(orients):
                term = value[o * SUBLANES : o * SUBLANES + classes]
                outs[o][part, :, cols] = term.astype(outs[o].dtype)


def volume_terms(stats, groups, near, far, orients, classes):
    parts, entries, width = near.shape
    rest = far.shape[1]
    rows = groups[0][1].shape[1]
    out_shape = (parts, classes, width)
    arrays, specs = in_vmem([*stats, *(table for _, table in groups), near, far])
    return pl.pallas_call(
        functools.partial(volume_kernel, len(groups), orients, classes),
        out_shape=[pltpu.VMEM((rows, LANES), F32)]
        + [pltpu.VMEM(out_shape, F32 if o == 0 else BF) for o in range(orients)],
        in_specs=specs,
        out_specs=[VMEM_SPEC] * (1 + orients),
        compiler_params=pltpu.CompilerParams(vmem_limit_bytes=VMEM_BYTES),
        cost_estimate=pl.CostEstimate(
            flops=4 * orients * classes * (entries + rest) * width,
            bytes_accessed=4 * (entries + rest) * width + 4 * orients * classes * width,
            transcendentals=0,
        ),
        name="volume_terms",
    )(*arrays)


def total_kernel(first, *rest):
    out = rest[-1]
    total = first[...]
    for term in rest[:-1]:
        total = total + term[...].astype(F32)
    for part in range(out.shape[0]):
        for k in range(out.shape[1]):
            out[part, k] = total[part, k : k + 1]


def total_volume(terms):
    parts, classes, width = terms[0].shape
    arrays, specs = in_vmem(terms)
    return pl.pallas_call(
        total_kernel,
        out_shape=jax.ShapeDtypeStruct((parts, classes, 1, width), F32),
        in_specs=specs,
        compiler_params=pltpu.CompilerParams(vmem_limit_bytes=VMEM_BYTES),
        name="total_volume",
    )(*arrays)


def local(dom, orient, cls, references, images, orient_lists, shift_ids, fixed_weights):
    classes, orients = references.shape[1], references.shape[2]
    table_x, table_y = (jnp.asarray(t) for t in trig_tables())

    def swap_dom(array, step):
        return lax.ppermute(array, "dom", xor_pairs(dom, step))

    def swap_orient(array, step):
        return lax.ppermute(array, "orient", xor_pairs(orient, step))

    bands, meta, shard = image_bands(
        orient_lists, shift_ids, fixed_weights, images, references, dom
    )
    arrived = {step: swap_dom(bands[step - 1], step) for step in [1, *range(dom - 1, 1, -1)]}
    tied, arrived[1] = lax.optimization_barrier((shard, arrived[1]))
    shards = [shard] + [
        swap_orient(tied if step == orient - 1 else shard, step) for step in range(1, orient)
    ]
    half = arrived[SHARED]
    groups = [([own_band(images, dom)], meta)]
    groups += [([arrived[step]], arrived[step]) for step in range(1, dom)]
    groups[SHARED] = ([half, lax.ppermute(half, "cls", xor_pairs(cls, 1))], half)

    width = images.shape[2] // dom
    aligned_near = aligned_rows(table_x, table_y, groups[:2], width)
    shards[1], aligned_near = lax.optimization_barrier((shards[1], aligned_near))
    every = range(orient)
    first, right = near_logits(table_x, table_y, shards, groups[:2], every[:EARLY], [], 0)
    near, right_late = near_logits(
        table_x, table_y, shards, groups[:2], every[EARLY:], first, 20
    )
    swapped = swap_dom(near[1], 1)
    right_late, swapped = lax.optimization_barrier((right_late, swapped))
    one_phase = dom == 4
    if one_phase:
        crossed = swap_dom(near[0], 2)
        crossed_over = swap_dom(near[1], 3)
    far = list(far_logits(table_x, [right, right_late], groups[2:], 6))
    if one_phase:
        far[1], crossed, crossed_over = lax.optimization_barrier((far[1], crossed, crossed_over))
        terms = [
            [near[0], swapped, swap_dom(far[0], 2), swap_dom(far[1], 3)],
            [far[0], swap_dom(far[1], 1), crossed, crossed_over],
        ]
    else:
        partial = [*near, *far]
        here = {s: partial[s] + swap_dom(partial[s ^ 1], 1) for s in range(2, dom, 2)}
        here[0] = near[0] + swapped
        step = 2
        while step < dom:
            there = {s: swap_dom(here[s ^ step], step) for s in here}
            step *= 2
            if step < dom:
                here = {s: here[s] + there[s] for s in here}
        terms = [[here[s], there[s]] for s in sorted(here)]
    aligned_far = aligned_rows(table_x, table_y, groups[2:], width)
    terms[0][-1], aligned_far = lax.optimization_barrier((terms[0][-1], aligned_far))
    stats = logit_stats(terms, classes, orients)

    stats = jnp.concatenate([stats, swap_dom(stats, 1)])
    stats_all = [stats, lax.ppermute(stats, "cls", xor_pairs(cls, 1))]
    prob, *terms = volume_terms(
        stats_all, groups, aligned_near, aligned_far, orients, classes
    )
    order = sorted(range(1, orients), key=lambda place: place != orients // 2)
    terms = [terms[0]] + [swap_orient(terms[o], o) for o in order]
    return prob[:, :classes], total_volume(terms)


def solution(mesh):
    in_specs = (
        P(None, "cls", None, ("dom", "orient")),
        P(None, ("dom", "orient"), None),
        P(("dom", "orient"), None),
        P(("dom", "orient"), None),
        P(("dom", "orient"), None),
    )
    out_specs = (P(("dom", "orient"), "cls"), P(None, "cls", "orient", "dom"))
    body = functools.partial(local, mesh.shape["dom"], mesh.shape["orient"], mesh.shape["cls"])
    return jax.shard_map(body, mesh=mesh, in_specs=in_specs, out_specs=out_specs, check_vma=False)
```

```python
import functools
import math

import jax
import jax.numpy as jnp
import numpy as np
from jax import lax
from jax.experimental import pallas as pl
from jax.experimental.pallas import tpu as pltpu
from jax.sharding import PartitionSpec as P

IMG = 256
TX = 8
TY = 8
HALF = TX // 2
LANES = 128
SUBLANES = 8
SHARED = 2
FLOPS_OF_MICRO = 1_000_000_000
VMEM_BYTES = 24 * 1024 * 1024
VMEM_SPEC = pl.BlockSpec(memory_space=pltpu.VMEM)
SMEM_SPEC = pl.BlockSpec(memory_space=pltpu.SMEM)
BF = jnp.bfloat16
F32 = jnp.float32


def trig_tables():
    steps = np.arange(1, HALF + 1)
    angle_x = 2.0 * math.pi / IMG * steps[:, None] * (np.arange(IMG) - IMG // 2)[None, :]
    angle_y = 2.0 * math.pi / IMG * np.arange(IMG // 2)[:, None] * steps[None, :]
    table_x = np.concatenate([np.cos(angle_x), np.sin(angle_x)], 0).astype(np.float32)
    table_y = np.concatenate([np.cos(angle_y), np.sin(angle_y)], 1).astype(np.float32)
    return table_x, table_y.reshape(-1)


def device_ids():
    return [lax.axis_index(name) for name in ("dom", "orient", "cls")]


def xor_pairs(size, step):
    return [(i, i ^ step) for i in range(size)]


def column_of(line):
    size = line.shape[1]
    rows = lax.broadcasted_iota(jnp.int32, (size, size), 0)
    cols = lax.broadcasted_iota(jnp.int32, (size, size), 1)
    return jnp.sum(jnp.where(rows == cols, line, 0.0), axis=1, keepdims=True)


def bands_kernel(steps, images, references, *rest):
    ids = device_ids()
    lists, rest = rest[:3], rest[3:]
    outs, meta, shard = rest[: len(steps)], rest[len(steps)], rest[len(steps) + 1]
    lines, sems, meta_sems, line_sems, shard_sem = rest[len(steps) + 2 :]
    copies = [pltpu.make_async_copy(references, shard, shard_sem)]
    for place, (step, out) in enumerate(zip(steps, outs)):
        width = out.shape[2] - LANES
        start = (ids[0] ^ step) * width
        if step == SHARED:
            start = 2 * start + ids[2] * width
        start = pl.multiple_of(start, width)
        for part in range(out.shape[0]):
            copies.append(
                pltpu.make_async_copy(
                    images.at[part, :, pl.ds(start, width)],
                    out.at[part, :, pl.ds(0, width)],
                    sems.at[place, part],
                )
            )
    line_copies = [
        pltpu.make_async_copy(source, lines[place], line_sems.at[place])
        for place, source in enumerate(lists)
    ]
    for copy in line_copies + copies:
        copy.start()
    for copy in line_copies:
        copy.wait()
    lane = lax.broadcasted_iota(jnp.int32, meta.shape[1:], 1)
    fixed = column_of(lines[2][...])
    high = fixed.astype(BF).astype(F32)
    middle = (fixed - high).astype(BF).astype(F32)
    values = [column_of(lines[0][...].astype(F32)), column_of(lines[1][...].astype(F32))]
    table = jnp.zeros(meta.shape[1:], F32)
    for place, value in enumerate(values + [high, middle, fixed - high - middle]):
        table = jnp.where(lane == place, value, table)
    meta[0] = table.astype(BF)
    meta[1] = jnp.zeros(meta.shape[1:], BF)
    meta_copies = [
        pltpu.make_async_copy(
            meta, out.at[:, :, pl.ds(out.shape[2] - LANES, LANES)], meta_sems.at[place]
        )
        for place, out in enumerate(outs)
    ]
    for copy in meta_copies:
        copy.start()
    for copy in copies + meta_copies:
        copy.wait()


def image_bands(orient_lists, shift_ids, fixed_weights, images, references, dom):
    parts, rows, pixels = images.shape
    width = pixels // dom
    steps = list(range(1, dom))
    sources = [images, references] + [
        array.reshape(1, rows) for array in (orient_lists, shift_ids, fixed_weights)
    ]
    sources = [pltpu.with_memory_space_constraint(array, pltpu.HBM) for array in sources]
    *bands, meta, shard = pl.pallas_call(
        functools.partial(bands_kernel, steps),
        out_shape=[
            pltpu.VMEM((parts, rows, width // (1 + (step == SHARED)) + LANES), images.dtype)
            for step in steps
        ]
        + [
            jax.ShapeDtypeStruct((parts, rows, LANES), BF),
            pltpu.VMEM(references.shape, references.dtype),
        ],
        in_specs=[pl.BlockSpec(memory_space=pl.ANY)] * len(sources),
        out_specs=[pl.BlockSpec(memory_space=pl.ANY)] * len(steps)
        + [pl.BlockSpec(memory_space=pltpu.VMEM), pl.BlockSpec(memory_space=pl.ANY)],
        scratch_shapes=[
            [pltpu.VMEM((1, rows), array.dtype) for array in sources[2:]],
            pltpu.SemaphoreType.DMA((len(steps), parts)),
            pltpu.SemaphoreType.DMA((len(steps),)),
            pltpu.SemaphoreType.DMA((3,)),
            pltpu.SemaphoreType.DMA,
        ],
        compiler_params=pltpu.CompilerParams(vmem_limit_bytes=VMEM_BYTES),
        cost_estimate=pl.CostEstimate(
            flops=0, bytes_accessed=4 * parts * rows * (pixels - width), transcendentals=0
        ),
        name="image_bands",
    )(*sources)
    return bands, meta, shard


def own_kernel(images, band, sems):
    ids = device_ids()
    width = band.shape[2]
    start = pl.multiple_of(ids[0] * width, width)
    copies = [
        pltpu.make_async_copy(images.at[part, :, pl.ds(start, width)], band.at[part], sems.at[part])
        for part in range(band.shape[0])
    ]
    for copy in copies:
        copy.start()
    for copy in copies:
        copy.wait()


def own_band(images, dom):
    parts, rows, pixels = images.shape
    shape = (parts, rows, pixels // dom)
    return pl.pallas_call(
        own_kernel,
        out_shape=pltpu.VMEM(shape, images.dtype),
        in_specs=[pl.BlockSpec(memory_space=pl.ANY)],
        out_specs=pl.BlockSpec(memory_space=pl.ANY),
        scratch_shapes=[pltpu.SemaphoreType.DMA((parts,))],
        compiler_params=pltpu.CompilerParams(vmem_limit_bytes=VMEM_BYTES),
        name="own_band",
    )(pltpu.with_memory_space_constraint(images, pltpu.HBM))


def in_vmem(arrays):
    placed = [pltpu.with_memory_space_constraint(array, pltpu.VMEM) for array in arrays]
    return placed, [VMEM_SPEC] * len(placed)


def flat(groups):
    return [image for images, _ in groups for image in images]


def sizes_of(groups):
    return [len(images) for images, _ in groups]


def by_group(sizes, refs):
    images, at = [], 0
    for size in sizes:
        images.append(refs[at : at + size])
        at += size
    return images, refs[at:]


def load(images, ids, part, start, size):
    if len(images) == 1:
        return images[0][part, :, pl.ds(pl.multiple_of(start, size), size)].astype(F32)
    half = images[0].shape[2] - LANES
    side = start // half
    cols = pl.ds(pl.multiple_of(start - side * half, size), size)
    mine, other = (image[part, :, cols].astype(F32) for image in images)
    return jnp.where(side == ids[2], mine, other)


def shift_references(refs, right, step, ids, orients, table_y):
    names = refs.shape[1]
    chunk = right.shape[2] // 2
    lines = chunk // IMG
    line_base = (ids[0] * orients + (ids[1] ^ step[1])) * lines
    for line in range(lines):
        to_re = slice(2 * line * IMG, (2 * line + 1) * IMG)
        to_im = slice((2 * line + 1) * IMG, (2 * line + 2) * IMG)
        base = (line_base + line) * TY
        cols = pl.ds(pl.multiple_of(step[0] * chunk + line * IMG, IMG), IMG)
        ref_re = refs[0, :, cols].astype(F32)
        ref_im = refs[1, :, cols].astype(F32)

        def put(b, re, im):
            right[step[0], b * names : (b + 1) * names, to_re] = re.astype(BF)
            right[step[0], b * names : (b + 1) * names, to_im] = im.astype(BF)

        put(TY // 2, ref_re, ref_im)
        for t in range(1, HALF + 1):
            cosine = table_y[base + t - 1]
            sine = table_y[base + HALF + t - 1]
            re_c, im_s = ref_re * cosine, ref_im * sine
            im_c, re_s = ref_im * cosine, ref_re * sine
            put(TY // 2 - t, re_c - im_s, im_c + re_s)
            if t < HALF:
                put(TY // 2 + t, re_c + im_s, im_c - re_s)


def shift_images(images, left, column, ids, table_x):
    chunk = left.shape[1] // 2
    rows = images[0][0].shape[1]
    for line in range(chunk // IMG):
        to_re = slice(2 * line * IMG, (2 * line + 1) * IMG)
        to_im = slice((2 * line + 1) * IMG, (2 * line + 2) * IMG)
        for g, group in enumerate(images):
            start = column * chunk + line * IMG
            re = load(group, ids, 0, start, IMG)
            im = load(group, ids, 1, start, IMG)

            def put(a, re, im):
                top = (g * TX + a) * rows
                left[top : top + rows, to_re] = re.astype(BF)
                left[top : top + rows, to_im] = im.astype(BF)

            put(TX // 2, re, im)
            for t in range(1, HALF + 1):
                cosine = table_x[t - 1 : t, :]
                sine = table_x[HALF + t - 1 : HALF + t, :]
                re_c, im_s = re * cosine, im * sine
                re_s, im_c = re * sine, im * cosine
                put(TX // 2 - t, re_c + im_s, im_c - re_s)
                if t < HALF:
                    put(TX // 2 + t, re_c - im_s, re_s + im_c)


def add_products(outs, left, right):
    rows = outs[0].shape[0]
    value = lax.dot_general(left, right, (((1,), (1,)), ((), ())), preferred_element_type=F32)
    for g, out in enumerate(outs):
        out[...] += value[g * rows : (g + 1) * rows]


def near_kernel(sizes, orients, steps, sums, table_y, table_x, *rest):
    ids = device_ids()
    groups, count = len(sizes), len(steps)
    shards, rest = rest[:count], rest[count:]
    images, rest = by_group(sizes, rest)
    before, rest = rest[: groups * sums], rest[groups * sums :]
    outs, (right, refs, left) = rest[:groups], rest[groups:]
    chunk = shards[0].shape[3]
    per_class = shards[0].shape[2]
    for place, shard in enumerate(shards):
        cols = slice(place * chunk, (place + 1) * chunk)
        for part in range(2):
            for k in range(shard.shape[1]):
                refs[part, k * per_class : (k + 1) * per_class, cols] = shard[part, k]
    for g, out in enumerate(outs):
        out[...] = before[g][...] if sums else jnp.zeros_like(out)

    def add_shard(place, carry):
        step = 2 * place + steps[0]
        shift_references(refs, right, (place, step), ids, orients, table_y)
        shift_images(images, left, ids[1] ^ step, ids, table_x)
        add_products(outs, left[...], right[place])
        return carry

    lax.fori_loop(0, count, add_shard, 0)


def far_kernel(sizes, counts, table_x, *rest):
    ids = device_ids()
    groups = len(sizes)
    rights, rest = rest[: len(counts)], rest[len(counts) :]
    images, rest = by_group(sizes, rest)
    outs, left = rest[:groups], rest[groups]
    for out in outs:
        out[...] = jnp.zeros_like(out)
    for first, (right, count) in enumerate(zip(rights, counts)):

        def add_shard(place, carry, first=first, right=right):
            shift_images(images, left, ids[1] ^ (2 * place + first), ids, table_x)
            add_products(outs, left[...], right[place])
            return carry

        lax.fori_loop(0, count, add_shard, 0)


def logits_cost(micros):
    return pl.CostEstimate(flops=micros * FLOPS_OF_MICRO, bytes_accessed=0, transcendentals=0)


def near_logits(table_x, table_y, shards, picked, steps, before, micros):
    parts, classes, orients, chunk = shards[0].shape
    groups = len(picked)
    rows = picked[0][0][0].shape[1]
    names = classes * orients
    count = len(steps)
    out_shape = (TX * rows, TY * names)
    used = [shards[step] for step in steps]
    arrays, specs = in_vmem([table_x, *used, *flat(picked), *before])
    *sums, right = pl.pallas_call(
        functools.partial(
            near_kernel, sizes_of(picked), len(shards), steps, len(before) > 0
        ),
        out_shape=[pltpu.VMEM(out_shape, F32)] * groups
        + [pltpu.VMEM((count, TY * names, 2 * chunk), BF)],
        in_specs=[SMEM_SPEC] + specs,
        out_specs=[VMEM_SPEC] * (groups + 1),
        scratch_shapes=[
            pltpu.VMEM((parts, names, count * chunk), BF),
            pltpu.VMEM((groups * TX * rows, 2 * chunk), BF),
        ],
        compiler_params=pltpu.CompilerParams(vmem_limit_bytes=VMEM_BYTES),
        cost_estimate=logits_cost(micros),
        name="near_logits",
    )(table_y, *arrays)
    return sums, right


def far_logits(table_x, rights, picked, micros):
    groups = len(picked)
    rows = picked[0][0][0].shape[1]
    names, chunk = rights[0].shape[1:]
    out_shape = (TX * rows, names)
    arrays, specs = in_vmem([table_x, *rights, *flat(picked)])
    return pl.pallas_call(
        functools.partial(far_kernel, sizes_of(picked), [right.shape[0] for right in rights]),
        out_shape=[pltpu.VMEM(out_shape, F32)] * groups,
        in_specs=specs,
        out_specs=[VMEM_SPEC] * groups,
        scratch_shapes=[pltpu.VMEM((groups * TX * rows, chunk), BF)],
        compiler_params=pltpu.CompilerParams(vmem_limit_bytes=VMEM_BYTES),
        cost_estimate=logits_cost(micros),
        name="far_logits",
    )(*arrays)


def stats_kernel(counts, classes, orients, *refs):
    *logits, out = refs
    rows, lanes = logits[0].shape[0] // TX, logits[0].shape[1]
    lane = lax.broadcasted_iota(jnp.int32, (rows, lanes), 1)
    class_of = (lane // orients) % classes
    out_lane = lax.broadcasted_iota(jnp.int32, (rows, LANES), 1)
    packed = jnp.zeros((SUBLANES, LANES), F32)
    for g, count in enumerate(counts):
        total = sum(ref[...] for ref in logits[:count])
        logits = logits[count:]
        pieces = [total[a * rows : (a + 1) * rows] for a in range(TX)]
        top = functools.reduce(jnp.maximum, pieces)
        top = jnp.max(top, axis=1, keepdims=True)
        sums = sum(jnp.exp(piece - top) for piece in pieces)
        line = jnp.where(out_lane == 0, top, 0.0)
        for k in range(classes):
            part = jnp.sum(jnp.where(class_of == k, sums, 0.0), axis=1, keepdims=True)
            line = jnp.where(out_lane == k + 1, part, line)
        for half in range(rows // SUBLANES):
            block = line[half * SUBLANES : (half + 1) * SUBLANES]
            place = (g * (rows // SUBLANES) + half) * SUBLANES
            packed = packed + pltpu.roll(block, place, 1)
    out[...] = packed


def logit_stats(terms, classes, orients):
    arrays, specs = in_vmem([array for held in terms for array in held])
    return pl.pallas_call(
        functools.partial(stats_kernel, [len(held) for held in terms], classes, orients),
        out_shape=pltpu.VMEM((SUBLANES, LANES), F32),
        in_specs=specs,
        out_specs=VMEM_SPEC,
        compiler_params=pltpu.CompilerParams(vmem_limit_bytes=VMEM_BYTES),
        name="logit_stats",
    )(*arrays)


def rows_kernel(sizes, table_y, table_x, *rest):
    ids = device_ids()
    groups = len(sizes)
    metas = rest[:groups]
    images, (out,) = by_group(sizes, rest[groups:])
    rows = metas[0].shape[1]
    width = out.shape[2]
    lines = width // IMG
    line_base = ids[0] * lines
    for g in range(groups):
        own = slice(g * rows, (g + 1) * rows)
        last = metas[g].shape[2] - LANES
        shift = metas[g][0, :, last:].astype(F32)[:, 1:2].astype(jnp.int32)
        move_x = jnp.broadcast_to(shift % TX - TX // 2, (rows, IMG))
        move_y = jnp.broadcast_to(shift // TX - TY // 2, (rows, LANES))
        phase_c = jnp.ones((rows, IMG), F32)
        phase_s = jnp.zeros((rows, IMG), F32)
        for t in range(1, HALF + 1):
            hit = jnp.abs(move_x) == t
            phase_c = jnp.where(hit, table_x[t - 1 : t, :], phase_c)
            phase_s = jnp.where(hit, table_x[HALF + t - 1 : HALF + t, :], phase_s)
        phase_s = jnp.where(move_x < 0, -phase_s, phase_s)
        hits = [jnp.abs(move_y) == t for t in range(1, HALF + 1)]
        sign = jnp.where(move_y < 0, -1.0, 1.0)

        def add_line(line, carry):
            base = (line_base + line) * TY
            cos_y = jnp.ones((rows, LANES), F32)
            sin_y = jnp.zeros((rows, LANES), F32)
            for t in range(1, HALF + 1):
                cos_y = jnp.where(hits[t - 1], table_y[base + t - 1], cos_y)
                sin_y = jnp.where(hits[t - 1], table_y[base + HALF + t - 1], sin_y)
            sin_y = sin_y * sign
            for part in range(IMG // LANES):
                across = slice(part * LANES, (part + 1) * LANES)
                start = pl.multiple_of(line * IMG + part * LANES, LANES)
                cols = pl.ds(start, LANES)
                cos_x, sin_x = phase_c[:, across], phase_s[:, across]
                cosine = cos_x * cos_y - sin_x * sin_y
                sine = sin_x * cos_y + cos_x * sin_y
                re = load(images[g], ids, 0, start, LANES)
                im = load(images[g], ids, 1, start, LANES)
                out[0, own, cols] = (re * cosine - im * sine).astype(BF)
                out[1, own, cols] = (re * sine + im * cosine).astype(BF)
            return carry

        lax.fori_loop(0, lines, add_line, 0, unroll=min(lines, 4))


def aligned_rows(table_x, table_y, picked, width):
    parts, rows = picked[0][0][0].shape[:2]
    groups = len(picked)
    arrays, specs = in_vmem([table_x] + [table for _, table in picked] + flat(picked))
    return pl.pallas_call(
        functools.partial(rows_kernel, sizes_of(picked)),
        out_shape=pltpu.VMEM((parts, groups * rows, width), BF),
        in_specs=[SMEM_SPEC] + specs,
        out_specs=VMEM_SPEC,
        compiler_params=pltpu.CompilerParams(vmem_limit_bytes=VMEM_BYTES),
        cost_estimate=pl.CostEstimate(
            flops=0,
            bytes_accessed=0,
            transcendentals=0,
        ),
        name="aligned_rows",
    )(table_y, *arrays)


def unpacked(packed, place, blocks):
    first = place * blocks * SUBLANES
    return jnp.concatenate(
        [pltpu.roll(packed, (LANES - first - i * SUBLANES) % LANES, 1) for i in range(blocks)]
    )


def volume_kernel(groups, orients, classes, *rest):
    ids = device_ids()
    stats, metas = rest[:2], rest[2 : 2 + groups]
    near, far = rest[2 + groups], rest[3 + groups]
    prob, outs = rest[4 + groups], rest[5 + groups :]
    rows = metas[0].shape[1]
    width = near.shape[2]
    chunk = min(width, 8 * IMG)
    lane = lax.broadcasted_iota(jnp.int32, (rows, LANES), 1)
    pieces = []
    for g in range(groups):
        top = g % 2 * SUBLANES
        mine, other = (
            unpacked(ref[top : top + SUBLANES, :], g // 2, rows // SUBLANES) for ref in stats
        )
        top = jnp.maximum(mine[:, 0:1], other[:, 0:1])
        mine_scale = jnp.exp(mine[:, 0:1] - top)
        other_scale = jnp.exp(other[:, 0:1] - top)
        held = (lane >= 1) & (lane <= classes)
        both = jnp.where(held, mine * mine_scale + other * other_scale, 0.0)
        totals = jnp.sum(both, axis=1, keepdims=True)
        spread = jnp.zeros((rows, LANES), F32)
        for k in range(classes):
            spread = jnp.where(lane % SUBLANES == k, mine[:, k + 1 : k + 2], spread)
        class_prob = spread * mine_scale / totals
        if g == 0:
            prob[...] = class_prob
        last = metas[g].shape[2] - LANES
        table = metas[g][0, :, last:].astype(F32)
        fixed = table[:, 2:3] + table[:, 3:4] + table[:, 4:5]
        weight = (fixed * class_prob).astype(BF).astype(F32)
        bin_of = table[:, 0:1].astype(jnp.int32) ^ ids[1]
        pieces.append(jnp.where(lane // SUBLANES == bin_of, weight, 0.0))
    mixes = []
    for held in (pieces[:2], pieces[2:]):
        mixing = jnp.transpose(jnp.concatenate(held, axis=0))
        mixes.append(mixing[: orients * SUBLANES].astype(BF))
    for part in range(2):
        for column in range(0, width, chunk):
            cols = slice(column, column + chunk)
            value = jnp.dot(mixes[0], near[part, :, cols], preferred_element_type=F32)
            value += jnp.dot(mixes[1], far[part, :, cols], preferred_element_type=F32)
            for o in range(orients):
                term = value[o * SUBLANES : o * SUBLANES + classes]
                outs[o][part, :, cols] = term.astype(outs[o].dtype)


def volume_terms(stats, groups, near, far, orients, classes):
    parts, entries, width = near.shape
    rest = far.shape[1]
    rows = groups[0][1].shape[1]
    out_shape = (parts, classes, width)
    arrays, specs = in_vmem([*stats, *(table for _, table in groups), near, far])
    return pl.pallas_call(
        functools.partial(volume_kernel, len(groups), orients, classes),
        out_shape=[pltpu.VMEM((rows, LANES), F32)]
        + [pltpu.VMEM(out_shape, F32 if o == 0 else BF) for o in range(orients)],
        in_specs=specs,
        out_specs=[VMEM_SPEC] * (1 + orients),
        compiler_params=pltpu.CompilerParams(vmem_limit_bytes=VMEM_BYTES),
        cost_estimate=pl.CostEstimate(
            flops=4 * orients * classes * (entries + rest) * width,
            bytes_accessed=4 * (entries + rest) * width + 4 * orients * classes * width,
            transcendentals=0,
        ),
        name="volume_terms",
    )(*arrays)


def total_kernel(first, *rest):
    out = rest[-1]
    total = first[...]
    for term in rest[:-1]:
        total = total + term[...].astype(F32)
    for part in range(out.shape[0]):
        for k in range(out.shape[1]):
            out[part, k] = total[part, k : k + 1]


def total_volume(terms):
    parts, classes, width = terms[0].shape
    arrays, specs = in_vmem(terms)
    return pl.pallas_call(
        total_kernel,
        out_shape=jax.ShapeDtypeStruct((parts, classes, 1, width), F32),
        in_specs=specs,
        compiler_params=pltpu.CompilerParams(vmem_limit_bytes=VMEM_BYTES),
        name="total_volume",
    )(*arrays)


def local(dom, orient, cls, references, images, orient_lists, shift_ids, fixed_weights):
    classes, orients = references.shape[1], references.shape[2]
    table_x, table_y = (jnp.asarray(t) for t in trig_tables())

    def swap_dom(array, step):
        return lax.ppermute(array, "dom", xor_pairs(dom, step))

    def swap_orient(array, step):
        return lax.ppermute(array, "orient", xor_pairs(orient, step))

    bands, meta, shard = image_bands(
        orient_lists, shift_ids, fixed_weights, images, references, dom
    )
    arrived = {step: swap_dom(bands[step - 1], step) for step in [1, *range(dom - 1, 1, -1)]}
    tied, arrived[1] = lax.optimization_barrier((shard, arrived[1]))
    shards = [shard] + [None] * (orient - 1)
    for step in [*range(2, orient, 2), *range(1, orient, 2)]:
        shards[step] = swap_orient(tied if step == orient - 1 else shard, step)
    half = arrived[SHARED]
    groups = [([own_band(images, dom)], meta)]
    groups += [([arrived[step]], arrived[step]) for step in range(1, dom)]
    groups[SHARED] = ([half, lax.ppermute(half, "cls", xor_pairs(cls, 1))], half)

    width = images.shape[2] // dom
    aligned_near = aligned_rows(table_x, table_y, groups[:2], width)
    shards[2], aligned_near = lax.optimization_barrier((shards[2], aligned_near))
    every = range(orient)
    first, right = near_logits(table_x, table_y, shards, groups[:2], every[0::2], [], 0)
    near, right_late = near_logits(
        table_x, table_y, shards, groups[:2], every[1::2], first, 20
    )
    swapped = swap_dom(near[1], 1)
    right_late, swapped = lax.optimization_barrier((right_late, swapped))
    one_phase = dom == 4
    if one_phase:
        crossed = swap_dom(near[0], 2)
        crossed_over = swap_dom(near[1], 3)
    far = list(far_logits(table_x, [right, right_late], groups[2:], 6))
    if one_phase:
        far[1], crossed, crossed_over = lax.optimization_barrier((far[1], crossed, crossed_over))
        terms = [
            [near[0], swapped, swap_dom(far[0], 2), swap_dom(far[1], 3)],
            [far[0], swap_dom(far[1], 1), crossed, crossed_over],
        ]
    else:
        partial = [*near, *far]
        here = {s: partial[s] + swap_dom(partial[s ^ 1], 1) for s in range(2, dom, 2)}
        here[0] = near[0] + swapped
        step = 2
        while step < dom:
            there = {s: swap_dom(here[s ^ step], step) for s in here}
            step *= 2
            if step < dom:
                here = {s: here[s] + there[s] for s in here}
        terms = [[here[s], there[s]] for s in sorted(here)]
    aligned_far = aligned_rows(table_x, table_y, groups[2:], width)
    terms[0][-1], aligned_far = lax.optimization_barrier((terms[0][-1], aligned_far))
    stats = logit_stats(terms, classes, orients)

    stats = jnp.concatenate([stats, swap_dom(stats, 1)])
    stats_all = [stats, lax.ppermute(stats, "cls", xor_pairs(cls, 1))]
    prob, *terms = volume_terms(
        stats_all, groups, aligned_near, aligned_far, orients, classes
    )
    order = sorted(range(1, orients), key=lambda place: place != orients // 2)
    terms = [terms[0]] + [swap_orient(terms[o], o) for o in order]
    return prob[:, :classes], total_volume(terms)


def solution(mesh):
    in_specs = (
        P(None, "cls", None, ("dom", "orient")),
        P(None, ("dom", "orient"), None),
        P(("dom", "orient"), None),
        P(("dom", "orient"), None),
        P(("dom", "orient"), None),
    )
    out_specs = (P(("dom", "orient"), "cls"), P(None, "cls", "orient", "dom"))
    body = functools.partial(local, mesh.shape["dom"], mesh.shape["orient"], mesh.shape["cls"])
    return jax.shard_map(body, mesh=mesh, in_specs=in_specs, out_specs=out_specs, check_vma=False)
```

```python
import functools
import math

import jax
import jax.numpy as jnp
import numpy as np
from jax import lax
from jax.experimental import pallas as pl
from jax.experimental.pallas import tpu as pltpu
from jax.sharding import PartitionSpec as P

IMG = 256
TX = 8
TY = 8
HALF = TX // 2
LANES = 128
SUBLANES = 8
SHARED = 2
FLOPS_OF_MICRO = 1_000_000_000
VMEM_BYTES = 24 * 1024 * 1024
VMEM_SPEC = pl.BlockSpec(memory_space=pltpu.VMEM)
SMEM_SPEC = pl.BlockSpec(memory_space=pltpu.SMEM)
BF = jnp.bfloat16
F32 = jnp.float32


def trig_tables():
    steps = np.arange(1, HALF + 1)
    angle_x = 2.0 * math.pi / IMG * steps[:, None] * (np.arange(IMG) - IMG // 2)[None, :]
    angle_y = 2.0 * math.pi / IMG * np.arange(IMG // 2)[:, None] * steps[None, :]
    table_x = np.concatenate([np.cos(angle_x), np.sin(angle_x)], 0).astype(np.float32)
    table_y = np.concatenate([np.cos(angle_y), np.sin(angle_y)], 1).astype(np.float32)
    return table_x, table_y.reshape(-1)


def device_ids():
    return [lax.axis_index(name) for name in ("dom", "orient", "cls")]


def xor_pairs(size, step):
    return [(i, i ^ step) for i in range(size)]


def column_of(line):
    size = line.shape[1]
    rows = lax.broadcasted_iota(jnp.int32, (size, size), 0)
    cols = lax.broadcasted_iota(jnp.int32, (size, size), 1)
    return jnp.sum(jnp.where(rows == cols, line, 0.0), axis=1, keepdims=True)


def bands_kernel(steps, images, references, *rest):
    ids = device_ids()
    lists, rest = rest[:3], rest[3:]
    outs, meta, shard = rest[: len(steps)], rest[len(steps)], rest[len(steps) + 1]
    lines, sems, meta_sems, line_sems, shard_sem = rest[len(steps) + 2 :]
    copies = [pltpu.make_async_copy(references, shard, shard_sem)]
    for place, (step, out) in enumerate(zip(steps, outs)):
        width = out.shape[2] - LANES
        start = (ids[0] ^ step) * width
        if step == SHARED:
            start = 2 * start + ids[2] * width
        start = pl.multiple_of(start, width)
        for part in range(out.shape[0]):
            copies.append(
                pltpu.make_async_copy(
                    images.at[part, :, pl.ds(start, width)],
                    out.at[part, :, pl.ds(0, width)],
                    sems.at[place, part],
                )
            )
    line_copies = [
        pltpu.make_async_copy(source, lines[place], line_sems.at[place])
        for place, source in enumerate(lists)
    ]
    for copy in line_copies + copies:
        copy.start()
    for copy in line_copies:
        copy.wait()
    lane = lax.broadcasted_iota(jnp.int32, meta.shape[1:], 1)
    fixed = column_of(lines[2][...])
    high = fixed.astype(BF).astype(F32)
    middle = (fixed - high).astype(BF).astype(F32)
    values = [column_of(lines[0][...].astype(F32)), column_of(lines[1][...].astype(F32))]
    table = jnp.zeros(meta.shape[1:], F32)
    for place, value in enumerate(values + [high, middle, fixed - high - middle]):
        table = jnp.where(lane == place, value, table)
    meta[0] = table.astype(BF)
    meta[1] = jnp.zeros(meta.shape[1:], BF)
    meta_copies = [
        pltpu.make_async_copy(
            meta, out.at[:, :, pl.ds(out.shape[2] - LANES, LANES)], meta_sems.at[place]
        )
        for place, out in enumerate(outs)
    ]
    for copy in meta_copies:
        copy.start()
    for copy in copies + meta_copies:
        copy.wait()


def image_bands(orient_lists, shift_ids, fixed_weights, images, references, dom):
    parts, rows, pixels = images.shape
    width = pixels // dom
    steps = list(range(1, dom))
    sources = [images, references] + [
        array.reshape(1, rows) for array in (orient_lists, shift_ids, fixed_weights)
    ]
    sources = [pltpu.with_memory_space_constraint(array, pltpu.HBM) for array in sources]
    *bands, meta, shard = pl.pallas_call(
        functools.partial(bands_kernel, steps),
        out_shape=[
            pltpu.VMEM((parts, rows, width // (1 + (step == SHARED)) + LANES), images.dtype)
            for step in steps
        ]
        + [
            jax.ShapeDtypeStruct((parts, rows, LANES), BF),
            pltpu.VMEM(references.shape, references.dtype),
        ],
        in_specs=[pl.BlockSpec(memory_space=pl.ANY)] * len(sources),
        out_specs=[pl.BlockSpec(memory_space=pl.ANY)] * len(steps)
        + [pl.BlockSpec(memory_space=pltpu.VMEM), pl.BlockSpec(memory_space=pl.ANY)],
        scratch_shapes=[
            [pltpu.VMEM((1, rows), array.dtype) for array in sources[2:]],
            pltpu.SemaphoreType.DMA((len(steps), parts)),
            pltpu.SemaphoreType.DMA((len(steps),)),
            pltpu.SemaphoreType.DMA((3,)),
            pltpu.SemaphoreType.DMA,
        ],
        compiler_params=pltpu.CompilerParams(vmem_limit_bytes=VMEM_BYTES),
        cost_estimate=pl.CostEstimate(
            flops=0, bytes_accessed=4 * parts * rows * (pixels - width), transcendentals=0
        ),
        name="image_bands",
    )(*sources)
    return bands, meta, shard


def own_kernel(images, band, sems):
    ids = device_ids()
    width = band.shape[2]
    start = pl.multiple_of(ids[0] * width, width)
    copies = [
        pltpu.make_async_copy(images.at[part, :, pl.ds(start, width)], band.at[part], sems.at[part])
        for part in range(band.shape[0])
    ]
    for copy in copies:
        copy.start()
    for copy in copies:
        copy.wait()


def own_band(images, dom):
    parts, rows, pixels = images.shape
    shape = (parts, rows, pixels // dom)
    return pl.pallas_call(
        own_kernel,
        out_shape=pltpu.VMEM(shape, images.dtype),
        in_specs=[pl.BlockSpec(memory_space=pl.ANY)],
        out_specs=pl.BlockSpec(memory_space=pl.ANY),
        scratch_shapes=[pltpu.SemaphoreType.DMA((parts,))],
        compiler_params=pltpu.CompilerParams(vmem_limit_bytes=VMEM_BYTES),
        name="own_band",
    )(pltpu.with_memory_space_constraint(images, pltpu.HBM))


def in_vmem(arrays):
    placed = [pltpu.with_memory_space_constraint(array, pltpu.VMEM) for array in arrays]
    return placed, [VMEM_SPEC] * len(placed)


def flat(groups):
    return [image for images, _ in groups for image in images]


def sizes_of(groups):
    return [len(images) for images, _ in groups]


def by_group(sizes, refs):
    images, at = [], 0
    for size in sizes:
        images.append(refs[at : at + size])
        at += size
    return images, refs[at:]


def load(images, ids, part, start, size):
    if len(images) == 1:
        return images[0][part, :, pl.ds(pl.multiple_of(start, size), size)].astype(F32)
    half = images[0].shape[2] - LANES
    side = start // half
    cols = pl.ds(pl.multiple_of(start - side * half, size), size)
    mine, other = (image[part, :, cols].astype(F32) for image in images)
    return jnp.where(side == ids[2], mine, other)


def shift_references(refs, right, step, ids, orients, table_y):
    names = refs.shape[1]
    chunk = right.shape[2] // 2
    lines = chunk // IMG
    line_base = (ids[0] * orients + (ids[1] ^ step[1])) * lines
    for line in range(lines):
        to_re = slice(2 * line * IMG, (2 * line + 1) * IMG)
        to_im = slice((2 * line + 1) * IMG, (2 * line + 2) * IMG)
        base = (line_base + line) * TY
        cols = slice(step[0] * chunk + line * IMG, step[0] * chunk + (line + 1) * IMG)
        ref_re = refs[0, :, cols].astype(F32)
        ref_im = refs[1, :, cols].astype(F32)

        def put(b, re, im):
            right[step[0], b * names : (b + 1) * names, to_re] = re.astype(BF)
            right[step[0], b * names : (b + 1) * names, to_im] = im.astype(BF)

        put(TY // 2, ref_re, ref_im)
        for t in range(1, HALF + 1):
            cosine = table_y[base + t - 1]
            sine = table_y[base + HALF + t - 1]
            re_c, im_s = ref_re * cosine, ref_im * sine
            im_c, re_s = ref_im * cosine, ref_re * sine
            put(TY // 2 - t, re_c - im_s, im_c + re_s)
            if t < HALF:
                put(TY // 2 + t, re_c + im_s, im_c - re_s)


def shift_images(images, left, column, ids, table_x):
    chunk = left.shape[1] // 2
    rows = images[0][0].shape[1]
    for line in range(chunk // IMG):
        to_re = slice(2 * line * IMG, (2 * line + 1) * IMG)
        to_im = slice((2 * line + 1) * IMG, (2 * line + 2) * IMG)
        for g, group in enumerate(images):
            start = column * chunk + line * IMG
            re = load(group, ids, 0, start, IMG)
            im = load(group, ids, 1, start, IMG)

            def put(a, re, im):
                top = (g * TX + a) * rows
                left[top : top + rows, to_re] = re.astype(BF)
                left[top : top + rows, to_im] = im.astype(BF)

            put(TX // 2, re, im)
            for t in range(1, HALF + 1):
                cosine = table_x[t - 1 : t, :]
                sine = table_x[HALF + t - 1 : HALF + t, :]
                re_c, im_s = re * cosine, im * sine
                re_s, im_c = re * sine, im * cosine
                put(TX // 2 - t, re_c + im_s, im_c - re_s)
                if t < HALF:
                    put(TX // 2 + t, re_c - im_s, re_s + im_c)


def add_products(outs, left, right):
    rows = outs[0].shape[0]
    value = lax.dot_general(left, right, (((1,), (1,)), ((), ())), preferred_element_type=F32)
    for g, out in enumerate(outs):
        out[...] += value[g * rows : (g + 1) * rows]


def near_kernel(sizes, orients, steps, sums, table_y, table_x, *rest):
    ids = device_ids()
    groups, count = len(sizes), len(steps)
    shards, rest = rest[:count], rest[count:]
    images, rest = by_group(sizes, rest)
    before, rest = rest[: groups * sums], rest[groups * sums :]
    outs, (right, refs, *lefts) = rest[:groups], rest[groups:]
    chunk = shards[0].shape[3]
    per_class = shards[0].shape[2]
    for place, shard in enumerate(shards):
        cols = slice(place * chunk, (place + 1) * chunk)
        for part in range(2):
            for k in range(shard.shape[1]):
                refs[part, k * per_class : (k + 1) * per_class, cols] = shard[part, k]
    for g, out in enumerate(outs):
        out[...] = before[g][...] if sums else jnp.zeros_like(out)

    for place in range(count):
        step = 2 * place + steps[0]
        left = lefts[place % 2]
        shift_references(refs, right, (place, step), ids, orients, table_y)
        shift_images(images, left, ids[1] ^ step, ids, table_x)
        add_products(outs, left[...], right[place])


def far_kernel(sizes, counts, table_x, *rest):
    ids = device_ids()
    groups = len(sizes)
    rights, rest = rest[: len(counts)], rest[len(counts) :]
    images, rest = by_group(sizes, rest)
    outs, lefts = rest[:groups], rest[groups:]
    for out in outs:
        out[...] = jnp.zeros_like(out)
    turn = 0
    for first, (right, count) in enumerate(zip(rights, counts)):
        for place in range(count):
            left = lefts[turn % 2]
            shift_images(images, left, ids[1] ^ (2 * place + first), ids, table_x)
            add_products(outs, left[...], right[place])
            turn += 1


def logits_cost(micros):
    return pl.CostEstimate(flops=micros * FLOPS_OF_MICRO, bytes_accessed=0, transcendentals=0)


def near_logits(table_x, table_y, shards, picked, steps, before, micros):
    parts, classes, orients, chunk = shards[0].shape
    groups = len(picked)
    rows = picked[0][0][0].shape[1]
    names = classes * orients
    count = len(steps)
    out_shape = (TX * rows, TY * names)
    used = [shards[step] for step in steps]
    arrays, specs = in_vmem([table_x, *used, *flat(picked), *before])
    *sums, right = pl.pallas_call(
        functools.partial(
            near_kernel, sizes_of(picked), len(shards), steps, len(before) > 0
        ),
        out_shape=[pltpu.VMEM(out_shape, F32)] * groups
        + [pltpu.VMEM((count, TY * names, 2 * chunk), BF)],
        in_specs=[SMEM_SPEC] + specs,
        out_specs=[VMEM_SPEC] * (groups + 1),
        scratch_shapes=[
            pltpu.VMEM((parts, names, count * chunk), BF),
            pltpu.VMEM((groups * TX * rows, 2 * chunk), BF),
            pltpu.VMEM((groups * TX * rows, 2 * chunk), BF),
        ],
        compiler_params=pltpu.CompilerParams(vmem_limit_bytes=VMEM_BYTES),
        cost_estimate=logits_cost(micros),
        name="near_logits",
    )(table_y, *arrays)
    return sums, right


def far_logits(table_x, rights, picked, micros):
    groups = len(picked)
    rows = picked[0][0][0].shape[1]
    names, chunk = rights[0].shape[1:]
    out_shape = (TX * rows, names)
    arrays, specs = in_vmem([table_x, *rights, *flat(picked)])
    return pl.pallas_call(
        functools.partial(far_kernel, sizes_of(picked), [right.shape[0] for right in rights]),
        out_shape=[pltpu.VMEM(out_shape, F32)] * groups,
        in_specs=specs,
        out_specs=[VMEM_SPEC] * groups,
        scratch_shapes=[pltpu.VMEM((groups * TX * rows, chunk), BF)] * 2,
        compiler_params=pltpu.CompilerParams(vmem_limit_bytes=VMEM_BYTES),
        cost_estimate=logits_cost(micros),
        name="far_logits",
    )(*arrays)


def stats_kernel(counts, classes, orients, *refs):
    *logits, out = refs
    rows, lanes = logits[0].shape[0] // TX, logits[0].shape[1]
    lane = lax.broadcasted_iota(jnp.int32, (rows, lanes), 1)
    class_of = (lane // orients) % classes
    out_lane = lax.broadcasted_iota(jnp.int32, (rows, LANES), 1)
    packed = jnp.zeros((SUBLANES, LANES), F32)
    for g, count in enumerate(counts):
        total = sum(ref[...] for ref in logits[:count])
        logits = logits[count:]
        pieces = [total[a * rows : (a + 1) * rows] for a in range(TX)]
        top = functools.reduce(jnp.maximum, pieces)
        top = jnp.max(top, axis=1, keepdims=True)
        sums = sum(jnp.exp(piece - top) for piece in pieces)
        line = jnp.where(out_lane == 0, top, 0.0)
        for k in range(classes):
            part = jnp.sum(jnp.where(class_of == k, sums, 0.0), axis=1, keepdims=True)
            line = jnp.where(out_lane == k + 1, part, line)
        for half in range(rows // SUBLANES):
            block = line[half * SUBLANES : (half + 1) * SUBLANES]
            place = (g * (rows // SUBLANES) + half) * SUBLANES
            packed = packed + pltpu.roll(block, place, 1)
    out[...] = packed


def logit_stats(terms, classes, orients):
    arrays, specs = in_vmem([array for held in terms for array in held])
    return pl.pallas_call(
        functools.partial(stats_kernel, [len(held) for held in terms], classes, orients),
        out_shape=pltpu.VMEM((SUBLANES, LANES), F32),
        in_specs=specs,
        out_specs=VMEM_SPEC,
        compiler_params=pltpu.CompilerParams(vmem_limit_bytes=VMEM_BYTES),
        name="logit_stats",
    )(*arrays)


def rows_kernel(sizes, table_y, table_x, *rest):
    ids = device_ids()
    groups = len(sizes)
    metas = rest[:groups]
    images, (out,) = by_group(sizes, rest[groups:])
    rows = metas[0].shape[1]
    width = out.shape[2]
    lines = width // IMG
    line_base = ids[0] * lines
    for g in range(groups):
        own = slice(g * rows, (g + 1) * rows)
        last = metas[g].shape[2] - LANES
        shift = metas[g][0, :, last:].astype(F32)[:, 1:2].astype(jnp.int32)
        move_x = jnp.broadcast_to(shift % TX - TX // 2, (rows, IMG))
        move_y = jnp.broadcast_to(shift // TX - TY // 2, (rows, LANES))
        phase_c = jnp.ones((rows, IMG), F32)
        phase_s = jnp.zeros((rows, IMG), F32)
        for t in range(1, HALF + 1):
            hit = jnp.abs(move_x) == t
            phase_c = jnp.where(hit, table_x[t - 1 : t, :], phase_c)
            phase_s = jnp.where(hit, table_x[HALF + t - 1 : HALF + t, :], phase_s)
        phase_s = jnp.where(move_x < 0, -phase_s, phase_s)
        hits = [jnp.abs(move_y) == t for t in range(1, HALF + 1)]
        sign = jnp.where(move_y < 0, -1.0, 1.0)

        def add_line(line, carry):
            base = (line_base + line) * TY
            cos_y = jnp.ones((rows, LANES), F32)
            sin_y = jnp.zeros((rows, LANES), F32)
            for t in range(1, HALF + 1):
                cos_y = jnp.where(hits[t - 1], table_y[base + t - 1], cos_y)
                sin_y = jnp.where(hits[t - 1], table_y[base + HALF + t - 1], sin_y)
            sin_y = sin_y * sign
            for part in range(IMG // LANES):
                across = slice(part * LANES, (part + 1) * LANES)
                start = pl.multiple_of(line * IMG + part * LANES, LANES)
                cols = pl.ds(start, LANES)
                cos_x, sin_x = phase_c[:, across], phase_s[:, across]
                cosine = cos_x * cos_y - sin_x * sin_y
                sine = sin_x * cos_y + cos_x * sin_y
                re = load(images[g], ids, 0, start, LANES)
                im = load(images[g], ids, 1, start, LANES)
                out[0, own, cols] = (re * cosine - im * sine).astype(BF)
                out[1, own, cols] = (re * sine + im * cosine).astype(BF)
            return carry

        lax.fori_loop(0, lines, add_line, 0, unroll=min(lines, 4))


def aligned_rows(table_x, table_y, picked, width):
    parts, rows = picked[0][0][0].shape[:2]
    groups = len(picked)
    arrays, specs = in_vmem([table_x] + [table for _, table in picked] + flat(picked))
    return pl.pallas_call(
        functools.partial(rows_kernel, sizes_of(picked)),
        out_shape=pltpu.VMEM((parts, groups * rows, width), BF),
        in_specs=[SMEM_SPEC] + specs,
        out_specs=VMEM_SPEC,
        compiler_params=pltpu.CompilerParams(vmem_limit_bytes=VMEM_BYTES),
        cost_estimate=pl.CostEstimate(
            flops=0,
            bytes_accessed=0,
            transcendentals=0,
        ),
        name="aligned_rows",
    )(table_y, *arrays)


def unpacked(packed, place, blocks):
    first = place * blocks * SUBLANES
    return jnp.concatenate(
        [pltpu.roll(packed, (LANES - first - i * SUBLANES) % LANES, 1) for i in range(blocks)]
    )


def volume_kernel(groups, orients, classes, *rest):
    ids = device_ids()
    stats, metas = rest[:2], rest[2 : 2 + groups]
    near, far = rest[2 + groups], rest[3 + groups]
    prob, outs = rest[4 + groups], rest[5 + groups :]
    rows = metas[0].shape[1]
    width = near.shape[2]
    chunk = min(width, 8 * IMG)
    lane = lax.broadcasted_iota(jnp.int32, (rows, LANES), 1)
    pieces = []
    for g in range(groups):
        top = g % 2 * SUBLANES
        mine, other = (
            unpacked(ref[top : top + SUBLANES, :], g // 2, rows // SUBLANES) for ref in stats
        )
        top = jnp.maximum(mine[:, 0:1], other[:, 0:1])
        mine_scale = jnp.exp(mine[:, 0:1] - top)
        other_scale = jnp.exp(other[:, 0:1] - top)
        held = (lane >= 1) & (lane <= classes)
        both = jnp.where(held, mine * mine_scale + other * other_scale, 0.0)
        totals = jnp.sum(both, axis=1, keepdims=True)
        spread = jnp.zeros((rows, LANES), F32)
        for k in range(classes):
            spread = jnp.where(lane % SUBLANES == k, mine[:, k + 1 : k + 2], spread)
        class_prob = spread * mine_scale / totals
        if g == 0:
            prob[...] = class_prob
        last = metas[g].shape[2] - LANES
        table = metas[g][0, :, last:].astype(F32)
        fixed = table[:, 2:3] + table[:, 3:4] + table[:, 4:5]
        weight = (fixed * class_prob).astype(BF).astype(F32)
        bin_of = table[:, 0:1].astype(jnp.int32) ^ ids[1]
        pieces.append(jnp.where(lane // SUBLANES == bin_of, weight, 0.0))
    mixes = []
    for held in (pieces[:2], pieces[2:]):
        mixing = jnp.transpose(jnp.concatenate(held, axis=0))
        mixes.append(mixing[: orients * SUBLANES].astype(BF))
    for part in range(2):
        for column in range(0, width, chunk):
            cols = slice(column, column + chunk)
            value = jnp.dot(mixes[0], near[part, :, cols], preferred_element_type=F32)
            value += jnp.dot(mixes[1], far[part, :, cols], preferred_element_type=F32)
            for o in range(orients):
                term = value[o * SUBLANES : o * SUBLANES + classes]
                outs[o][part, :, cols] = term.astype(outs[o].dtype)


def volume_terms(stats, groups, near, far, orients, classes):
    parts, entries, width = near.shape
    rest = far.shape[1]
    rows = groups[0][1].shape[1]
    out_shape = (parts, classes, width)
    arrays, specs = in_vmem([*stats, *(table for _, table in groups), near, far])
    return pl.pallas_call(
        functools.partial(volume_kernel, len(groups), orients, classes),
        out_shape=[pltpu.VMEM((rows, LANES), F32)]
        + [pltpu.VMEM(out_shape, F32 if o == 0 else BF) for o in range(orients)],
        in_specs=specs,
        out_specs=[VMEM_SPEC] * (1 + orients),
        compiler_params=pltpu.CompilerParams(vmem_limit_bytes=VMEM_BYTES),
        cost_estimate=pl.CostEstimate(
            flops=4 * orients * classes * (entries + rest) * width,
            bytes_accessed=4 * (entries + rest) * width + 4 * orients * classes * width,
            transcendentals=0,
        ),
        name="volume_terms",
    )(*arrays)


def total_kernel(first, *rest):
    out = rest[-1]
    total = first[...]
    for term in rest[:-1]:
        total = total + term[...].astype(F32)
    for part in range(out.shape[0]):
        for k in range(out.shape[1]):
            out[part, k] = total[part, k : k + 1]


def total_volume(terms):
    parts, classes, width = terms[0].shape
    arrays, specs = in_vmem(terms)
    return pl.pallas_call(
        total_kernel,
        out_shape=jax.ShapeDtypeStruct((parts, classes, 1, width), F32),
        in_specs=specs,
        compiler_params=pltpu.CompilerParams(vmem_limit_bytes=VMEM_BYTES),
        name="total_volume",
    )(*arrays)


def local(dom, orient, cls, references, images, orient_lists, shift_ids, fixed_weights):
    classes, orients = references.shape[1], references.shape[2]
    table_x, table_y = (jnp.asarray(t) for t in trig_tables())

    def swap_dom(array, step):
        return lax.ppermute(array, "dom", xor_pairs(dom, step))

    def swap_orient(array, step):
        return lax.ppermute(array, "orient", xor_pairs(orient, step))

    bands, meta, shard = image_bands(
        orient_lists, shift_ids, fixed_weights, images, references, dom
    )
    arrived = {step: swap_dom(bands[step - 1], step) for step in [1, *range(dom - 1, 1, -1)]}
    tied, arrived[1] = lax.optimization_barrier((shard, arrived[1]))
    shards = [shard] + [None] * (orient - 1)
    for step in [*range(2, orient, 2), *range(1, orient, 2)]:
        shards[step] = swap_orient(tied if step == orient - 1 else shard, step)
    half = arrived[SHARED]
    groups = [([own_band(images, dom)], meta)]
    groups += [([arrived[step]], arrived[step]) for step in range(1, dom)]
    groups[SHARED] = ([half, lax.ppermute(half, "cls", xor_pairs(cls, 1))], half)

    width = images.shape[2] // dom
    aligned_near = aligned_rows(table_x, table_y, groups[:2], width)
    shards[2], aligned_near = lax.optimization_barrier((shards[2], aligned_near))
    every = range(orient)
    first, right = near_logits(table_x, table_y, shards, groups[:2], every[0::2], [], 0)
    near, right_late = near_logits(
        table_x, table_y, shards, groups[:2], every[1::2], first, 20
    )
    swapped = swap_dom(near[1], 1)
    right_late, swapped = lax.optimization_barrier((right_late, swapped))
    one_phase = dom == 4
    if one_phase:
        crossed = swap_dom(near[0], 2)
        crossed_over = swap_dom(near[1], 3)
    far = list(far_logits(table_x, [right, right_late], groups[2:], 6))
    if one_phase:
        far[1], crossed = lax.optimization_barrier((far[1], crossed))
        terms = [
            [near[0], swapped, swap_dom(far[0], 2), swap_dom(far[1], 3)],
            [far[0], swap_dom(far[1], 1), crossed, crossed_over],
        ]
    else:
        partial = [*near, *far]
        here = {s: partial[s] + swap_dom(partial[s ^ 1], 1) for s in range(2, dom, 2)}
        here[0] = near[0] + swapped
        step = 2
        while step < dom:
            there = {s: swap_dom(here[s ^ step], step) for s in here}
            step *= 2
            if step < dom:
                here = {s: here[s] + there[s] for s in here}
        terms = [[here[s], there[s]] for s in sorted(here)]
    if one_phase:
        groups[2][0][0], terms[1][3] = lax.optimization_barrier((groups[2][0][0], terms[1][3]))
    aligned_far = aligned_rows(table_x, table_y, groups[2:], width)
    terms[0][-1], aligned_far = lax.optimization_barrier((terms[0][-1], aligned_far))
    stats = logit_stats(terms, classes, orients)

    stats = jnp.concatenate([stats, swap_dom(stats, 1)])
    stats_all = [stats, lax.ppermute(stats, "cls", xor_pairs(cls, 1))]
    prob, *terms = volume_terms(
        stats_all, groups, aligned_near, aligned_far, orients, classes
    )
    order = sorted(range(1, orients), key=lambda place: place != orients // 2)
    terms = [terms[0]] + [swap_orient(terms[o], o) for o in order]
    return prob[:, :classes], total_volume(terms)


def solution(mesh):
    in_specs = (
        P(None, "cls", None, ("dom", "orient")),
        P(None, ("dom", "orient"), None),
        P(("dom", "orient"), None),
        P(("dom", "orient"), None),
        P(("dom", "orient"), None),
    )
    out_specs = (P(("dom", "orient"), "cls"), P(None, "cls", "orient", "dom"))
    body = functools.partial(local, mesh.shape["dom"], mesh.shape["orient"], mesh.shape["cls"])
    return jax.shard_map(body, mesh=mesh, in_specs=in_specs, out_specs=out_specs, check_vma=False)
```

```python
import functools
import math

import jax
import jax.numpy as jnp
import numpy as np
from jax import lax
from jax.experimental import pallas as pl
from jax.experimental.pallas import tpu as pltpu
from jax.sharding import PartitionSpec as P

IMG = 256
TX = 8
TY = 8
HALF = TX // 2
LANES = 128
SUBLANES = 8
SHARED = 2
FLOPS_OF_MICRO = 1_000_000_000
VMEM_BYTES = 24 * 1024 * 1024
VMEM_SPEC = pl.BlockSpec(memory_space=pltpu.VMEM)
SMEM_SPEC = pl.BlockSpec(memory_space=pltpu.SMEM)
BF = jnp.bfloat16
F32 = jnp.float32


def trig_tables():
    steps = np.arange(1, HALF + 1)
    angle_x = 2.0 * math.pi / IMG * steps[:, None] * (np.arange(IMG) - IMG // 2)[None, :]
    angle_y = 2.0 * math.pi / IMG * np.arange(IMG // 2)[:, None] * steps[None, :]
    table_x = np.concatenate([np.cos(angle_x), np.sin(angle_x)], 0).astype(np.float32)
    table_y = np.concatenate([np.cos(angle_y), np.sin(angle_y)], 1).astype(np.float32)
    return table_x, table_y.reshape(-1)


def device_ids():
    return [lax.axis_index(name) for name in ("dom", "orient", "cls")]


def xor_pairs(size, step):
    return [(i, i ^ step) for i in range(size)]


def column_of(line):
    size = line.shape[1]
    rows = lax.broadcasted_iota(jnp.int32, (size, size), 0)
    cols = lax.broadcasted_iota(jnp.int32, (size, size), 1)
    return jnp.sum(jnp.where(rows == cols, line, 0.0), axis=1, keepdims=True)


def bands_kernel(steps, images, references, *rest):
    ids = device_ids()
    lists, rest = rest[:3], rest[3:]
    outs, meta, shard = rest[: len(steps)], rest[len(steps)], rest[len(steps) + 1]
    lines, sems, meta_sems, line_sems, shard_sem = rest[len(steps) + 2 :]
    copies = [pltpu.make_async_copy(references, shard, shard_sem)]
    for place, (step, out) in enumerate(zip(steps, outs)):
        width = out.shape[2] - LANES
        start = (ids[0] ^ step) * width
        if step == SHARED:
            start = 2 * start + ids[2] * width
        start = pl.multiple_of(start, width)
        for part in range(out.shape[0]):
            copies.append(
                pltpu.make_async_copy(
                    images.at[part, :, pl.ds(start, width)],
                    out.at[part, :, pl.ds(0, width)],
                    sems.at[place, part],
                )
            )
    line_copies = [
        pltpu.make_async_copy(source, lines[place], line_sems.at[place])
        for place, source in enumerate(lists)
    ]
    for copy in line_copies + copies:
        copy.start()
    for copy in line_copies:
        copy.wait()
    lane = lax.broadcasted_iota(jnp.int32, meta.shape[1:], 1)
    fixed = column_of(lines[2][...])
    high = fixed.astype(BF).astype(F32)
    middle = (fixed - high).astype(BF).astype(F32)
    values = [column_of(lines[0][...].astype(F32)), column_of(lines[1][...].astype(F32))]
    table = jnp.zeros(meta.shape[1:], F32)
    for place, value in enumerate(values + [high, middle, fixed - high - middle]):
        table = jnp.where(lane == place, value, table)
    meta[0] = table.astype(BF)
    meta[1] = jnp.zeros(meta.shape[1:], BF)
    meta_copies = [
        pltpu.make_async_copy(
            meta, out.at[:, :, pl.ds(out.shape[2] - LANES, LANES)], meta_sems.at[place]
        )
        for place, out in enumerate(outs)
    ]
    for copy in meta_copies:
        copy.start()
    for copy in copies + meta_copies:
        copy.wait()


def image_bands(orient_lists, shift_ids, fixed_weights, images, references, dom):
    parts, rows, pixels = images.shape
    width = pixels // dom
    steps = list(range(1, dom))
    sources = [images, references] + [
        array.reshape(1, rows) for array in (orient_lists, shift_ids, fixed_weights)
    ]
    sources = [pltpu.with_memory_space_constraint(array, pltpu.HBM) for array in sources]
    *bands, meta, shard = pl.pallas_call(
        functools.partial(bands_kernel, steps),
        out_shape=[
            pltpu.VMEM((parts, rows, width // (1 + (step == SHARED)) + LANES), images.dtype)
            for step in steps
        ]
        + [
            jax.ShapeDtypeStruct((parts, rows, LANES), BF),
            pltpu.VMEM(references.shape, references.dtype),
        ],
        in_specs=[pl.BlockSpec(memory_space=pl.ANY)] * len(sources),
        out_specs=[pl.BlockSpec(memory_space=pl.ANY)] * len(steps)
        + [pl.BlockSpec(memory_space=pltpu.VMEM), pl.BlockSpec(memory_space=pl.ANY)],
        scratch_shapes=[
            [pltpu.VMEM((1, rows), array.dtype) for array in sources[2:]],
            pltpu.SemaphoreType.DMA((len(steps), parts)),
            pltpu.SemaphoreType.DMA((len(steps),)),
            pltpu.SemaphoreType.DMA((3,)),
            pltpu.SemaphoreType.DMA,
        ],
        compiler_params=pltpu.CompilerParams(vmem_limit_bytes=VMEM_BYTES),
        cost_estimate=pl.CostEstimate(
            flops=0, bytes_accessed=4 * parts * rows * (pixels - width), transcendentals=0
        ),
        name="image_bands",
    )(*sources)
    return bands, meta, shard


def own_kernel(images, band, sems):
    ids = device_ids()
    width = band.shape[2]
    start = pl.multiple_of(ids[0] * width, width)
    copies = [
        pltpu.make_async_copy(images.at[part, :, pl.ds(start, width)], band.at[part], sems.at[part])
        for part in range(band.shape[0])
    ]
    for copy in copies:
        copy.start()
    for copy in copies:
        copy.wait()


def own_band(images, dom):
    parts, rows, pixels = images.shape
    shape = (parts, rows, pixels // dom)
    return pl.pallas_call(
        own_kernel,
        out_shape=pltpu.VMEM(shape, images.dtype),
        in_specs=[pl.BlockSpec(memory_space=pl.ANY)],
        out_specs=pl.BlockSpec(memory_space=pl.ANY),
        scratch_shapes=[pltpu.SemaphoreType.DMA((parts,))],
        compiler_params=pltpu.CompilerParams(vmem_limit_bytes=VMEM_BYTES),
        name="own_band",
    )(pltpu.with_memory_space_constraint(images, pltpu.HBM))


def in_vmem(arrays):
    placed = [pltpu.with_memory_space_constraint(array, pltpu.VMEM) for array in arrays]
    return placed, [VMEM_SPEC] * len(placed)


def flat(groups):
    return [image for images, _ in groups for image in images]


def sizes_of(groups):
    return [len(images) for images, _ in groups]


def by_group(sizes, refs):
    images, at = [], 0
    for size in sizes:
        images.append(refs[at : at + size])
        at += size
    return images, refs[at:]


def load(images, ids, part, start, size):
    if len(images) == 1:
        return images[0][part, :, pl.ds(pl.multiple_of(start, size), size)].astype(F32)
    half = images[0].shape[2] - LANES
    side = start // half
    cols = pl.ds(pl.multiple_of(start - side * half, size), size)
    mine, other = (image[part, :, cols].astype(F32) for image in images)
    return jnp.where(side == ids[2], mine, other)


def shift_references(refs, right, step, ids, orients, table_y):
    names = refs.shape[1]
    chunk = right.shape[2] // 2
    lines = chunk // IMG
    line_base = (ids[0] * orients + (ids[1] ^ step[1])) * lines
    for line in range(lines):
        to_re = slice(2 * line * IMG, (2 * line + 1) * IMG)
        to_im = slice((2 * line + 1) * IMG, (2 * line + 2) * IMG)
        base = (line_base + line) * TY
        cols = slice(step[0] * chunk + line * IMG, step[0] * chunk + (line + 1) * IMG)
        ref_re = refs[0, :, cols].astype(F32)
        ref_im = refs[1, :, cols].astype(F32)

        def put(b, re, im):
            right[step[0], b * names : (b + 1) * names, to_re] = re.astype(BF)
            right[step[0], b * names : (b + 1) * names, to_im] = im.astype(BF)

        put(TY // 2, ref_re, ref_im)
        for t in range(1, HALF + 1):
            cosine = table_y[base + t - 1]
            sine = table_y[base + HALF + t - 1]
            re_c, im_s = ref_re * cosine, ref_im * sine
            im_c, re_s = ref_im * cosine, ref_re * sine
            put(TY // 2 - t, re_c - im_s, im_c + re_s)
            if t < HALF:
                put(TY // 2 + t, re_c + im_s, im_c - re_s)


def shift_images(images, left, column, ids, table_x):
    chunk = left.shape[1] // 2
    rows = images[0][0].shape[1]
    for line in range(chunk // IMG):
        to_re = slice(2 * line * IMG, (2 * line + 1) * IMG)
        to_im = slice((2 * line + 1) * IMG, (2 * line + 2) * IMG)
        for g, group in enumerate(images):
            start = column * chunk + line * IMG
            re = load(group, ids, 0, start, IMG)
            im = load(group, ids, 1, start, IMG)

            def put(a, re, im):
                top = (g * TX + a) * rows
                left[top : top + rows, to_re] = re.astype(BF)
                left[top : top + rows, to_im] = im.astype(BF)

            put(TX // 2, re, im)
            for t in range(1, HALF + 1):
                cosine = table_x[t - 1 : t, :]
                sine = table_x[HALF + t - 1 : HALF + t, :]
                re_c, im_s = re * cosine, im * sine
                re_s, im_c = re * sine, im * cosine
                put(TX // 2 - t, re_c + im_s, im_c - re_s)
                if t < HALF:
                    put(TX // 2 + t, re_c - im_s, re_s + im_c)


def add_products(outs, left, right):
    rows = outs[0].shape[0]
    value = lax.dot_general(left, right, (((1,), (1,)), ((), ())), preferred_element_type=F32)
    for g, out in enumerate(outs):
        out[...] += value[g * rows : (g + 1) * rows]


def near_kernel(sizes, orients, steps, sums, table_y, table_x, *rest):
    ids = device_ids()
    groups, count = len(sizes), len(steps)
    shards, rest = rest[:count], rest[count:]
    images, rest = by_group(sizes, rest)
    before, rest = rest[: groups * sums], rest[groups * sums :]
    outs, (right, refs, *lefts) = rest[:groups], rest[groups:]
    chunk = shards[0].shape[3]
    per_class = shards[0].shape[2]
    for place, shard in enumerate(shards):
        cols = slice(place * chunk, (place + 1) * chunk)
        for part in range(2):
            for k in range(shard.shape[1]):
                refs[part, k * per_class : (k + 1) * per_class, cols] = shard[part, k]
    for g, out in enumerate(outs):
        out[...] = before[g][...] if sums else jnp.zeros_like(out)

    for place in range(count):
        step = 2 * place + steps[0]
        left = lefts[place % 2]
        shift_references(refs, right, (place, step), ids, orients, table_y)
        shift_images(images, left, ids[1] ^ step, ids, table_x)
        add_products(outs, left[...], right[place])


def far_kernel(sizes, counts, table_x, *rest):
    ids = device_ids()
    groups = len(sizes)
    rights, rest = rest[: len(counts)], rest[len(counts) :]
    images, rest = by_group(sizes, rest)
    outs, lefts = rest[:groups], rest[groups:]
    for out in outs:
        out[...] = jnp.zeros_like(out)
    turn = 0
    for first, (right, count) in enumerate(zip(rights, counts)):
        for place in range(count):
            left = lefts[turn % 2]
            shift_images(images, left, ids[1] ^ (2 * place + first), ids, table_x)
            add_products(outs, left[...], right[place])
            turn += 1


def logits_cost(micros):
    return pl.CostEstimate(flops=micros * FLOPS_OF_MICRO, bytes_accessed=0, transcendentals=0)


def near_logits(table_x, table_y, shards, picked, steps, before, micros):
    parts, classes, orients, chunk = shards[0].shape
    groups = len(picked)
    rows = picked[0][0][0].shape[1]
    names = classes * orients
    count = len(steps)
    out_shape = (TX * rows, TY * names)
    used = [shards[step] for step in steps]
    arrays, specs = in_vmem([table_x, *used, *flat(picked), *before])
    *sums, right = pl.pallas_call(
        functools.partial(
            near_kernel, sizes_of(picked), len(shards), steps, len(before) > 0
        ),
        out_shape=[pltpu.VMEM(out_shape, F32)] * groups
        + [pltpu.VMEM((count, TY * names, 2 * chunk), BF)],
        in_specs=[SMEM_SPEC] + specs,
        out_specs=[VMEM_SPEC] * (groups + 1),
        scratch_shapes=[
            pltpu.VMEM((parts, names, count * chunk), BF),
            pltpu.VMEM((groups * TX * rows, 2 * chunk), BF),
            pltpu.VMEM((groups * TX * rows, 2 * chunk), BF),
        ],
        compiler_params=pltpu.CompilerParams(vmem_limit_bytes=VMEM_BYTES),
        cost_estimate=logits_cost(micros),
        name="near_logits",
    )(table_y, *arrays)
    return sums, right


def far_logits(table_x, rights, picked, micros):
    groups = len(picked)
    rows = picked[0][0][0].shape[1]
    names, chunk = rights[0].shape[1:]
    out_shape = (TX * rows, names)
    arrays, specs = in_vmem([table_x, *rights, *flat(picked)])
    return pl.pallas_call(
        functools.partial(far_kernel, sizes_of(picked), [right.shape[0] for right in rights]),
        out_shape=[pltpu.VMEM(out_shape, F32)] * groups,
        in_specs=specs,
        out_specs=[VMEM_SPEC] * groups,
        scratch_shapes=[pltpu.VMEM((groups * TX * rows, chunk), BF)] * 2,
        compiler_params=pltpu.CompilerParams(vmem_limit_bytes=VMEM_BYTES),
        cost_estimate=logits_cost(micros),
        name="far_logits",
    )(*arrays)


def stats_kernel(counts, classes, orients, *refs):
    *logits, out = refs
    rows, lanes = logits[0].shape[0] // TX, logits[0].shape[1]
    lane = lax.broadcasted_iota(jnp.int32, (rows, lanes), 1)
    class_of = (lane // orients) % classes
    out_lane = lax.broadcasted_iota(jnp.int32, (rows, LANES), 1)
    packed = jnp.zeros((SUBLANES, LANES), F32)
    for g, count in enumerate(counts):
        total = sum(ref[...] for ref in logits[:count])
        logits = logits[count:]
        pieces = [total[a * rows : (a + 1) * rows] for a in range(TX)]
        top = functools.reduce(jnp.maximum, pieces)
        top = jnp.max(top, axis=1, keepdims=True)
        sums = sum(jnp.exp(piece - top) for piece in pieces)
        line = jnp.where(out_lane == 0, top, 0.0)
        for k in range(classes):
            part = jnp.sum(jnp.where(class_of == k, sums, 0.0), axis=1, keepdims=True)
            line = jnp.where(out_lane == k + 1, part, line)
        for half in range(rows // SUBLANES):
            block = line[half * SUBLANES : (half + 1) * SUBLANES]
            place = (g * (rows // SUBLANES) + half) * SUBLANES
            packed = packed + pltpu.roll(block, place, 1)
    out[...] = packed


def logit_stats(terms, classes, orients):
    arrays, specs = in_vmem([array for held in terms for array in held])
    return pl.pallas_call(
        functools.partial(stats_kernel, [len(held) for held in terms], classes, orients),
        out_shape=pltpu.VMEM((SUBLANES, LANES), F32),
        in_specs=specs,
        out_specs=VMEM_SPEC,
        compiler_params=pltpu.CompilerParams(vmem_limit_bytes=VMEM_BYTES),
        name="logit_stats",
    )(*arrays)


def rows_kernel(sizes, table_y, table_x, *rest):
    ids = device_ids()
    groups = len(sizes)
    metas = rest[:groups]
    images, (out,) = by_group(sizes, rest[groups:])
    rows = metas[0].shape[1]
    width = out.shape[2]
    lines = width // IMG
    line_base = ids[0] * lines
    for g in range(groups):
        own = slice(g * rows, (g + 1) * rows)
        last = metas[g].shape[2] - LANES
        shift = metas[g][0, :, last:].astype(F32)[:, 1:2].astype(jnp.int32)
        move_x = jnp.broadcast_to(shift % TX - TX // 2, (rows, IMG))
        move_y = jnp.broadcast_to(shift // TX - TY // 2, (rows, LANES))
        phase_c = jnp.ones((rows, IMG), F32)
        phase_s = jnp.zeros((rows, IMG), F32)
        for t in range(1, HALF + 1):
            hit = jnp.abs(move_x) == t
            phase_c = jnp.where(hit, table_x[t - 1 : t, :], phase_c)
            phase_s = jnp.where(hit, table_x[HALF + t - 1 : HALF + t, :], phase_s)
        phase_s = jnp.where(move_x < 0, -phase_s, phase_s)
        hits = [jnp.abs(move_y) == t for t in range(1, HALF + 1)]
        sign = jnp.where(move_y < 0, -1.0, 1.0)

        def add_line(line, carry):
            base = (line_base + line) * TY
            cos_y = jnp.ones((rows, LANES), F32)
            sin_y = jnp.zeros((rows, LANES), F32)
            for t in range(1, HALF + 1):
                cos_y = jnp.where(hits[t - 1], table_y[base + t - 1], cos_y)
                sin_y = jnp.where(hits[t - 1], table_y[base + HALF + t - 1], sin_y)
            sin_y = sin_y * sign
            for part in range(IMG // LANES):
                across = slice(part * LANES, (part + 1) * LANES)
                start = pl.multiple_of(line * IMG + part * LANES, LANES)
                cols = pl.ds(start, LANES)
                cos_x, sin_x = phase_c[:, across], phase_s[:, across]
                cosine = cos_x * cos_y - sin_x * sin_y
                sine = sin_x * cos_y + cos_x * sin_y
                re = load(images[g], ids, 0, start, LANES)
                im = load(images[g], ids, 1, start, LANES)
                out[0, own, cols] = (re * cosine - im * sine).astype(BF)
                out[1, own, cols] = (re * sine + im * cosine).astype(BF)
            return carry

        lax.fori_loop(0, lines, add_line, 0, unroll=min(lines, 4))


def aligned_rows(table_x, table_y, picked, width):
    parts, rows = picked[0][0][0].shape[:2]
    groups = len(picked)
    arrays, specs = in_vmem([table_x] + [table for _, table in picked] + flat(picked))
    return pl.pallas_call(
        functools.partial(rows_kernel, sizes_of(picked)),
        out_shape=pltpu.VMEM((parts, groups * rows, width), BF),
        in_specs=[SMEM_SPEC] + specs,
        out_specs=VMEM_SPEC,
        compiler_params=pltpu.CompilerParams(vmem_limit_bytes=VMEM_BYTES),
        cost_estimate=pl.CostEstimate(
            flops=0,
            bytes_accessed=0,
            transcendentals=0,
        ),
        name="aligned_rows",
    )(table_y, *arrays)


def unpacked(packed, place, blocks):
    first = place * blocks * SUBLANES
    return jnp.concatenate(
        [pltpu.roll(packed, (LANES - first - i * SUBLANES) % LANES, 1) for i in range(blocks)]
    )


def volume_kernel(groups, orients, classes, *rest):
    ids = device_ids()
    stats, metas = rest[:2], rest[2 : 2 + groups]
    near, far = rest[2 + groups], rest[3 + groups]
    prob, outs = rest[4 + groups], rest[5 + groups :]
    rows = metas[0].shape[1]
    width = near.shape[2]
    chunk = min(width, 8 * IMG)
    lane = lax.broadcasted_iota(jnp.int32, (rows, LANES), 1)
    pieces = []
    for g in range(groups):
        top = g % 2 * SUBLANES
        mine, other = (
            unpacked(ref[top : top + SUBLANES, :], g // 2, rows // SUBLANES) for ref in stats
        )
        top = jnp.maximum(mine[:, 0:1], other[:, 0:1])
        mine_scale = jnp.exp(mine[:, 0:1] - top)
        other_scale = jnp.exp(other[:, 0:1] - top)
        held = (lane >= 1) & (lane <= classes)
        both = jnp.where(held, mine * mine_scale + other * other_scale, 0.0)
        totals = jnp.sum(both, axis=1, keepdims=True)
        spread = jnp.zeros((rows, LANES), F32)
        for k in range(classes):
            spread = jnp.where(lane % SUBLANES == k, mine[:, k + 1 : k + 2], spread)
        class_prob = spread * mine_scale / totals
        if g == 0:
            prob[...] = class_prob
        last = metas[g].shape[2] - LANES
        table = metas[g][0, :, last:].astype(F32)
        fixed = table[:, 2:3] + table[:, 3:4] + table[:, 4:5]
        weight = (fixed * class_prob).astype(BF).astype(F32)
        bin_of = table[:, 0:1].astype(jnp.int32) ^ ids[1]
        pieces.append(jnp.where(lane // SUBLANES == bin_of, weight, 0.0))
    mixes = []
    for held in (pieces[:2], pieces[2:]):
        mixing = jnp.transpose(jnp.concatenate(held, axis=0))
        mixes.append(mixing[: orients * SUBLANES].astype(BF))
    for part in range(2):
        for column in range(0, width, chunk):
            cols = slice(column, column + chunk)
            value = jnp.dot(mixes[0], near[part, :, cols], preferred_element_type=F32)
            value += jnp.dot(mixes[1], far[part, :, cols], preferred_element_type=F32)
            for o in range(orients):
                term = value[o * SUBLANES : o * SUBLANES + classes]
                outs[o][part, :, cols] = term.astype(outs[o].dtype)


def volume_terms(stats, groups, near, far, orients, classes):
    parts, entries, width = near.shape
    rest = far.shape[1]
    rows = groups[0][1].shape[1]
    out_shape = (parts, classes, width)
    arrays, specs = in_vmem([*stats, *(table for _, table in groups), near, far])
    return pl.pallas_call(
        functools.partial(volume_kernel, len(groups), orients, classes),
        out_shape=[pltpu.VMEM((rows, LANES), F32)]
        + [pltpu.VMEM(out_shape, F32 if o == 0 else BF) for o in range(orients)],
        in_specs=specs,
        out_specs=[VMEM_SPEC] * (1 + orients),
        compiler_params=pltpu.CompilerParams(vmem_limit_bytes=VMEM_BYTES),
        cost_estimate=pl.CostEstimate(
            flops=4 * orients * classes * (entries + rest) * width,
            bytes_accessed=4 * (entries + rest) * width + 4 * orients * classes * width,
            transcendentals=0,
        ),
        name="volume_terms",
    )(*arrays)


def total_kernel(first, *rest):
    out = rest[-1]
    total = first[...]
    for term in rest[:-1]:
        total = total + term[...].astype(F32)
    for part in range(out.shape[0]):
        for k in range(out.shape[1]):
            out[part, k] = total[part, k : k + 1]


def total_volume(terms):
    parts, classes, width = terms[0].shape
    arrays, specs = in_vmem(terms)
    return pl.pallas_call(
        total_kernel,
        out_shape=jax.ShapeDtypeStruct((parts, classes, 1, width), F32),
        in_specs=specs,
        compiler_params=pltpu.CompilerParams(vmem_limit_bytes=VMEM_BYTES),
        name="total_volume",
    )(*arrays)


def local(dom, orient, cls, references, images, orient_lists, shift_ids, fixed_weights):
    classes, orients = references.shape[1], references.shape[2]
    table_x, table_y = (jnp.asarray(t) for t in trig_tables())

    def swap_dom(array, step):
        return lax.ppermute(array, "dom", xor_pairs(dom, step))

    def swap_orient(array, step):
        return lax.ppermute(array, "orient", xor_pairs(orient, step))

    bands, meta, shard = image_bands(
        orient_lists, shift_ids, fixed_weights, images, references, dom
    )
    arrived = {step: swap_dom(bands[step - 1], step) for step in [1, *range(dom - 1, 1, -1)]}
    tied, arrived[1] = lax.optimization_barrier((shard, arrived[1]))
    shards = [shard] + [None] * (orient - 1)
    for step in [*range(2, orient, 2), *range(1, orient, 2)]:
        shards[step] = swap_orient(tied if step == orient - 1 else shard, step)
    half = arrived[SHARED]
    groups = [([own_band(images, dom)], meta)]
    groups += [([arrived[step]], arrived[step]) for step in range(1, dom)]
    groups[SHARED] = ([half, lax.ppermute(half, "cls", xor_pairs(cls, 1))], half)

    width = images.shape[2] // dom
    aligned_near = aligned_rows(table_x, table_y, groups[:2], width)
    shards[2], aligned_near = lax.optimization_barrier((shards[2], aligned_near))
    every = range(orient)
    first, right = near_logits(table_x, table_y, shards, groups[:2], every[0::2], [], 0)
    near, right_late = near_logits(
        table_x, table_y, shards, groups[:2], every[1::2], first, 20
    )
    swapped = swap_dom(near[1], 1)
    right_late, swapped = lax.optimization_barrier((right_late, swapped))
    one_phase = dom == 4
    if one_phase:
        crossed = swap_dom(near[0], 2)
        crossed_over = swap_dom(near[1], 3)
    far = list(far_logits(table_x, [right, right_late], groups[2:], 6))
    if one_phase:
        terms = [
            [near[0], swapped, swap_dom(far[0], 2), swap_dom(far[1], 3)],
            [far[0], swap_dom(far[1], 1), crossed, crossed_over],
        ]
    else:
        partial = [*near, *far]
        here = {s: partial[s] + swap_dom(partial[s ^ 1], 1) for s in range(2, dom, 2)}
        here[0] = near[0] + swapped
        step = 2
        while step < dom:
            there = {s: swap_dom(here[s ^ step], step) for s in here}
            step *= 2
            if step < dom:
                here = {s: here[s] + there[s] for s in here}
        terms = [[here[s], there[s]] for s in sorted(here)]
    if one_phase:
        groups[2][0][0], *terms[1][2:] = lax.optimization_barrier(
            (groups[2][0][0], *terms[1][2:])
        )
    aligned_far = aligned_rows(table_x, table_y, groups[2:], width)
    terms[0][-1], aligned_far = lax.optimization_barrier((terms[0][-1], aligned_far))
    stats = logit_stats(terms, classes, orients)

    stats = jnp.concatenate([stats, swap_dom(stats, 1)])
    stats_all = [stats, lax.ppermute(stats, "cls", xor_pairs(cls, 1))]
    prob, *terms = volume_terms(
        stats_all, groups, aligned_near, aligned_far, orients, classes
    )
    order = sorted(range(1, orients), key=lambda place: place != orients // 2)
    terms = [terms[0]] + [swap_orient(terms[o], o) for o in order]
    return prob[:, :classes], total_volume(terms)


def solution(mesh):
    in_specs = (
        P(None, "cls", None, ("dom", "orient")),
        P(None, ("dom", "orient"), None),
        P(("dom", "orient"), None),
        P(("dom", "orient"), None),
        P(("dom", "orient"), None),
    )
    out_specs = (P(("dom", "orient"), "cls"), P(None, "cls", "orient", "dom"))
    body = functools.partial(local, mesh.shape["dom"], mesh.shape["orient"], mesh.shape["cls"])
    return jax.shard_map(body, mesh=mesh, in_specs=in_specs, out_specs=out_specs, check_vma=False)
```

```python
import functools
import math

import jax
import jax.numpy as jnp
import numpy as np
from jax import lax
from jax.experimental import pallas as pl
from jax.experimental.pallas import tpu as pltpu
from jax.sharding import PartitionSpec as P

IMG = 256
TX = 8
TY = 8
HALF = TX // 2
LANES = 128
SUBLANES = 8
SHARED = 2
FLOPS_OF_MICRO = 1_000_000_000
VMEM_BYTES = 24 * 1024 * 1024
VMEM_SPEC = pl.BlockSpec(memory_space=pltpu.VMEM)
SMEM_SPEC = pl.BlockSpec(memory_space=pltpu.SMEM)
BF = jnp.bfloat16
F32 = jnp.float32


def trig_tables():
    steps = np.arange(1, HALF + 1)
    angle_x = 2.0 * math.pi / IMG * steps[:, None] * (np.arange(IMG) - IMG // 2)[None, :]
    angle_y = 2.0 * math.pi / IMG * np.arange(IMG // 2)[:, None] * steps[None, :]
    table_x = np.concatenate([np.cos(angle_x), np.sin(angle_x)], 0).astype(np.float32)
    table_y = np.concatenate([np.cos(angle_y), np.sin(angle_y)], 1).astype(np.float32)
    return table_x, table_y.reshape(-1)


def device_ids():
    return [lax.axis_index(name) for name in ("dom", "orient", "cls")]


def xor_pairs(size, step):
    return [(i, i ^ step) for i in range(size)]


def column_of(line):
    size = line.shape[1]
    rows = lax.broadcasted_iota(jnp.int32, (size, size), 0)
    cols = lax.broadcasted_iota(jnp.int32, (size, size), 1)
    return jnp.sum(jnp.where(rows == cols, line, 0.0), axis=1, keepdims=True)


def bands_kernel(steps, images, references, *rest):
    ids = device_ids()
    lists, rest = rest[:3], rest[3:]
    outs, meta, shard = rest[: len(steps)], rest[len(steps)], rest[len(steps) + 1]
    lines, sems, meta_sems, line_sems, shard_sem = rest[len(steps) + 2 :]
    copies = [pltpu.make_async_copy(references, shard, shard_sem)]
    for place, (step, out) in enumerate(zip(steps, outs)):
        width = out.shape[2] - LANES
        start = (ids[0] ^ step) * width
        if step == SHARED:
            start = 2 * start + ids[2] * width
        start = pl.multiple_of(start, width)
        for part in range(out.shape[0]):
            copies.append(
                pltpu.make_async_copy(
                    images.at[part, :, pl.ds(start, width)],
                    out.at[part, :, pl.ds(0, width)],
                    sems.at[place, part],
                )
            )
    line_copies = [
        pltpu.make_async_copy(source, lines[place], line_sems.at[place])
        for place, source in enumerate(lists)
    ]
    for copy in line_copies + copies:
        copy.start()
    for copy in line_copies:
        copy.wait()
    lane = lax.broadcasted_iota(jnp.int32, meta.shape[1:], 1)
    fixed = column_of(lines[2][...])
    high = fixed.astype(BF).astype(F32)
    middle = (fixed - high).astype(BF).astype(F32)
    values = [column_of(lines[0][...].astype(F32)), column_of(lines[1][...].astype(F32))]
    table = jnp.zeros(meta.shape[1:], F32)
    for place, value in enumerate(values + [high, middle, fixed - high - middle]):
        table = jnp.where(lane == place, value, table)
    meta[0] = table.astype(BF)
    meta[1] = jnp.zeros(meta.shape[1:], BF)
    meta_copies = [
        pltpu.make_async_copy(
            meta, out.at[:, :, pl.ds(out.shape[2] - LANES, LANES)], meta_sems.at[place]
        )
        for place, out in enumerate(outs)
    ]
    for copy in meta_copies:
        copy.start()
    for copy in copies + meta_copies:
        copy.wait()


def image_bands(orient_lists, shift_ids, fixed_weights, images, references, dom):
    parts, rows, pixels = images.shape
    width = pixels // dom
    steps = list(range(1, dom))
    sources = [images, references] + [
        array.reshape(1, rows) for array in (orient_lists, shift_ids, fixed_weights)
    ]
    sources = [pltpu.with_memory_space_constraint(array, pltpu.HBM) for array in sources]
    *bands, meta, shard = pl.pallas_call(
        functools.partial(bands_kernel, steps),
        out_shape=[
            pltpu.VMEM((parts, rows, width // (1 + (step == SHARED)) + LANES), images.dtype)
            for step in steps
        ]
        + [
            jax.ShapeDtypeStruct((parts, rows, LANES), BF),
            pltpu.VMEM(references.shape, references.dtype),
        ],
        in_specs=[pl.BlockSpec(memory_space=pl.ANY)] * len(sources),
        out_specs=[pl.BlockSpec(memory_space=pl.ANY)] * len(steps)
        + [pl.BlockSpec(memory_space=pltpu.VMEM), pl.BlockSpec(memory_space=pl.ANY)],
        scratch_shapes=[
            [pltpu.VMEM((1, rows), array.dtype) for array in sources[2:]],
            pltpu.SemaphoreType.DMA((len(steps), parts)),
            pltpu.SemaphoreType.DMA((len(steps),)),
            pltpu.SemaphoreType.DMA((3,)),
            pltpu.SemaphoreType.DMA,
        ],
        compiler_params=pltpu.CompilerParams(vmem_limit_bytes=VMEM_BYTES),
        cost_estimate=pl.CostEstimate(
            flops=0, bytes_accessed=4 * parts * rows * (pixels - width), transcendentals=0
        ),
        name="image_bands",
    )(*sources)
    return bands, meta, shard


def own_kernel(images, band, sems):
    ids = device_ids()
    width = band.shape[2]
    start = pl.multiple_of(ids[0] * width, width)
    copies = [
        pltpu.make_async_copy(images.at[part, :, pl.ds(start, width)], band.at[part], sems.at[part])
        for part in range(band.shape[0])
    ]
    for copy in copies:
        copy.start()
    for copy in copies:
        copy.wait()


def own_band(images, dom):
    parts, rows, pixels = images.shape
    shape = (parts, rows, pixels // dom)
    return pl.pallas_call(
        own_kernel,
        out_shape=pltpu.VMEM(shape, images.dtype),
        in_specs=[pl.BlockSpec(memory_space=pl.ANY)],
        out_specs=pl.BlockSpec(memory_space=pl.ANY),
        scratch_shapes=[pltpu.SemaphoreType.DMA((parts,))],
        compiler_params=pltpu.CompilerParams(vmem_limit_bytes=VMEM_BYTES),
        name="own_band",
    )(pltpu.with_memory_space_constraint(images, pltpu.HBM))


def in_vmem(arrays):
    placed = [pltpu.with_memory_space_constraint(array, pltpu.VMEM) for array in arrays]
    return placed, [VMEM_SPEC] * len(placed)


def flat(groups):
    return [image for images, _ in groups for image in images]


def sizes_of(groups):
    return [len(images) for images, _ in groups]


def by_group(sizes, refs):
    images, at = [], 0
    for size in sizes:
        images.append(refs[at : at + size])
        at += size
    return images, refs[at:]


def load(images, ids, part, start, size):
    if len(images) == 1:
        return images[0][part, :, pl.ds(pl.multiple_of(start, size), size)].astype(F32)
    half = images[0].shape[2] - LANES
    side = start // half
    cols = pl.ds(pl.multiple_of(start - side * half, size), size)
    mine, other = (image[part, :, cols].astype(F32) for image in images)
    return jnp.where(side == ids[2], mine, other)


def shift_references(refs, right, step, ids, orients, table_y):
    names = refs.shape[1]
    chunk = right.shape[2] // 2
    lines = chunk // IMG
    line_base = (ids[0] * orients + (ids[1] ^ step[1])) * lines
    for line in range(lines):
        to_re = slice(2 * line * IMG, (2 * line + 1) * IMG)
        to_im = slice((2 * line + 1) * IMG, (2 * line + 2) * IMG)
        base = (line_base + line) * TY
        cols = slice(step[0] * chunk + line * IMG, step[0] * chunk + (line + 1) * IMG)
        ref_re = refs[0, :, cols].astype(F32)
        ref_im = refs[1, :, cols].astype(F32)

        def put(b, re, im):
            right[step[0], b * names : (b + 1) * names, to_re] = re.astype(BF)
            right[step[0], b * names : (b + 1) * names, to_im] = im.astype(BF)

        put(TY // 2, ref_re, ref_im)
        for t in range(1, HALF + 1):
            cosine = table_y[base + t - 1]
            sine = table_y[base + HALF + t - 1]
            re_c, im_s = ref_re * cosine, ref_im * sine
            im_c, re_s = ref_im * cosine, ref_re * sine
            put(TY // 2 - t, re_c - im_s, im_c + re_s)
            if t < HALF:
                put(TY // 2 + t, re_c + im_s, im_c - re_s)


def shift_images(images, left, column, ids, table_x):
    chunk = left.shape[1] // 2
    rows = images[0][0].shape[1]
    for line in range(chunk // IMG):
        to_re = slice(2 * line * IMG, (2 * line + 1) * IMG)
        to_im = slice((2 * line + 1) * IMG, (2 * line + 2) * IMG)
        for g, group in enumerate(images):
            start = column * chunk + line * IMG
            re = load(group, ids, 0, start, IMG)
            im = load(group, ids, 1, start, IMG)

            def put(a, re, im):
                top = (g * TX + a) * rows
                left[top : top + rows, to_re] = re.astype(BF)
                left[top : top + rows, to_im] = im.astype(BF)

            put(TX // 2, re, im)
            for t in range(1, HALF + 1):
                cosine = table_x[t - 1 : t, :]
                sine = table_x[HALF + t - 1 : HALF + t, :]
                re_c, im_s = re * cosine, im * sine
                re_s, im_c = re * sine, im * cosine
                put(TX // 2 - t, re_c + im_s, im_c - re_s)
                if t < HALF:
                    put(TX // 2 + t, re_c - im_s, re_s + im_c)


def add_products(outs, left, right):
    rows = outs[0].shape[0]
    value = lax.dot_general(left, right, (((1,), (1,)), ((), ())), preferred_element_type=F32)
    for g, out in enumerate(outs):
        out[...] += value[g * rows : (g + 1) * rows]


def near_kernel(sizes, orients, steps, sums, table_y, table_x, *rest):
    ids = device_ids()
    groups, count = len(sizes), len(steps)
    shards, rest = rest[:count], rest[count:]
    images, rest = by_group(sizes, rest)
    before, rest = rest[: groups * sums], rest[groups * sums :]
    outs, (right, refs, *lefts) = rest[:groups], rest[groups:]
    chunk = shards[0].shape[3]
    per_class = shards[0].shape[2]
    for place, shard in enumerate(shards):
        cols = slice(place * chunk, (place + 1) * chunk)
        for part in range(2):
            for k in range(shard.shape[1]):
                refs[part, k * per_class : (k + 1) * per_class, cols] = shard[part, k]
    for g, out in enumerate(outs):
        out[...] = before[g][...] if sums else jnp.zeros_like(out)

    for place in range(count):
        step = 2 * place + steps[0]
        left = lefts[place % 2]
        shift_references(refs, right, (place, step), ids, orients, table_y)
        shift_images(images, left, ids[1] ^ step, ids, table_x)
        add_products(outs, left[...], right[place])


def far_kernel(sizes, counts, table_x, *rest):
    ids = device_ids()
    groups = len(sizes)
    rights, rest = rest[: len(counts)], rest[len(counts) :]
    images, rest = by_group(sizes, rest)
    outs, lefts = rest[:groups], rest[groups:]
    for out in outs:
        out[...] = jnp.zeros_like(out)
    turn = 0
    for first, (right, count) in enumerate(zip(rights, counts)):
        for place in range(count):
            left = lefts[turn % 2]
            shift_images(images, left, ids[1] ^ (2 * place + first), ids, table_x)
            add_products(outs, left[...], right[place])
            turn += 1


def logits_cost(micros):
    return pl.CostEstimate(flops=micros * FLOPS_OF_MICRO, bytes_accessed=0, transcendentals=0)


def near_logits(table_x, table_y, shards, picked, steps, before, micros):
    parts, classes, orients, chunk = shards[0].shape
    groups = len(picked)
    rows = picked[0][0][0].shape[1]
    names = classes * orients
    count = len(steps)
    out_shape = (TX * rows, TY * names)
    used = [shards[step] for step in steps]
    arrays, specs = in_vmem([table_x, *used, *flat(picked), *before])
    *sums, right = pl.pallas_call(
        functools.partial(
            near_kernel, sizes_of(picked), len(shards), steps, len(before) > 0
        ),
        out_shape=[pltpu.VMEM(out_shape, F32)] * groups
        + [pltpu.VMEM((count, TY * names, 2 * chunk), BF)],
        in_specs=[SMEM_SPEC] + specs,
        out_specs=[VMEM_SPEC] * (groups + 1),
        scratch_shapes=[
            pltpu.VMEM((parts, names, count * chunk), BF),
            pltpu.VMEM((groups * TX * rows, 2 * chunk), BF),
            pltpu.VMEM((groups * TX * rows, 2 * chunk), BF),
        ],
        compiler_params=pltpu.CompilerParams(vmem_limit_bytes=VMEM_BYTES),
        cost_estimate=logits_cost(micros),
        name="near_logits",
    )(table_y, *arrays)
    return sums, right


def far_logits(table_x, rights, picked, micros):
    groups = len(picked)
    rows = picked[0][0][0].shape[1]
    names, chunk = rights[0].shape[1:]
    out_shape = (TX * rows, names)
    arrays, specs = in_vmem([table_x, *rights, *flat(picked)])
    return pl.pallas_call(
        functools.partial(far_kernel, sizes_of(picked), [right.shape[0] for right in rights]),
        out_shape=[pltpu.VMEM(out_shape, F32)] * groups,
        in_specs=specs,
        out_specs=[VMEM_SPEC] * groups,
        scratch_shapes=[pltpu.VMEM((groups * TX * rows, chunk), BF)] * 2,
        compiler_params=pltpu.CompilerParams(vmem_limit_bytes=VMEM_BYTES),
        cost_estimate=logits_cost(micros),
        name="far_logits",
    )(*arrays)


def stats_kernel(counts, classes, orients, *refs):
    *logits, out = refs
    rows, lanes = logits[0].shape[0] // TX, logits[0].shape[1]
    lane = lax.broadcasted_iota(jnp.int32, (rows, lanes), 1)
    class_of = (lane // orients) % classes
    out_lane = lax.broadcasted_iota(jnp.int32, (rows, LANES), 1)
    packed = jnp.zeros((SUBLANES, LANES), F32)
    for g, count in enumerate(counts):
        total = sum(ref[...] for ref in logits[:count])
        logits = logits[count:]
        pieces = [total[a * rows : (a + 1) * rows] for a in range(TX)]
        top = functools.reduce(jnp.maximum, pieces)
        top = jnp.max(top, axis=1, keepdims=True)
        sums = sum(jnp.exp(piece - top) for piece in pieces)
        line = jnp.where(out_lane == 0, top, 0.0)
        for k in range(classes):
            part = jnp.sum(jnp.where(class_of == k, sums, 0.0), axis=1, keepdims=True)
            line = jnp.where(out_lane == k + 1, part, line)
        for half in range(rows // SUBLANES):
            block = line[half * SUBLANES : (half + 1) * SUBLANES]
            place = (g * (rows // SUBLANES) + half) * SUBLANES
            packed = packed + pltpu.roll(block, place, 1)
    out[...] = packed


def logit_stats(terms, classes, orients):
    arrays, specs = in_vmem([array for held in terms for array in held])
    return pl.pallas_call(
        functools.partial(stats_kernel, [len(held) for held in terms], classes, orients),
        out_shape=pltpu.VMEM((SUBLANES, LANES), F32),
        in_specs=specs,
        out_specs=VMEM_SPEC,
        compiler_params=pltpu.CompilerParams(vmem_limit_bytes=VMEM_BYTES),
        name="logit_stats",
    )(*arrays)


def rows_kernel(sizes, table_y, table_x, *rest):
    ids = device_ids()
    groups = len(sizes)
    metas = rest[:groups]
    images, (out,) = by_group(sizes, rest[groups:])
    rows = metas[0].shape[1]
    width = out.shape[2]
    lines = width // IMG
    line_base = ids[0] * lines
    for g in range(groups):
        own = slice(g * rows, (g + 1) * rows)
        last = metas[g].shape[2] - LANES
        shift = metas[g][0, :, last:].astype(F32)[:, 1:2].astype(jnp.int32)
        move_x = jnp.broadcast_to(shift % TX - TX // 2, (rows, IMG))
        move_y = jnp.broadcast_to(shift // TX - TY // 2, (rows, LANES))
        phase_c = jnp.ones((rows, IMG), F32)
        phase_s = jnp.zeros((rows, IMG), F32)
        for t in range(1, HALF + 1):
            hit = jnp.abs(move_x) == t
            phase_c = jnp.where(hit, table_x[t - 1 : t, :], phase_c)
            phase_s = jnp.where(hit, table_x[HALF + t - 1 : HALF + t, :], phase_s)
        phase_s = jnp.where(move_x < 0, -phase_s, phase_s)
        hits = [jnp.abs(move_y) == t for t in range(1, HALF + 1)]
        sign = jnp.where(move_y < 0, -1.0, 1.0)

        def add_line(line, carry):
            base = (line_base + line) * TY
            cos_y = jnp.ones((rows, LANES), F32)
            sin_y = jnp.zeros((rows, LANES), F32)
            for t in range(1, HALF + 1):
                cos_y = jnp.where(hits[t - 1], table_y[base + t - 1], cos_y)
                sin_y = jnp.where(hits[t - 1], table_y[base + HALF + t - 1], sin_y)
            sin_y = sin_y * sign
            for part in range(IMG // LANES):
                across = slice(part * LANES, (part + 1) * LANES)
                start = pl.multiple_of(line * IMG + part * LANES, LANES)
                cols = pl.ds(start, LANES)
                cos_x, sin_x = phase_c[:, across], phase_s[:, across]
                cosine = cos_x * cos_y - sin_x * sin_y
                sine = sin_x * cos_y + cos_x * sin_y
                re = load(images[g], ids, 0, start, LANES)
                im = load(images[g], ids, 1, start, LANES)
                out[0, own, cols] = (re * cosine - im * sine).astype(BF)
                out[1, own, cols] = (re * sine + im * cosine).astype(BF)
            return carry

        lax.fori_loop(0, lines, add_line, 0, unroll=min(lines, 4))


def aligned_rows(table_x, table_y, picked, width):
    parts, rows = picked[0][0][0].shape[:2]
    groups = len(picked)
    arrays, specs = in_vmem([table_x] + [table for _, table in picked] + flat(picked))
    return pl.pallas_call(
        functools.partial(rows_kernel, sizes_of(picked)),
        out_shape=pltpu.VMEM((parts, groups * rows, width), BF),
        in_specs=[SMEM_SPEC] + specs,
        out_specs=VMEM_SPEC,
        compiler_params=pltpu.CompilerParams(vmem_limit_bytes=VMEM_BYTES),
        cost_estimate=pl.CostEstimate(
            flops=0,
            bytes_accessed=0,
            transcendentals=0,
        ),
        name="aligned_rows",
    )(table_y, *arrays)


def unpacked(packed, place, blocks):
    first = place * blocks * SUBLANES
    return jnp.concatenate(
        [pltpu.roll(packed, (LANES - first - i * SUBLANES) % LANES, 1) for i in range(blocks)]
    )


def volume_kernel(groups, orients, classes, *rest):
    ids = device_ids()
    stats, metas = rest[:2], rest[2 : 2 + groups]
    near, far = rest[2 + groups], rest[3 + groups]
    prob, outs = rest[4 + groups], rest[5 + groups :]
    rows = metas[0].shape[1]
    width = near.shape[2]
    chunk = min(width, 8 * IMG)
    lane = lax.broadcasted_iota(jnp.int32, (rows, LANES), 1)
    pieces = []
    for g in range(groups):
        top = g % 2 * SUBLANES
        mine, other = (
            unpacked(ref[top : top + SUBLANES, :], g // 2, rows // SUBLANES) for ref in stats
        )
        top = jnp.maximum(mine[:, 0:1], other[:, 0:1])
        mine_scale = jnp.exp(mine[:, 0:1] - top)
        other_scale = jnp.exp(other[:, 0:1] - top)
        held = (lane >= 1) & (lane <= classes)
        both = jnp.where(held, mine * mine_scale + other * other_scale, 0.0)
        totals = jnp.sum(both, axis=1, keepdims=True)
        spread = jnp.zeros((rows, LANES), F32)
        for k in range(classes):
            spread = jnp.where(lane % SUBLANES == k, mine[:, k + 1 : k + 2], spread)
        class_prob = spread * mine_scale / totals
        if g == 0:
            prob[...] = class_prob
        last = metas[g].shape[2] - LANES
        table = metas[g][0, :, last:].astype(F32)
        fixed = table[:, 2:3] + table[:, 3:4] + table[:, 4:5]
        weight = (fixed * class_prob).astype(BF).astype(F32)
        bin_of = table[:, 0:1].astype(jnp.int32) ^ ids[1]
        pieces.append(jnp.where(lane // SUBLANES == bin_of, weight, 0.0))
    mixes = []
    for held in (pieces[:2], pieces[2:]):
        mixing = jnp.transpose(jnp.concatenate(held, axis=0))
        mixes.append(mixing[: orients * SUBLANES].astype(BF))
    for part in range(2):
        for column in range(0, width, chunk):
            cols = slice(column, column + chunk)
            value = jnp.dot(mixes[0], near[part, :, cols], preferred_element_type=F32)
            value += jnp.dot(mixes[1], far[part, :, cols], preferred_element_type=F32)
            for o in range(orients):
                term = value[o * SUBLANES : o * SUBLANES + classes]
                outs[o][part, :, cols] = term.astype(outs[o].dtype)


def volume_terms(stats, groups, near, far, orients, classes):
    parts, entries, width = near.shape
    rest = far.shape[1]
    rows = groups[0][1].shape[1]
    out_shape = (parts, classes, width)
    arrays, specs = in_vmem([*stats, *(table for _, table in groups), near, far])
    return pl.pallas_call(
        functools.partial(volume_kernel, len(groups), orients, classes),
        out_shape=[pltpu.VMEM((rows, LANES), F32)]
        + [pltpu.VMEM(out_shape, F32 if o == 0 else BF) for o in range(orients)],
        in_specs=specs,
        out_specs=[VMEM_SPEC] * (1 + orients),
        compiler_params=pltpu.CompilerParams(vmem_limit_bytes=VMEM_BYTES),
        cost_estimate=pl.CostEstimate(
            flops=4 * orients * classes * (entries + rest) * width,
            bytes_accessed=4 * (entries + rest) * width + 4 * orients * classes * width,
            transcendentals=0,
        ),
        name="volume_terms",
    )(*arrays)


def total_kernel(first, *rest):
    terms, (out, held, sems) = rest[:-3], rest[-3:]
    copies = []
    for part in range(held.shape[0]):
        total = first[part]
        for term in terms:
            total = total + term[part].astype(F32)
        for k in range(held.shape[1]):
            held[part, k] = total[k : k + 1]
        copies.append(pltpu.make_async_copy(held.at[part], out.at[part], sems.at[part]))
        copies[-1].start()
    for copy in copies:
        copy.wait()


def total_volume(terms):
    parts, classes, width = terms[0].shape
    arrays, specs = in_vmem(terms)
    return pl.pallas_call(
        total_kernel,
        out_shape=jax.ShapeDtypeStruct((parts, classes, 1, width), F32),
        in_specs=specs,
        out_specs=pl.BlockSpec(memory_space=pl.ANY),
        scratch_shapes=[
            pltpu.VMEM((parts, classes, 1, width), F32),
            pltpu.SemaphoreType.DMA((parts,)),
        ],
        compiler_params=pltpu.CompilerParams(vmem_limit_bytes=VMEM_BYTES),
        name="total_volume",
    )(*arrays)


def local(dom, orient, cls, references, images, orient_lists, shift_ids, fixed_weights):
    classes, orients = references.shape[1], references.shape[2]
    table_x, table_y = (jnp.asarray(t) for t in trig_tables())

    def swap_dom(array, step):
        return lax.ppermute(array, "dom", xor_pairs(dom, step))

    def swap_orient(array, step):
        return lax.ppermute(array, "orient", xor_pairs(orient, step))

    bands, meta, shard = image_bands(
        orient_lists, shift_ids, fixed_weights, images, references, dom
    )
    arrived = {step: swap_dom(bands[step - 1], step) for step in [1, *range(dom - 1, 1, -1)]}
    tied, arrived[1] = lax.optimization_barrier((shard, arrived[1]))
    shards = [shard] + [None] * (orient - 1)
    for step in [*range(2, orient, 2), *range(1, orient, 2)]:
        shards[step] = swap_orient(tied if step == orient - 1 else shard, step)
    half = arrived[SHARED]
    groups = [([own_band(images, dom)], meta)]
    groups += [([arrived[step]], arrived[step]) for step in range(1, dom)]
    groups[SHARED] = ([half, lax.ppermute(half, "cls", xor_pairs(cls, 1))], half)

    width = images.shape[2] // dom
    aligned_near = aligned_rows(table_x, table_y, groups[:2], width)
    shards[2], aligned_near = lax.optimization_barrier((shards[2], aligned_near))
    every = range(orient)
    first, right = near_logits(table_x, table_y, shards, groups[:2], every[0::2], [], 0)
    near, right_late = near_logits(
        table_x, table_y, shards, groups[:2], every[1::2], first, 20
    )
    swapped = swap_dom(near[1], 1)
    right_late, swapped = lax.optimization_barrier((right_late, swapped))
    one_phase = dom == 4
    if one_phase:
        crossed = swap_dom(near[0], 2)
        crossed_over = swap_dom(near[1], 3)
    far = list(far_logits(table_x, [right, right_late], groups[2:], 6))
    if one_phase:
        terms = [
            [near[0], swapped, swap_dom(far[0], 2), swap_dom(far[1], 3)],
            [far[0], swap_dom(far[1], 1), crossed, crossed_over],
        ]
    else:
        partial = [*near, *far]
        here = {s: partial[s] + swap_dom(partial[s ^ 1], 1) for s in range(2, dom, 2)}
        here[0] = near[0] + swapped
        step = 2
        while step < dom:
            there = {s: swap_dom(here[s ^ step], step) for s in here}
            step *= 2
            if step < dom:
                here = {s: here[s] + there[s] for s in here}
        terms = [[here[s], there[s]] for s in sorted(here)]
    if one_phase:
        groups[2][0][0], *terms[1][2:] = lax.optimization_barrier(
            (groups[2][0][0], *terms[1][2:])
        )
    aligned_far = aligned_rows(table_x, table_y, groups[2:], width)
    terms[0][-1], aligned_far = lax.optimization_barrier((terms[0][-1], aligned_far))
    stats = logit_stats(terms, classes, orients)

    stats = jnp.concatenate([stats, swap_dom(stats, 1)])
    stats_all = [stats, lax.ppermute(stats, "cls", xor_pairs(cls, 1))]
    prob, *terms = volume_terms(
        stats_all, groups, aligned_near, aligned_far, orients, classes
    )
    order = sorted(range(1, orients), key=lambda place: place != orients // 2)
    terms = [terms[0]] + [swap_orient(terms[o], o) for o in order]
    return prob[:, :classes], total_volume(terms)


def solution(mesh):
    in_specs = (
        P(None, "cls", None, ("dom", "orient")),
        P(None, ("dom", "orient"), None),
        P(("dom", "orient"), None),
        P(("dom", "orient"), None),
        P(("dom", "orient"), None),
    )
    out_specs = (P(("dom", "orient"), "cls"), P(None, "cls", "orient", "dom"))
    body = functools.partial(local, mesh.shape["dom"], mesh.shape["orient"], mesh.shape["cls"])
    return jax.shard_map(body, mesh=mesh, in_specs=in_specs, out_specs=out_specs, check_vma=False)
```

```python
import functools
import math

import jax
import jax.numpy as jnp
import numpy as np
from jax import lax
from jax.experimental import pallas as pl
from jax.experimental.pallas import tpu as pltpu
from jax.sharding import PartitionSpec as P

IMG = 256
TX = 8
TY = 8
HALF = TX // 2
LANES = 128
SUBLANES = 8
SHARED = 2
FLOPS_OF_MICRO = 1_000_000_000
VMEM_BYTES = 24 * 1024 * 1024
VMEM_SPEC = pl.BlockSpec(memory_space=pltpu.VMEM)
SMEM_SPEC = pl.BlockSpec(memory_space=pltpu.SMEM)
BF = jnp.bfloat16
F32 = jnp.float32


def trig_tables():
    steps = np.arange(1, HALF + 1)
    angle_x = 2.0 * math.pi / IMG * steps[:, None] * (np.arange(IMG) - IMG // 2)[None, :]
    angle_y = 2.0 * math.pi / IMG * np.arange(IMG // 2)[:, None] * steps[None, :]
    table_x = np.concatenate([np.cos(angle_x), np.sin(angle_x)], 0).astype(np.float32)
    table_y = np.concatenate([np.cos(angle_y), np.sin(angle_y)], 1).astype(np.float32)
    return table_x, table_y.reshape(-1)


def device_ids():
    return [lax.axis_index(name) for name in ("dom", "orient", "cls")]


def xor_pairs(size, step):
    return [(i, i ^ step) for i in range(size)]


def column_of(line):
    size = line.shape[1]
    rows = lax.broadcasted_iota(jnp.int32, (size, size), 0)
    cols = lax.broadcasted_iota(jnp.int32, (size, size), 1)
    return jnp.sum(jnp.where(rows == cols, line, 0.0), axis=1, keepdims=True)


def bands_kernel(steps, images, references, *rest):
    ids = device_ids()
    lists, rest = rest[:3], rest[3:]
    outs, meta, shard = rest[: len(steps)], rest[len(steps)], rest[len(steps) + 1]
    lines, sems, meta_sems, line_sems, shard_sem = rest[len(steps) + 2 :]
    copies = [pltpu.make_async_copy(references, shard, shard_sem)]
    for place, (step, out) in enumerate(zip(steps, outs)):
        width = out.shape[2] - LANES
        start = (ids[0] ^ step) * width
        if step == SHARED:
            start = 2 * start + ids[2] * width
        start = pl.multiple_of(start, width)
        for part in range(out.shape[0]):
            copies.append(
                pltpu.make_async_copy(
                    images.at[part, :, pl.ds(start, width)],
                    out.at[part, :, pl.ds(0, width)],
                    sems.at[place, part],
                )
            )
    line_copies = [
        pltpu.make_async_copy(source, lines[place], line_sems.at[place])
        for place, source in enumerate(lists)
    ]
    for copy in line_copies + copies:
        copy.start()
    for copy in line_copies:
        copy.wait()
    lane = lax.broadcasted_iota(jnp.int32, meta.shape[1:], 1)
    fixed = column_of(lines[2][...])
    high = fixed.astype(BF).astype(F32)
    middle = (fixed - high).astype(BF).astype(F32)
    values = [column_of(lines[0][...].astype(F32)), column_of(lines[1][...].astype(F32))]
    table = jnp.zeros(meta.shape[1:], F32)
    for place, value in enumerate(values + [high, middle, fixed - high - middle]):
        table = jnp.where(lane == place, value, table)
    meta[0] = table.astype(BF)
    meta[1] = jnp.zeros(meta.shape[1:], BF)
    meta_copies = [
        pltpu.make_async_copy(
            meta, out.at[:, :, pl.ds(out.shape[2] - LANES, LANES)], meta_sems.at[place]
        )
        for place, out in enumerate(outs)
    ]
    for copy in meta_copies:
        copy.start()
    for copy in copies + meta_copies:
        copy.wait()


def image_bands(orient_lists, shift_ids, fixed_weights, images, references, dom):
    parts, rows, pixels = images.shape
    width = pixels // dom
    steps = list(range(1, dom))
    sources = [images, references] + [
        array.reshape(1, rows) for array in (orient_lists, shift_ids, fixed_weights)
    ]
    sources = [pltpu.with_memory_space_constraint(array, pltpu.HBM) for array in sources]
    *bands, meta, shard = pl.pallas_call(
        functools.partial(bands_kernel, steps),
        out_shape=[
            pltpu.VMEM((parts, rows, width // (1 + (step == SHARED)) + LANES), images.dtype)
            for step in steps
        ]
        + [
            jax.ShapeDtypeStruct((parts, rows, LANES), BF),
            pltpu.VMEM(references.shape, references.dtype),
        ],
        in_specs=[pl.BlockSpec(memory_space=pl.ANY)] * len(sources),
        out_specs=[pl.BlockSpec(memory_space=pl.ANY)] * len(steps)
        + [pl.BlockSpec(memory_space=pltpu.VMEM), pl.BlockSpec(memory_space=pl.ANY)],
        scratch_shapes=[
            [pltpu.VMEM((1, rows), array.dtype) for array in sources[2:]],
            pltpu.SemaphoreType.DMA((len(steps), parts)),
            pltpu.SemaphoreType.DMA((len(steps),)),
            pltpu.SemaphoreType.DMA((3,)),
            pltpu.SemaphoreType.DMA,
        ],
        compiler_params=pltpu.CompilerParams(vmem_limit_bytes=VMEM_BYTES),
        cost_estimate=pl.CostEstimate(
            flops=0, bytes_accessed=4 * parts * rows * (pixels - width), transcendentals=0
        ),
        name="image_bands",
    )(*sources)
    return bands, meta, shard


def own_kernel(images, band, sems):
    ids = device_ids()
    width = band.shape[2]
    start = pl.multiple_of(ids[0] * width, width)
    copies = [
        pltpu.make_async_copy(images.at[part, :, pl.ds(start, width)], band.at[part], sems.at[part])
        for part in range(band.shape[0])
    ]
    for copy in copies:
        copy.start()
    for copy in copies:
        copy.wait()


def own_band(images, dom):
    parts, rows, pixels = images.shape
    shape = (parts, rows, pixels // dom)
    return pl.pallas_call(
        own_kernel,
        out_shape=pltpu.VMEM(shape, images.dtype),
        in_specs=[pl.BlockSpec(memory_space=pl.ANY)],
        out_specs=pl.BlockSpec(memory_space=pl.ANY),
        scratch_shapes=[pltpu.SemaphoreType.DMA((parts,))],
        compiler_params=pltpu.CompilerParams(vmem_limit_bytes=VMEM_BYTES),
        name="own_band",
    )(pltpu.with_memory_space_constraint(images, pltpu.HBM))


def in_vmem(arrays):
    placed = [pltpu.with_memory_space_constraint(array, pltpu.VMEM) for array in arrays]
    return placed, [VMEM_SPEC] * len(placed)


def flat(groups):
    return [image for images, _ in groups for image in images]


def sizes_of(groups):
    return [len(images) for images, _ in groups]


def by_group(sizes, refs):
    images, at = [], 0
    for size in sizes:
        images.append(refs[at : at + size])
        at += size
    return images, refs[at:]


def load(images, ids, part, start, size):
    if len(images) == 1:
        return images[0][part, :, pl.ds(pl.multiple_of(start, size), size)].astype(F32)
    half = images[0].shape[2] - LANES
    side = start // half
    cols = pl.ds(pl.multiple_of(start - side * half, size), size)
    mine, other = (image[part, :, cols].astype(F32) for image in images)
    return jnp.where(side == ids[2], mine, other)


def shift_references(refs, right, step, ids, orients, table_y):
    names = refs.shape[1]
    chunk = right.shape[2] // 2
    lines = chunk // IMG
    line_base = (ids[0] * orients + (ids[1] ^ step[1])) * lines
    for line in range(lines):
        to_re = slice(2 * line * IMG, (2 * line + 1) * IMG)
        to_im = slice((2 * line + 1) * IMG, (2 * line + 2) * IMG)
        base = (line_base + line) * TY
        cols = slice(step[0] * chunk + line * IMG, step[0] * chunk + (line + 1) * IMG)
        ref_re = refs[0, :, cols].astype(F32)
        ref_im = refs[1, :, cols].astype(F32)

        def put(b, re, im):
            right[step[0], b * names : (b + 1) * names, to_re] = re.astype(BF)
            right[step[0], b * names : (b + 1) * names, to_im] = im.astype(BF)

        put(TY // 2, ref_re, ref_im)
        for t in range(1, HALF + 1):
            cosine = table_y[base + t - 1]
            sine = table_y[base + HALF + t - 1]
            re_c, im_s = ref_re * cosine, ref_im * sine
            im_c, re_s = ref_im * cosine, ref_re * sine
            put(TY // 2 - t, re_c - im_s, im_c + re_s)
            if t < HALF:
                put(TY // 2 + t, re_c + im_s, im_c - re_s)


def shift_images(images, left, column, ids, table_x):
    chunk = left.shape[1] // 2
    rows = images[0][0].shape[1]
    for line in range(chunk // IMG):
        to_re = slice(2 * line * IMG, (2 * line + 1) * IMG)
        to_im = slice((2 * line + 1) * IMG, (2 * line + 2) * IMG)
        for g, group in enumerate(images):
            start = column * chunk + line * IMG
            re = load(group, ids, 0, start, IMG)
            im = load(group, ids, 1, start, IMG)

            def put(a, re, im):
                top = (g * TX + a) * rows
                left[top : top + rows, to_re] = re.astype(BF)
                left[top : top + rows, to_im] = im.astype(BF)

            put(TX // 2, re, im)
            for t in range(1, HALF + 1):
                cosine = table_x[t - 1 : t, :]
                sine = table_x[HALF + t - 1 : HALF + t, :]
                re_c, im_s = re * cosine, im * sine
                re_s, im_c = re * sine, im * cosine
                put(TX // 2 - t, re_c + im_s, im_c - re_s)
                if t < HALF:
                    put(TX // 2 + t, re_c - im_s, re_s + im_c)


def add_products(outs, left, right):
    rows = outs[0].shape[0]
    value = lax.dot_general(left, right, (((1,), (1,)), ((), ())), preferred_element_type=F32)
    for g, out in enumerate(outs):
        out[...] += value[g * rows : (g + 1) * rows]


def near_kernel(sizes, orients, steps, sums, table_y, table_x, *rest):
    ids = device_ids()
    groups, count = len(sizes), len(steps)
    shards, rest = rest[:count], rest[count:]
    images, rest = by_group(sizes, rest)
    before, rest = rest[: groups * sums], rest[groups * sums :]
    outs, (right, refs, *lefts) = rest[:groups], rest[groups:]
    chunk = shards[0].shape[3]
    per_class = shards[0].shape[2]
    for place, shard in enumerate(shards):
        cols = slice(place * chunk, (place + 1) * chunk)
        for part in range(2):
            for k in range(shard.shape[1]):
                refs[part, k * per_class : (k + 1) * per_class, cols] = shard[part, k]
    for g, out in enumerate(outs):
        out[...] = before[g][...] if sums else jnp.zeros_like(out)

    for place in range(count):
        step = 2 * place + steps[0]
        left = lefts[place % 2]
        shift_references(refs, right, (place, step), ids, orients, table_y)
        shift_images(images, left, ids[1] ^ step, ids, table_x)
        add_products(outs, left[...], right[place])


def far_kernel(sizes, counts, table_x, *rest):
    ids = device_ids()
    groups = len(sizes)
    rights, rest = rest[: len(counts)], rest[len(counts) :]
    images, rest = by_group(sizes, rest)
    outs, lefts = rest[:groups], rest[groups:]
    for out in outs:
        out[...] = jnp.zeros_like(out)
    turn = 0
    for first, (right, count) in enumerate(zip(rights, counts)):
        for place in range(count):
            left = lefts[turn % 2]
            shift_images(images, left, ids[1] ^ (2 * place + first), ids, table_x)
            add_products(outs, left[...], right[place])
            turn += 1


def logits_cost(micros):
    return pl.CostEstimate(flops=micros * FLOPS_OF_MICRO, bytes_accessed=0, transcendentals=0)


def near_logits(table_x, table_y, shards, picked, steps, before, micros):
    parts, classes, orients, chunk = shards[0].shape
    groups = len(picked)
    rows = picked[0][0][0].shape[1]
    names = classes * orients
    count = len(steps)
    out_shape = (TX * rows, TY * names)
    used = [shards[step] for step in steps]
    arrays, specs = in_vmem([table_x, *used, *flat(picked), *before])
    *sums, right = pl.pallas_call(
        functools.partial(
            near_kernel, sizes_of(picked), len(shards), steps, len(before) > 0
        ),
        out_shape=[pltpu.VMEM(out_shape, F32)] * groups
        + [pltpu.VMEM((count, TY * names, 2 * chunk), BF)],
        in_specs=[SMEM_SPEC] + specs,
        out_specs=[VMEM_SPEC] * (groups + 1),
        scratch_shapes=[
            pltpu.VMEM((parts, names, count * chunk), BF),
            pltpu.VMEM((groups * TX * rows, 2 * chunk), BF),
            pltpu.VMEM((groups * TX * rows, 2 * chunk), BF),
        ],
        compiler_params=pltpu.CompilerParams(vmem_limit_bytes=VMEM_BYTES),
        cost_estimate=logits_cost(micros),
        name="near_logits",
    )(table_y, *arrays)
    return sums, right


def far_logits(table_x, rights, picked, micros):
    groups = len(picked)
    rows = picked[0][0][0].shape[1]
    names, chunk = rights[0].shape[1:]
    out_shape = (TX * rows, names)
    arrays, specs = in_vmem([table_x, *rights, *flat(picked)])
    return pl.pallas_call(
        functools.partial(far_kernel, sizes_of(picked), [right.shape[0] for right in rights]),
        out_shape=[pltpu.VMEM(out_shape, F32)] * groups,
        in_specs=specs,
        out_specs=[VMEM_SPEC] * groups,
        scratch_shapes=[pltpu.VMEM((groups * TX * rows, chunk), BF)] * 2,
        compiler_params=pltpu.CompilerParams(vmem_limit_bytes=VMEM_BYTES),
        cost_estimate=logits_cost(micros),
        name="far_logits",
    )(*arrays)


def stats_kernel(counts, classes, orients, *refs):
    *logits, out = refs
    rows, lanes = logits[0].shape[0] // TX, logits[0].shape[1]
    lane = lax.broadcasted_iota(jnp.int32, (rows, lanes), 1)
    class_of = (lane // orients) % classes
    out_lane = lax.broadcasted_iota(jnp.int32, (rows, LANES), 1)
    packed = jnp.zeros((SUBLANES, LANES), F32)
    for g, count in enumerate(counts):
        total = sum(ref[...] for ref in logits[:count])
        logits = logits[count:]
        pieces = [total[a * rows : (a + 1) * rows] for a in range(TX)]
        top = functools.reduce(jnp.maximum, pieces)
        top = jnp.max(top, axis=1, keepdims=True)
        sums = sum(jnp.exp(piece - top) for piece in pieces)
        line = jnp.where(out_lane == 0, top, 0.0)
        for k in range(classes):
            part = jnp.sum(jnp.where(class_of == k, sums, 0.0), axis=1, keepdims=True)
            line = jnp.where(out_lane == k + 1, part, line)
        for half in range(rows // SUBLANES):
            block = line[half * SUBLANES : (half + 1) * SUBLANES]
            place = (g * (rows // SUBLANES) + half) * SUBLANES
            packed = packed + pltpu.roll(block, place, 1)
    out[...] = packed


def logit_stats(terms, classes, orients):
    arrays, specs = in_vmem([array for held in terms for array in held])
    return pl.pallas_call(
        functools.partial(stats_kernel, [len(held) for held in terms], classes, orients),
        out_shape=pltpu.VMEM((SUBLANES, LANES), F32),
        in_specs=specs,
        out_specs=VMEM_SPEC,
        compiler_params=pltpu.CompilerParams(vmem_limit_bytes=VMEM_BYTES),
        name="logit_stats",
    )(*arrays)


def rows_kernel(sizes, table_y, table_x, *rest):
    ids = device_ids()
    groups = len(sizes)
    metas = rest[:groups]
    images, (out,) = by_group(sizes, rest[groups:])
    rows = metas[0].shape[1]
    width = out.shape[2]
    lines = width // IMG
    line_base = ids[0] * lines
    for g in range(groups):
        own = slice(g * rows, (g + 1) * rows)
        last = metas[g].shape[2] - LANES
        shift = metas[g][0, :, last:].astype(F32)[:, 1:2].astype(jnp.int32)
        move_x = jnp.broadcast_to(shift % TX - TX // 2, (rows, IMG))
        move_y = jnp.broadcast_to(shift // TX - TY // 2, (rows, LANES))
        phase_c = jnp.ones((rows, IMG), F32)
        phase_s = jnp.zeros((rows, IMG), F32)
        for t in range(1, HALF + 1):
            hit = jnp.abs(move_x) == t
            phase_c = jnp.where(hit, table_x[t - 1 : t, :], phase_c)
            phase_s = jnp.where(hit, table_x[HALF + t - 1 : HALF + t, :], phase_s)
        phase_s = jnp.where(move_x < 0, -phase_s, phase_s)
        hits = [jnp.abs(move_y) == t for t in range(1, HALF + 1)]
        sign = jnp.where(move_y < 0, -1.0, 1.0)

        def add_line(line, carry):
            base = (line_base + line) * TY
            cos_y = jnp.ones((rows, LANES), F32)
            sin_y = jnp.zeros((rows, LANES), F32)
            for t in range(1, HALF + 1):
                cos_y = jnp.where(hits[t - 1], table_y[base + t - 1], cos_y)
                sin_y = jnp.where(hits[t - 1], table_y[base + HALF + t - 1], sin_y)
            sin_y = sin_y * sign
            for part in range(IMG // LANES):
                across = slice(part * LANES, (part + 1) * LANES)
                start = pl.multiple_of(line * IMG + part * LANES, LANES)
                cols = pl.ds(start, LANES)
                cos_x, sin_x = phase_c[:, across], phase_s[:, across]
                cosine = cos_x * cos_y - sin_x * sin_y
                sine = sin_x * cos_y + cos_x * sin_y
                re = load(images[g], ids, 0, start, LANES)
                im = load(images[g], ids, 1, start, LANES)
                out[0, own, cols] = (re * cosine - im * sine).astype(BF)
                out[1, own, cols] = (re * sine + im * cosine).astype(BF)
            return carry

        lax.fori_loop(0, lines, add_line, 0, unroll=min(lines, 8))


def aligned_rows(table_x, table_y, picked, width):
    parts, rows = picked[0][0][0].shape[:2]
    groups = len(picked)
    arrays, specs = in_vmem([table_x] + [table for _, table in picked] + flat(picked))
    return pl.pallas_call(
        functools.partial(rows_kernel, sizes_of(picked)),
        out_shape=pltpu.VMEM((parts, groups * rows, width), BF),
        in_specs=[SMEM_SPEC] + specs,
        out_specs=VMEM_SPEC,
        compiler_params=pltpu.CompilerParams(vmem_limit_bytes=VMEM_BYTES),
        cost_estimate=pl.CostEstimate(
            flops=0,
            bytes_accessed=0,
            transcendentals=0,
        ),
        name="aligned_rows",
    )(table_y, *arrays)


def unpacked(packed, place, blocks):
    first = place * blocks * SUBLANES
    return jnp.concatenate(
        [pltpu.roll(packed, (LANES - first - i * SUBLANES) % LANES, 1) for i in range(blocks)]
    )


def volume_kernel(groups, orients, classes, *rest):
    ids = device_ids()
    stats, metas = rest[:2], rest[2 : 2 + groups]
    near, far = rest[2 + groups], rest[3 + groups]
    prob, outs = rest[4 + groups], rest[5 + groups :]
    rows = metas[0].shape[1]
    width = near.shape[2]
    chunk = min(width, 4 * IMG)
    lane = lax.broadcasted_iota(jnp.int32, (rows, LANES), 1)
    pieces = []
    for g in range(groups):
        top = g % 2 * SUBLANES
        mine, other = (
            unpacked(ref[top : top + SUBLANES, :], g // 2, rows // SUBLANES) for ref in stats
        )
        top = jnp.maximum(mine[:, 0:1], other[:, 0:1])
        mine_scale = jnp.exp(mine[:, 0:1] - top)
        other_scale = jnp.exp(other[:, 0:1] - top)
        held = (lane >= 1) & (lane <= classes)
        both = jnp.where(held, mine * mine_scale + other * other_scale, 0.0)
        totals = jnp.sum(both, axis=1, keepdims=True)
        spread = jnp.zeros((rows, LANES), F32)
        for k in range(classes):
            spread = jnp.where(lane % SUBLANES == k, mine[:, k + 1 : k + 2], spread)
        class_prob = spread * mine_scale / totals
        if g == 0:
            prob[...] = class_prob
        last = metas[g].shape[2] - LANES
        table = metas[g][0, :, last:].astype(F32)
        fixed = table[:, 2:3] + table[:, 3:4] + table[:, 4:5]
        weight = (fixed * class_prob).astype(BF).astype(F32)
        bin_of = table[:, 0:1].astype(jnp.int32) ^ ids[1]
        pieces.append(jnp.where(lane // SUBLANES == bin_of, weight, 0.0))
    mixes = []
    for held in (pieces[:2], pieces[2:]):
        mixing = jnp.transpose(jnp.concatenate(held, axis=0))
        mixes.append(mixing[: orients * SUBLANES].astype(BF))
    for part in range(2):
        for column in range(0, width, chunk):
            cols = slice(column, column + chunk)
            value = jnp.dot(mixes[0], near[part, :, cols], preferred_element_type=F32)
            value += jnp.dot(mixes[1], far[part, :, cols], preferred_element_type=F32)
            for o in range(orients):
                term = value[o * SUBLANES : o * SUBLANES + classes]
                outs[o][part, :, cols] = term.astype(outs[o].dtype)


def volume_terms(stats, groups, near, far, orients, classes):
    parts, entries, width = near.shape
    rest = far.shape[1]
    rows = groups[0][1].shape[1]
    out_shape = (parts, classes, width)
    arrays, specs = in_vmem([*stats, *(table for _, table in groups), near, far])
    return pl.pallas_call(
        functools.partial(volume_kernel, len(groups), orients, classes),
        out_shape=[pltpu.VMEM((rows, LANES), F32)]
        + [pltpu.VMEM(out_shape, F32 if o == 0 else BF) for o in range(orients)],
        in_specs=specs,
        out_specs=[VMEM_SPEC] * (1 + orients),
        compiler_params=pltpu.CompilerParams(vmem_limit_bytes=VMEM_BYTES),
        cost_estimate=pl.CostEstimate(
            flops=4 * orients * classes * (entries + rest) * width,
            bytes_accessed=4 * (entries + rest) * width + 4 * orients * classes * width,
            transcendentals=0,
        ),
        name="volume_terms",
    )(*arrays)


def total_kernel(first, *rest):
    out = rest[-1]
    total = first[...]
    for term in rest[:-1]:
        total = total + term[...].astype(F32)
    for part in range(out.shape[0]):
        for k in range(out.shape[1]):
            out[part, k] = total[part, k : k + 1]


def total_volume(terms):
    parts, classes, width = terms[0].shape
    arrays, specs = in_vmem(terms)
    return pl.pallas_call(
        total_kernel,
        out_shape=jax.ShapeDtypeStruct((parts, classes, 1, width), F32),
        in_specs=specs,
        compiler_params=pltpu.CompilerParams(vmem_limit_bytes=VMEM_BYTES),
        name="total_volume",
    )(*arrays)


def local(dom, orient, cls, references, images, orient_lists, shift_ids, fixed_weights):
    classes, orients = references.shape[1], references.shape[2]
    table_x, table_y = (jnp.asarray(t) for t in trig_tables())

    def swap_dom(array, step):
        return lax.ppermute(array, "dom", xor_pairs(dom, step))

    def swap_orient(array, step):
        return lax.ppermute(array, "orient", xor_pairs(orient, step))

    bands, meta, shard = image_bands(
        orient_lists, shift_ids, fixed_weights, images, references, dom
    )
    arrived = {step: swap_dom(bands[step - 1], step) for step in [1, *range(dom - 1, 1, -1)]}
    tied, arrived[1] = lax.optimization_barrier((shard, arrived[1]))
    shards = [shard] + [None] * (orient - 1)
    for step in [*range(2, orient, 2), *range(1, orient, 2)]:
        shards[step] = swap_orient(tied if step == orient - 1 else shard, step)
    half = arrived[SHARED]
    groups = [([own_band(images, dom)], meta)]
    groups += [([arrived[step]], arrived[step]) for step in range(1, dom)]
    groups[SHARED] = ([half, lax.ppermute(half, "cls", xor_pairs(cls, 1))], half)

    width = images.shape[2] // dom
    aligned_near = aligned_rows(table_x, table_y, groups[:2], width)
    shards[2], aligned_near = lax.optimization_barrier((shards[2], aligned_near))
    every = range(orient)
    first, right = near_logits(table_x, table_y, shards, groups[:2], every[0::2], [], 0)
    near, right_late = near_logits(
        table_x, table_y, shards, groups[:2], every[1::2], first, 20
    )
    swapped = swap_dom(near[1], 1)
    right_late, swapped = lax.optimization_barrier((right_late, swapped))
    one_phase = dom == 4
    if one_phase:
        crossed = swap_dom(near[0], 2)
        crossed_over = swap_dom(near[1], 3)
    far = list(far_logits(table_x, [right, right_late], groups[2:], 6))
    if one_phase:
        terms = [
            [near[0], swapped, swap_dom(far[0], 2), swap_dom(far[1], 3)],
            [far[0], swap_dom(far[1], 1), crossed, crossed_over],
        ]
    else:
        partial = [*near, *far]
        here = {s: partial[s] + swap_dom(partial[s ^ 1], 1) for s in range(2, dom, 2)}
        here[0] = near[0] + swapped
        step = 2
        while step < dom:
            there = {s: swap_dom(here[s ^ step], step) for s in here}
            step *= 2
            if step < dom:
                here = {s: here[s] + there[s] for s in here}
        terms = [[here[s], there[s]] for s in sorted(here)]
    if one_phase:
        groups[2][0][0], *terms[1][2:] = lax.optimization_barrier(
            (groups[2][0][0], *terms[1][2:])
        )
    aligned_far = aligned_rows(table_x, table_y, groups[2:], width)
    terms[0][-1], aligned_far = lax.optimization_barrier((terms[0][-1], aligned_far))
    stats = logit_stats(terms, classes, orients)

    stats = jnp.concatenate([stats, swap_dom(stats, 1)])
    stats_all = [stats, lax.ppermute(stats, "cls", xor_pairs(cls, 1))]
    prob, *terms = volume_terms(
        stats_all, groups, aligned_near, aligned_far, orients, classes
    )
    order = sorted(range(1, orients), key=lambda place: place != orients // 2)
    terms = [terms[0]] + [swap_orient(terms[o], o) for o in order]
    return prob[:, :classes], total_volume(terms)


def solution(mesh):
    in_specs = (
        P(None, "cls", None, ("dom", "orient")),
        P(None, ("dom", "orient"), None),
        P(("dom", "orient"), None),
        P(("dom", "orient"), None),
        P(("dom", "orient"), None),
    )
    out_specs = (P(("dom", "orient"), "cls"), P(None, "cls", "orient", "dom"))
    body = functools.partial(local, mesh.shape["dom"], mesh.shape["orient"], mesh.shape["cls"])
    return jax.shard_map(body, mesh=mesh, in_specs=in_specs, out_specs=out_specs, check_vma=False)
```
